32 devices in a mesh: dp: 16 (over z, y, core), seq: 2 (over x).
Axes of the slice: x: 2, y: 2, z: 4, core: 2. Of those that a mesh axis runs over, the one named last changes fastest.
Arguments:
- inputs: bfloat16 [48, 100, 768], P('dp'), may hold values from -6 to 6
- memory: bfloat16 [48, 1024, 768], P('dp', 'seq'), may hold values from -6 to 6
- lengths: int32 [48], P('dp'), may hold values from 256 to 1024, as said below
- matched: int32 [48, 64], P('dp'), may hold values from 0 to 99, as said below
- cotangent: bfloat16 [48, 64, 768], P('dp'), may hold values from -6 to 6
- weights: bfloat16 [1, 12544, 768], P(None, ('dp', 'seq')), as said below
Outputs:
- outputs: float32 [48, 100, 768], P('dp')
- input_grads: float32 [48, 100, 768], P('dp')
- memory_grads: float32 [48, 1024, 768], P('dp', 'seq')
- weight_grads: float32 [1, 12544, 768], P(None, ('dp', 'seq'))
The draws below stay inside these ranges and needn't reach their ends.
Inputs may be any that keep to these rules, and one draw needn't show every extreme that they name: Token j of image i is padding where j >= lengths[i]; in each group of 3 consecutive images one image, drawn from the seed, has all 1024 tokens. `matched`: each row holds 64 different query indices. `weights`: rows from 12305 on are zero.
All inputs are finite; a program needn't handle non-finite values.
Results may differ from the reference program's by a relative error of at most 0.02.
The reference program's roundings to bfloat16 on the way count: a program that leaves them out, or rounds other values in their place, can miss the bound.
Values may be sent and summed in bfloat16 or wider, within the bound.
No kernel may reach another device: no remote copies, remote signals or barrier semaphores. Data moves between devices by JAX's collectives and lax.ppermute only.
A program may use at most 192 MiB of HBM per device.

```python
import jax
import jax.numpy as jnp
from jax import lax

D = 768
H = 12
HEAD = 64
FF = 3072
Q = 100
MATCH = 64
LAYERS = 1
IMG_DEV = 3
IMAGES = 48
MEM = 1024
ROWS_USED = 12305
ROWS = 12544


def draw_lengths(key, part):
    key = jax.random.fold_in(key, 11)
    first_key, second_key = jax.random.split(key)
    drawn = jax.random.randint(first_key, (IMAGES,), MEM // 4, MEM + 1)
    chosen = jax.random.randint(second_key, (IMAGES // IMG_DEV,), 0, IMG_DEV)
    image_ids = jnp.arange(IMAGES)
    full_image = image_ids % IMG_DEV == chosen[image_ids // IMG_DEV]
    return jnp.where(full_image, MEM, drawn).astype(jnp.int32)


def draw_matched(key, part):
    key = jax.random.fold_in(key, 23)
    row_keys = jax.random.split(key, IMAGES)
    orders = jax.vmap(lambda row_key: jax.random.permutation(row_key, Q))(row_keys)
    image_ids = jnp.arange(IMAGES)
    target = jnp.where(image_ids == 0, Q - 1, jnp.where(image_ids == 1, 0, orders[:, 0]))
    where_at = jnp.argmax((orders == target[:, None]).astype(jnp.int32), axis=1)
    columns = (jnp.arange(Q)[None, :] + where_at[:, None]) % Q
    rolled = jnp.take_along_axis(orders, columns, axis=1)
    return rolled[:, :MATCH].astype(jnp.int32)


def draw_weights(key, part):
    key = jax.random.fold_in(key, 37)
    row_ids = jnp.arange(ROWS)
    base_row = 8 * D + 2 * FF
    gain_start = base_row + 7 + FF // D
    unit_scale = D ** (-0.5)
    scaling = jnp.full((ROWS,), unit_scale, jnp.float32)
    scaling = jnp.where(row_ids < D, 1.5 * unit_scale, scaling)
    scaling = jnp.where((row_ids >= 3 * D) & (row_ids < 4 * D), 4.0 * unit_scale, scaling)
    scaling = jnp.where((row_ids >= 4 * D) & (row_ids < 5 * D), 1.5 * unit_scale, scaling)
    scaling = jnp.where((row_ids >= 7 * D) & (row_ids < 8 * D), 6.0 * unit_scale, scaling)
    scaling = jnp.where((row_ids >= 8 * D + FF) & (row_ids < base_row), 1.5 * FF ** (-0.5), scaling)
    scaling = jnp.where((row_ids >= base_row) & (row_ids < gain_start), 0.2, scaling)
    gain_rows = (row_ids >= gain_start) & (row_ids < gain_start + 6) & ((row_ids - gain_start) % 2 == 0)
    offset_rows = (row_ids >= gain_start) & (row_ids < gain_start + 6) & ((row_ids - gain_start) % 2 == 1)
    scaling = jnp.where(gain_rows, 0.25, scaling)
    scaling = jnp.where(offset_rows, 0.2, scaling)
    scaling = jnp.where(row_ids >= ROWS_USED, 0.0, scaling)
    offset = jnp.where(gain_rows, 1.0, 0.0)
    noise = jnp.clip(jax.random.normal(key, (LAYERS, ROWS, D), jnp.float32), -3.0, 3.0)
    return (noise * scaling[None, :, None] + offset[None, :, None]).astype(jnp.bfloat16)


def level_of(own_key, extent, cuts, least, top_value):
    level = 1.0
    for position, parts in cuts:
        draws = jax.random.uniform(jax.random.fold_in(jax.random.fold_in(own_key, 6), position), (parts,), jnp.float32, least / len(cuts), top_value / len(cuts))
        level = level * jnp.repeat(jnp.exp(draws), extent[position] // parts).reshape((-1,) + (1,) * (len(extent) - 1 - position))
    return level


def bell_draw(stream_key, shape, spread, limit, pieces=(), held_as=jnp.bfloat16):
    values = spread * jax.random.normal(stream_key, shape, jnp.float32)
    if pieces:
        values = values * level_of(stream_key, shape, pieces, -0.22, 0.18)
    return jnp.clip(values, -limit, limit).astype(held_as)


def setup_inputs(seed: int = 0) -> dict:
    streams_of = jax.random.split(jax.random.key(seed), 7)
    inputs = bell_draw(streams_of[0], (IMAGES, Q, D), 1.0, 6.0, ((0, 16),))
    memory = bell_draw(streams_of[1], (IMAGES, MEM, D), 1.0, 6.0, ((0, 16), (1, 2)))
    lengths = draw_lengths(jax.random.fold_in(streams_of[6], 71), 0)
    matched = draw_matched(jax.random.fold_in(streams_of[6], 71), 0)
    cotangent = bell_draw(streams_of[4], (IMAGES, MATCH, D), 1.0, 6.0, ((0, 16),))
    weights = draw_weights(jax.random.fold_in(streams_of[6], 71), 0)
    return dict(inputs=inputs, memory=memory, lengths=lengths, matched=matched, cotangent=cotangent, weights=weights)


@jax.custom_vjp
def low(v):
    return lax.optimization_barrier(v.astype(jnp.bfloat16)).astype(jnp.float32)

@jax.custom_vjp
def low_back(v):
    return v

def low_keep(v):
    return (low(v), None)

def low_pass(kept, grad):
    return (grad,)

def back_keep(v):
    return (v, None)

def back_low(kept, grad):
    return (low(grad),)
low.defvjp(low_keep, low_pass)
low_back.defvjp(back_keep, back_low)
eps_norm = 1e-05
big_negative = -1e+30

def matmul_high(left_operand, right_operand):
    return jnp.dot(left_operand, right_operand, precision=lax.Precision.HIGHEST, preferred_element_type=jnp.float32)

def unpack(flat_rows):
    base_row = 8 * D + 2 * FF
    tail_row = base_row + 7 + FF // D
    matrices = [flat_rows[index * D:(index + 1) * D] for index in range(8)]
    inner_row_block = flat_rows[8 * D:8 * D + FF]
    outer_row_block = flat_rows[8 * D + FF:base_row]
    vectors = [flat_rows[base_row + index] for index in range(7)]
    inner_bias = flat_rows[base_row + 7:tail_row].reshape(FF)
    norm_rows = [flat_rows[tail_row + index] for index in range(6)]
    return (matrices, inner_row_block, outer_row_block, vectors, inner_bias, norm_rows)

def layer_norm(values_in, gain_row, offset_row):
    center = values_in - lax.optimization_barrier(jnp.mean(values_in, axis=-1, keepdims=True))
    inverse = lax.rsqrt(lax.optimization_barrier(jnp.mean(center * center, axis=-1, keepdims=True)) + eps_norm)
    return center * inverse * gain_row + offset_row

def attend(query_rows, key_rows, value_rows, valid):
    heads_q = query_rows.reshape(query_rows.shape[0], H, HEAD)
    heads_k = key_rows.reshape(key_rows.shape[0], H, HEAD)
    heads_v = value_rows.reshape(value_rows.shape[0], H, HEAD)
    scores = low_back(jnp.einsum('qhe,khe->hqk', heads_q, heads_k, precision=lax.Precision.HIGHEST))
    if valid is not None:
        scores = jnp.where(valid[None, None, :], scores, big_negative)
    probs = low(jax.nn.softmax(scores, axis=-1))
    mixed = jnp.einsum('hqk,khe->qhe', probs, heads_v, precision=lax.Precision.HIGHEST)
    return low(low_back(mixed.reshape(query_rows.shape[0], D)))

def decoder_layer(flat_rows, state, memory_rows, valid):
    matrices, inner_row_block, outer_row_block, vectors, inner_bias, norm_rows = unpack(flat_rows)
    scaling = HEAD ** (-0.5)
    entry_point = low(state)
    query_self = low(low_back((matmul_high(entry_point, matrices[0]) + vectors[0]) * scaling))
    key_self = low(low_back(matmul_high(entry_point, matrices[1])))
    value_self = low(low_back(matmul_high(entry_point, matrices[2]) + vectors[1]))
    mixed_self = attend(query_self, key_self, value_self, None)
    branch_self = low_back(matmul_high(mixed_self, matrices[3]) + vectors[2])
    first = layer_norm(state + branch_self, norm_rows[0], norm_rows[1])
    entry_two = low(first)
    query_cross = low(low_back((matmul_high(entry_two, matrices[4]) + vectors[3]) * scaling))
    key_cross = low(low_back(matmul_high(memory_rows, matrices[5])))
    value_cross = low(low_back(matmul_high(memory_rows, matrices[6]) + vectors[4]))
    mixed_cross = attend(query_cross, key_cross, value_cross, valid)
    branch_cross = low_back(matmul_high(mixed_cross, matrices[7]) + vectors[5])
    second = layer_norm(first + branch_cross, norm_rows[2], norm_rows[3])
    third_entry = low(second)
    hidden = low_back(jnp.einsum('qd,fd->qf', third_entry, inner_row_block, precision=lax.Precision.HIGHEST) + inner_bias)
    active_layer = low(jax.nn.gelu(hidden, approximate=True))
    branch_inner = low_back(matmul_high(active_layer, outer_row_block) + vectors[6])
    return layer_norm(second + branch_inner, norm_rows[4], norm_rows[5])

def image_forward(flat_layers, image_in, image_mem, length):
    valid = jnp.arange(MEM) < length
    memory_rows = low(image_mem)
    state = image_in
    for layer_index in range(LAYERS):
        state = decoder_layer(flat_layers[layer_index], state, memory_rows, valid)
    return state

def reference(inputs, memory, lengths, matched, cotangent, weights):
    flat_layers = weights.astype(jnp.float32)

    def one_image(carry, item):
        image_in, image_mem, length, match_rows, image_cot = item

        def picked(flat_arg, input_arg, memory_arg):
            final = image_forward(flat_arg, input_arg, memory_arg, length)
            return (jnp.take(final, match_rows, axis=0), final)
        chosen, pullback, final = jax.vjp(picked, flat_layers, image_in.astype(jnp.float32), image_mem.astype(jnp.float32), has_aux=True)
        grad_flat, grad_in, grad_mem = pullback(image_cot.astype(jnp.float32))
        return (carry + grad_flat, (final, grad_in, grad_mem))
    total, stacked = lax.scan(one_image, jnp.zeros_like(flat_layers), (inputs, memory, lengths, matched, cotangent))
    outputs, input_grads, memory_grads = stacked
    return (outputs, input_grads, memory_grads, total)
```

```python
from functools import partial

import jax
import jax.numpy as jnp
from jax import lax
from jax.experimental import pallas as pl
from jax.experimental.pallas import tpu as pltpu
from jax.sharding import PartitionSpec as P

D = 768
H = 12
HEAD = 64
FF = 3072
PAIRS = H // 2
LANES = 2 * HEAD
QP = 112
VEC_ROW = 8 * D + 2 * FF
VECS = 24
TAIL = 256
HEAD_ROWS = 128
QUERY_HEAD = 64
SCALE = HEAD ** (-0.5)
EPS = 1e-05
NEG = -1e30
F32 = jnp.float32
BF16 = jnp.bfloat16
MIB = 1024 * 1024


def dot_nn(a, b):
    return lax.dot_general(a, b, (((1,), (0,)), ((), ())), preferred_element_type=F32)


def dot_nt(a, b):
    return lax.dot_general(a, b, (((1,), (1,)), ((), ())), preferred_element_type=F32)


def dot_tn(a, b):
    return lax.dot_general(a, b, (((0,), (0,)), ((), ())), preferred_element_type=F32)


def norm_parts(v):
    center = v - jnp.mean(v, axis=-1, keepdims=True)
    inverse = lax.rsqrt(jnp.mean(center * center, axis=-1, keepdims=True) + EPS)
    return center * inverse, inverse


def norm_back(dy, hat, inverse, gain):
    scaled = dy * gain
    mean_one = jnp.mean(scaled, axis=-1, keepdims=True)
    mean_two = jnp.mean(scaled * hat, axis=-1, keepdims=True)
    return inverse * (scaled - mean_one - hat * mean_two)


def rowsum(v):
    return jnp.sum(v.astype(F32), axis=0, keepdims=True)


def head_masks():
    lane = lax.broadcasted_iota(jnp.int32, (1, LANES), 1)
    first = jnp.where(lane < HEAD, 1.0, 0.0)
    return first.astype(BF16), (1.0 - first).astype(BF16)


def two_heads(block, masks):
    return jnp.concatenate([block * masks[0], block * masks[1]], axis=0)


def join_heads(stacked):
    lane = lax.broadcasted_iota(jnp.int32, (QP, LANES), 1)
    return jnp.where(lane < HEAD, stacked[:QP], stacked[QP:])


def weight_block(index):
    return pl.BlockSpec((D, D), lambda *_: (index, 0))


def whole(shape):
    return pl.BlockSpec(shape, lambda *_: (0,) * len(shape))


def params(mib):
    return pltpu.CompilerParams(vmem_limit_bytes=mib * MIB)


def cost(flops, moved):
    return pl.CostEstimate(flops=flops // 1000, bytes_accessed=moved // 1000, transcendentals=0)


FIRST_BLOCKS = (0, 1, 2, 5, 6, 3, 4)
SPREAD = ((0, 0, 0), (0, 0, 1), (0, 1, 0), (1, 0, 0), (0, 1, 1), (1, 1, 0), (1, 0, 1), (1, 1, 1))
PAIR_ROWS = 784
HOLDER = (3, 1, 1, 1)


class Assembly:
    def __init__(self, flags, bufs, weights, sems, vec_low, vec_sem):
        self.core, self.x, self.y, self.z = flags[0], flags[1], flags[2], flags[3]
        self.bufs, self.weights, self.sems = bufs, weights, sems
        self.vec_low, self.vec_sem = vec_low, vec_sem
        self.ready = set()

    def buf(self, dc, dz2, spread):
        return self.bufs[dc * 16 + dz2 * 8 + SPREAD.index(spread)]

    def start_vec(self):
        first = VEC_ROW - 15 * PAIR_ROWS - 384
        for dc in (0, 1):
            for dz2 in (0, 1):
                for dz1, dy, dx in SPREAD:
                    here = (self.z ^ (2 * dz2 + dz1), self.y ^ dy, self.core ^ dc, self.x ^ dx)
                    hit = (here[0] == HOLDER[0]) & (here[1] == HOLDER[1]) & (here[2] == HOLDER[2]) & (here[3] == HOLDER[3])

                    @pl.when(hit)
                    def _(source=self.buf(dc, dz2, (dz1, dy, dx))):
                        pltpu.make_async_copy(source.at[pl.ds(first, 32)], self.vec_low, self.vec_sem).start()

    def wait_vec(self):
        pltpu.make_async_copy(self.weights.at[pl.ds(0, 32)], self.vec_low, self.vec_sem).wait()

    def start_group(self, dz2):
        def rows(start, count):
            return pl.ds(pl.multiple_of(start, 16), count)

        for dz1 in (0, 1):
            for dy in (0, 1):
                for dc in (0, 1):
                    pair = (self.z ^ (2 * dz2 + dz1)) * 4 + (self.y ^ dy) * 2 + (self.core ^ dc)
                    base, sem = pair * PAIR_ROWS, self.sems.at[pair]
                    near, far = self.buf(dc, dz2, (dz1, dy, 0)), self.buf(dc, dz2, (dz1, dy, 1))
                    for source, x in ((near, self.x), (far, 1 - self.x)):
                        target = self.weights.at[rows(base + 400 * x, 384)]
                        pltpu.make_async_copy(source.at[rows(16 * x, 384)], target, sem).start()
                    target = self.weights.at[rows(base + 384, 16)]
                    pltpu.make_async_copy(near.at[rows(384 * (1 - self.x), 16)], target, sem).start()

    def start(self):
        self.start_vec()
        for low in (True, False):

            @pl.when((self.z < 2) == low)
            def _(low=low):
                for dz2 in (0, 1) if low else (1, 0):
                    self.start_group(dz2)

    def wait(self, pair):
        if pair not in self.ready:
            self.ready.add(pair)
            rows = self.weights.at[pl.ds(pair * PAIR_ROWS, PAIR_ROWS)]
            pltpu.make_async_copy(rows, rows, self.sems.at[pair]).wait()

    def block(self, number):
        for pair in range(number * D // PAIR_ROWS, (number * D + D - 1) // PAIR_ROWS + 1):
            self.wait(pair)


class Direct:
    def __init__(self, w_hbm, weights, sems, vec_low, vec_sem):
        self.copies = {}
        for number in FIRST_BLOCKS:
            rows = pl.ds(number * D, D)
            self.copies[number] = pltpu.make_async_copy(w_hbm.at[rows], weights.at[rows], sems.at[number])
        self.vec = pltpu.make_async_copy(w_hbm.at[pl.ds(VEC_ROW, 32)], vec_low, vec_sem)
        self.ready = set()

    def start(self):
        self.vec.start()
        for number in FIRST_BLOCKS:
            self.copies[number].start()

    def wait_vec(self):
        self.vec.wait()

    def block(self, number):
        if number not in self.ready:
            self.ready.add(number)
            self.copies[number].wait()


def forward_kernel(queries, custom, left_ref, flags, xb_ref, m_hbm, *refs):
    count = 32 if custom else 1
    bufs, refs = refs[:count], refs[count:]
    qs_out, ks_out, vs_out, os_out, y1_out, qc_out, k_out, v_out, o_out, stat_ref = refs[:10]
    w_out = refs[10] if custom else None
    weights, m_ref, qs_ref, ks_ref, vs_ref, os_ref, y1_ref, qc_ref, k_ref, v_ref, o_ref, vec_low = refs[10 + custom : 22 + custom]
    w_sems, m_sems, out_sems, kv_sems, vec_sem, all_sems = refs[22 + custom :]
    images = m_ref.shape[0]
    tokens = m_ref.shape[1]
    if custom:
        feed = Assembly(flags, bufs, weights, w_sems, vec_low, vec_sem)
    else:
        feed = Direct(bufs[0], weights, w_sems, vec_low, vec_sem)

    def load_memory(image):
        return pltpu.make_async_copy(m_hbm.at[image], m_ref.at[image], m_sems.at[image])

    def matrix(block):
        feed.block(block)
        return weights[block * D : (block + 1) * D, :]

    def leave_weights(half):
        rows = pl.ds(half * 8 * PAIR_ROWS, 8 * PAIR_ROWS)
        return pltpu.make_async_copy(weights.at[rows], w_out.at[rows], all_sems.at[half])

    small = [(qs_ref, qs_out), (ks_ref, ks_out), (vs_ref, vs_out), (os_ref, os_out), (y1_ref, y1_out), (qc_ref, qc_out)]

    def leave(number):
        return pltpu.make_async_copy(*small[number], out_sems.at[number])

    def leave_image(image, number):
        source, target = [(k_ref, k_out), (v_ref, v_out), (o_ref, o_out)][number]
        return pltpu.make_async_copy(source.at[image], target.at[image], kv_sems.at[image, number])

    feed.start()
    for image in range(images):
        load_memory(image).start()
    feed.wait_vec()
    vec = vec_low[...].astype(F32)
    xb = xb_ref[...]
    qs_ref[...] = ((dot_nn(xb, matrix(0)) + vec[0:1, :]) * SCALE).astype(BF16)
    leave(0).start()
    ks_ref[...] = dot_nn(xb, matrix(1)).astype(BF16)
    leave(1).start()
    vs_ref[...] = (dot_nn(xb, matrix(2)) + vec[1:2, :]).astype(BF16)
    leave(2).start()
    masks = head_masks()
    real = lax.broadcasted_iota(jnp.int32, (2 * QP, QP), 1) < queries
    for image in range(images):
        rows = slice(image * QP, (image + 1) * QP)
        for pair in range(PAIRS):
            lanes = slice(pair * LANES, (pair + 1) * LANES)
            scores = dot_nt(two_heads(qs_ref[rows, lanes], masks), ks_ref[rows, lanes])
            scores = jnp.where(real, scores, NEG)
            probs = jnp.exp(scores - jnp.max(scores, axis=-1, keepdims=True))
            probs = probs / jnp.sum(probs, axis=-1, keepdims=True)
            os_ref[rows, lanes] = join_heads(dot_nn(probs.astype(BF16), vs_ref[rows, lanes])).astype(BF16)
    leave(3).start()
    y1 = xb.astype(F32) + (dot_nn(os_ref[...], matrix(3)) + vec[2:3, :])
    y1_ref[...] = y1
    leave(4).start()
    hat, _ = norm_parts(y1)
    x1 = hat * vec[11:12, :] + vec[12:13, :]
    qc_ref[...] = ((dot_nn(x1.astype(BF16), matrix(4)) + vec[3:4, :]) * SCALE).astype(BF16)
    leave(5).start()

    feed.block(5)
    feed.block(6)
    if custom:
        for pair in range(8):
            feed.wait(pair)
        leave_weights(0).start()
    column = lax.broadcasted_iota(jnp.int32, (2 * QP, 128), 1)
    for image in range(images):
        load_memory(image).wait()
        rows = slice(image * QP, (image + 1) * QP)
        k_ref[image] = dot_nn(m_ref[image], matrix(5)).astype(BF16)
        v_ref[image] = (dot_nn(m_ref[image], matrix(6)) + vec[4:5, :]).astype(BF16)
        leave_image(image, 0).start()
        leave_image(image, 1).start()
        valid = lax.broadcasted_iota(jnp.int32, (2 * QP, tokens), 1) < left_ref[image]
        stat = jnp.zeros((2 * QP, 128), F32)
        for pair in range(PAIRS):
            lanes = slice(pair * LANES, (pair + 1) * LANES)
            scores = dot_nt(two_heads(qc_ref[rows, lanes], masks), k_ref[image, :, lanes])
            scores = jnp.where(valid, scores, NEG)
            top = jnp.max(scores, axis=-1, keepdims=True)
            probs = jnp.exp(scores - top)
            total = jnp.sum(probs, axis=-1, keepdims=True)
            mixed = dot_nn(probs.astype(BF16), v_ref[image, :, lanes]) / total
            o_ref[image, :, lanes] = join_heads(mixed).astype(BF16)
            stat = jnp.where(column == pair, top + jnp.log(total), stat)
        stat_ref[image] = jnp.where(left_ref[image] > 0, stat.T[:8], NEG)
        leave_image(image, 2).start()
        if custom and image == 0:
            for pair in range(8, 16):
                feed.wait(pair)
            leave_weights(1).start()
    for number in range(len(small)):
        leave(number).wait()
    for image in range(images):
        for number in range(3):
            leave_image(image, number).wait()
    if custom:
        leave_weights(0).wait()
        leave_weights(1).wait()


def forward(left, flags, xb, memory, bufs, queries):
    custom = len(bufs) > 1
    rows = xb.shape[0]
    images, tokens, _ = memory.shape
    narrow = jax.ShapeDtypeStruct((rows, D), BF16)
    tall = jax.ShapeDtypeStruct(memory.shape, BF16)
    anywhere = pl.BlockSpec(memory_space=pl.ANY)
    small = pltpu.VMEM((rows, D), BF16)
    large = pltpu.VMEM(memory.shape, BF16)
    held = 16 * PAIR_ROWS if custom else 7 * D
    return pl.pallas_call(
        partial(forward_kernel, queries, custom),
        grid_spec=pltpu.PrefetchScalarGridSpec(
            num_scalar_prefetch=2,
            grid=(1,),
            in_specs=[whole((rows, D)), anywhere] + [anywhere] * len(bufs),
            out_specs=[anywhere] * 9 + [whole((images, 8, 2 * QP))] + [anywhere] * custom,
            scratch_shapes=[
                pltpu.VMEM((held, D), BF16),
                large, small, small, small, small,
                pltpu.VMEM((rows, D), F32),
                small, large, large,
                pltpu.VMEM((images, QP, D), BF16),
                pltpu.VMEM((32, D), BF16),
                pltpu.SemaphoreType.DMA((16,)),
                pltpu.SemaphoreType.DMA((images,)),
                pltpu.SemaphoreType.DMA((6,)),
                pltpu.SemaphoreType.DMA((images, 3)),
                pltpu.SemaphoreType.DMA(()),
                pltpu.SemaphoreType.DMA((2,)),
            ],
        ),
        out_shape=[
            narrow, narrow, narrow, narrow,
            jax.ShapeDtypeStruct((rows, D), F32),
            narrow, tall, tall,
            jax.ShapeDtypeStruct((images, QP, D), BF16),
            jax.ShapeDtypeStruct((images, 8, 2 * QP), F32),
        ]
        + [jax.ShapeDtypeStruct((held, D), BF16)] * custom,
        cost_estimate=cost(0, 0),
        compiler_params=params(60),
        name="forward",
    )(left, flags, xb, memory, *bufs)


def pieces(start, count, size):
    found = []
    done = 0
    while done < count:
        pair, offset = divmod(start + done, size)
        length = min(count - done, size - offset)
        found.append((done, pair, offset, length))
        done += length
    return found


class Halves:
    def __init__(self, keep, send, my_core):
        self.keep, self.send, self.my_core = keep, send, my_core

    def copy(self, target, source, pair, offset, length, sem):
        place = pair // self.cores()
        index = []
        for extent in reversed(target.shape[:-2]):
            index.insert(0, place % extent)
            place = place // extent
        return pltpu.make_async_copy(source, target.at[(*index, pl.ds(offset, length))], sem)

    def cores(self):
        return 1 if self.send is None else 2

    def start(self, source, pair, offset, length, sem):
        if self.send is None:
            self.copy(self.keep, source, pair, offset, length, sem).start()
            return

        @pl.when(self.my_core == pair % 2)
        def _():
            self.copy(self.keep, source, pair, offset, length, sem).start()

        @pl.when(self.my_core != pair % 2)
        def _():
            self.copy(self.send, source, pair, offset, length, sem).start()

    def wait(self, source, pair, offset, length, sem):
        self.copy(self.keep, source, pair, offset, length, sem).wait()


def middle_kernel(parts, split, *refs):
    flags, y1_ref = refs[:2]
    o_refs, stat_refs = refs[2 : 2 + parts], refs[2 + parts : 2 + 2 * parts]
    refs = refs[2 + 2 * parts :]
    w_hbm, vec, cot_ref, match_ref, out_hbm = refs[:5]
    halves = Halves(refs[5], refs[6] if split else None, flags[0])
    refs = refs[6 + split :]
    cross_halves = Halves(refs[0], refs[1] if split else None, flags[0])
    refs = refs[1 + split :]
    db_ref, doc_ref, tot_ref, dvec_ref = refs[:4]
    ocf, ocb, y2, x2b, u, slope, acc, e3b, staged, blank, out_ref, dco_ref, co, feed = refs[4:18]
    sems, blank_sem, out_sem, side_sems, w_sems = refs[18:]
    phase, step = pl.program_id(0), pl.program_id(1)
    steps = FF // D
    images = match_ref.shape[0]
    column = lax.broadcasted_iota(jnp.int32, (2 * QP, 128), 1)
    lane = lax.broadcasted_iota(jnp.int32, (QP, LANES), 1)
    size = halves.keep.shape[-2]
    side = cross_halves.keep.shape[-2]

    def load(block):
        target = co if block == 7 else feed.at[block - 8]
        return pltpu.make_async_copy(w_hbm.at[pl.ds(block * D, D)], target, w_sems.at[block - 7])

    def leave_out():
        return pltpu.make_async_copy(out_ref, out_hbm, out_sem)

    def leave_side(act):
        starts = [(dco_ref, 3 * D - QUERY_HEAD, D), (staged.at[0, 0], 4 * D - QUERY_HEAD, HEAD_ROWS)]
        for which, (source, start, count) in enumerate(starts):
            if (which == 0) != (act[0] == "o"):
                continue
            for number, (done, pair, offset, length) in enumerate(pieces(start, count, side)):
                piece = source.at[pl.ds(done, length)]
                getattr(cross_halves, act[1])(piece, pair, offset, length, side_sems.at[which, number])

    def leave(which, at, act):
        skip = HEAD_ROWS if which + at == 0 else 0
        start = which * FF + at * D + skip - HEAD_ROWS
        for number, (done, pair, offset, length) in enumerate(pieces(start, D - skip, size)):
            source = staged.at[at % 2, which, pl.ds(done + skip, length)]
            getattr(halves, act)(source, pair, offset, length, sems.at[at, which, number])

    def leave_blank(act):
        for _, pair, offset, length in pieces(2 * FF - HEAD_ROWS, TAIL, size):
            getattr(halves, act)(blank, pair, offset, length, blank_sem)

    def ordered(first, second):
        if parts != 2:
            return first, second
        swap = flags[1] != 0
        return jnp.where(swap, second, first), jnp.where(swap, first, second)

    @pl.when((phase == 0) & (step == 0))
    def _():
        load(7).start()
        for at in range(steps):
            load(8 + at).start()
            load(8 + steps + at).start()
        for image in range(images):
            rows = slice(image * QP, (image + 1) * QP)
            stats = [ref[image] for ref in stat_refs]
            if parts == 2:
                stats = ordered(*stats)
            top = stats[0]
            for n in range(1, parts):
                top = jnp.maximum(top, stats[n])
            mass = [jnp.exp(stats[n] - top) for n in range(parts)]
            total = mass[0]
            for n in range(1, parts):
                total = total + mass[n]
            tot_ref[image, 0:8, :] = top + jnp.log(total)
            shares = [jnp.concatenate([m / total, jnp.zeros((120, 2 * QP), F32)], axis=0).T for m in mass]
            for pair in range(PAIRS):
                lanes = slice(pair * LANES, (pair + 1) * LANES)
                values = [ref[image, :, lanes].astype(F32) for ref in o_refs]
                if parts == 2:
                    values = ordered(*values)
                mixed = jnp.zeros((QP, LANES), F32)
                for n in range(parts):
                    share = shares[n][:, pair : pair + 1]
                    mixed = mixed + values[n] * jnp.where(lane < HEAD, share[:QP], share[QP:])
                ocf[rows, lanes] = mixed
        ocb[...] = ocf[...].astype(BF16)
        hat, _ = norm_parts(y1_ref[...])
        x1 = hat * vec[11:12, :] + vec[12:13, :]
        load(7).wait()
        total = x1 + (dot_nn(ocb[...], co[...]) + vec[5:6, :])
        y2[...] = total
        hat, _ = norm_parts(total)
        x2 = hat * vec[13:14, :] + vec[14:15, :]
        x2b[...] = x2.astype(BF16)
        acc[...] = x2 + vec[6:7, :]

    for at in range(steps):

        @pl.when((phase == 0) & (step == at))
        def _(at=at):
            load(8 + at).wait()
            load(8 + steps + at).wait()

    f1, f2 = feed.at[step], feed.at[steps + step]

    @pl.when(phase == 0)
    def _():
        h = dot_nt(x2b[...], f1[...]) + vec[pl.ds(7 + step, 1), :]
        root = 0.7978845608028654
        square = h * h
        t = jnp.tanh(root * (h + 0.044715 * (h * square)))
        half = 0.5 * (1.0 + t)
        slope[step] = half + (0.5 * root) * h * (1.0 - t * t) * (1.0 + 0.134145 * square)
        active = (h * half).astype(BF16)
        u[step] = active
        acc[...] += dot_nn(active, f2[...])

    @pl.when((phase == 1) & (step == 0))
    def _():
        blank[...] = jnp.zeros_like(blank)
        leave_blank("start")
        dvec_ref[...] = jnp.zeros_like(dvec_ref)
        hat, inverse = norm_parts(acc[...])
        out = hat * vec[15:16, :] + vec[16:17, :]
        grads = []
        for image in range(images):
            out_ref[image] = out[image * QP : (image + 1) * QP]
            matched = match_ref[image]
            hit = lax.broadcasted_iota(jnp.int32, (QP, matched.shape[1]), 0) == matched
            grads.append(dot_nn(jnp.where(hit, 1.0, 0.0).astype(BF16), cot_ref[image]))
        leave_out().start()
        dy = jnp.concatenate(grads, axis=0)
        dvec_ref[15:16, :] = rowsum(dy * hat)
        dvec_ref[16:17, :] = rowsum(dy)
        dc = norm_back(dy, hat, inverse, vec[15:16, :])
        low = dc.astype(BF16)
        e3b[...] = low
        dvec_ref[6:7, :] = rowsum(low)
        acc[...] = dc

    for at in range(2, steps):

        @pl.when((phase == 1) & (step == at))
        def _(at=at):
            leave(0, at - 2, "wait")
            leave(1, at - 2, "wait")
            if at == 2:
                leave_side(("f", "wait"))

    @pl.when(phase == 1)
    def _():
        du = dot_nt(e3b[...], f2[...])
        dh = (du * slope[step]).astype(BF16)
        slot = lax.rem(step, 2)
        staged[slot, 1] = dot_tn(u[step], e3b[...]).astype(BF16)
        staged[slot, 0] = dot_tn(dh, x2b[...]).astype(BF16)

        @pl.when(step == 0)
        def _():
            leave_side(("f", "start"))

        for at in range(steps):

            @pl.when(step == at)
            def _(at=at):
                leave(0, at, "start")
                leave(1, at, "start")

        dvec_ref[pl.ds(7 + step, 1), :] = rowsum(dh)
        acc[...] += dot_nn(dh, f1[...])

    @pl.when((phase == 1) & (step == steps - 1))
    def _():
        hat, inverse = norm_parts(y2[...])
        dy = acc[...]
        dvec_ref[13:14, :] = rowsum(dy * hat)
        dvec_ref[14:15, :] = rowsum(dy)
        db = norm_back(dy, hat, inverse, vec[13:14, :])
        db_ref[...] = db
        low = db.astype(BF16)
        dvec_ref[5:6, :] = rowsum(low)
        dco_ref[...] = dot_tn(ocb[...], low).astype(BF16)
        leave_side(("o", "start"))
        doc = dot_nt(low, co[...]).astype(BF16)
        doc_ref[...] = doc
        both = doc.astype(F32) * ocf[...]
        for image in range(images):
            rows = slice(image * QP, (image + 1) * QP)
            tot = jnp.zeros((2 * QP, 128), F32)
            for pair in range(PAIRS):
                piece = both[rows, pair * LANES : (pair + 1) * LANES]
                one = jnp.sum(jnp.where(lane < HEAD, piece, 0.0), axis=-1, keepdims=True)
                two = jnp.sum(jnp.where(lane < HEAD, 0.0, piece), axis=-1, keepdims=True)
                tot = jnp.where(column == pair, jnp.concatenate([one, two], axis=0), tot)
            tot_ref[image, 8:16, :] = tot.T[:8]
        leave_blank("wait")
        leave_out().wait()
        leave_side(("o", "wait"))
        for which in (0, 1):
            leave(which, steps - 2, "wait")
            leave(which, steps - 1, "wait")


def halves_shape(shape, split):
    return [jax.ShapeDtypeStruct(shape, BF16)] * (1 + split)


def middle(flags, y1, o_parts, stat_parts, w, vec, cot, matched, far_shape, cross_shape, split):
    rows = y1.shape[0]
    images = cot.shape[0]
    steps = FF // D
    parts = len(o_parts)
    anywhere = pl.BlockSpec(memory_space=pl.ANY)
    return pl.pallas_call(
        partial(middle_kernel, parts, split),
        grid_spec=pltpu.PrefetchScalarGridSpec(
            num_scalar_prefetch=1,
            grid=(2, steps),
            in_specs=[whole(y1.shape)]
            + [whole(o_parts[0].shape)] * parts
            + [whole(stat_parts[0].shape)] * parts
            + [anywhere, whole((VECS, D)), whole(cot.shape), whole((images, 1, matched.shape[1]))],
            out_specs=[anywhere] * (3 + 2 * split)
            + [
                whole((rows, D)),
                whole((rows, D)),
                whole((images, 16, 2 * QP)),
                whole((VECS, D)),
            ],
            scratch_shapes=[
                pltpu.VMEM((rows, D), F32),
                pltpu.VMEM((rows, D), BF16),
                pltpu.VMEM((rows, D), F32),
                pltpu.VMEM((rows, D), BF16),
                pltpu.VMEM((steps, rows, D), BF16),
                pltpu.VMEM((steps, rows, D), F32),
                pltpu.VMEM((rows, D), F32),
                pltpu.VMEM((rows, D), BF16),
                pltpu.VMEM((2, 2, D, D), BF16),
                pltpu.VMEM((TAIL, D), BF16),
                pltpu.VMEM((images, QP, D), F32),
                pltpu.VMEM((D, D), BF16),
                pltpu.VMEM((D, D), BF16),
                pltpu.VMEM((2 * steps, D, D), BF16),
                pltpu.SemaphoreType.DMA((steps, 2, 2)),
                pltpu.SemaphoreType.DMA(()),
                pltpu.SemaphoreType.DMA(()),
                pltpu.SemaphoreType.DMA((2, 2)),
                pltpu.SemaphoreType.DMA((1 + 2 * steps,)),
            ],
        ),
        out_shape=[jax.ShapeDtypeStruct((images, QP, D), F32)]
        + halves_shape(far_shape, split)
        + halves_shape(cross_shape, split)
        + [
            jax.ShapeDtypeStruct((rows, D), F32),
            jax.ShapeDtypeStruct((rows, D), BF16),
            jax.ShapeDtypeStruct((images, 16, 2 * QP), F32),
            jax.ShapeDtypeStruct((VECS, D), F32),
        ],
        cost_estimate=cost(2 * rows * D * (6 * FF + 3 * D), 2 * FF * D * 6),
        compiler_params=params(60),
        name="middle",
    )(flags, y1, *o_parts, *stat_parts, w, vec, cot, matched[:, None, :])


def cross_backward_kernel(left_ref, q_ref, k_ref, v_ref, do_ref, tot_ref, dq_ref, dk_ref, dv_ref):
    tokens = k_ref.shape[1]
    masks = head_masks()
    valid = lax.broadcasted_iota(jnp.int32, (tokens, 2 * QP), 0) < left_ref[pl.program_id(0)]
    for pair in range(PAIRS):
        lanes = slice(pair * LANES, (pair + 1) * LANES)
        key, value = k_ref[0, :, lanes], v_ref[0, :, lanes]
        query = two_heads(q_ref[0, :, lanes], masks)
        dout = two_heads(do_ref[0, :, lanes], masks)
        scores = dot_nt(key, query)
        probs = jnp.where(valid, jnp.exp(scores - tot_ref[0, pair : pair + 1, :]), 0.0)
        dprobs = dot_nt(value, dout)
        dscores = (probs * (dprobs - tot_ref[0, 8 + pair : 9 + pair, :])).astype(BF16)
        dv_ref[0, :, lanes] = dot_nn(probs.astype(BF16), dout).astype(BF16)
        dk_ref[0, :, lanes] = dot_nn(dscores, query).astype(BF16)
        dq_ref[0, :, lanes] = join_heads(dot_tn(key, dscores).T).astype(BF16)


def cross_backward(left, qc, key, value, doc, tot):
    images, tokens, _ = key.shape
    q_block = pl.BlockSpec((1, QP, D), lambda i, _: (i, 0, 0))
    m_block = pl.BlockSpec((1, tokens, D), lambda i, _: (i, 0, 0))
    s_block = pl.BlockSpec((1, 16, 2 * QP), lambda i, _: (i, 0, 0))
    return pl.pallas_call(
        cross_backward_kernel,
        grid_spec=pltpu.PrefetchScalarGridSpec(
            num_scalar_prefetch=1,
            grid=(images,),
            in_specs=[q_block, m_block, m_block, q_block, s_block],
            out_specs=[q_block, m_block, m_block],
        ),
        out_shape=[
            jax.ShapeDtypeStruct((images, QP, D), BF16),
            jax.ShapeDtypeStruct(key.shape, BF16),
            jax.ShapeDtypeStruct(key.shape, BF16),
        ],
        cost_estimate=cost(4 * images * 2 * QP * tokens * D // 3, images * tokens * D * 8),
        compiler_params=params(60),
        name="cross_backward",
    )(left, qc.reshape(images, QP, D), key, value, doc.reshape(images, QP, D), tot)


def memory_weights_kernel(split, flags, *refs):
    m_ref, dk_ref, dv_ref = refs[1 + split : 4 + split]
    refs = refs[4 + split :]
    if split:
        a, b, c, d = refs[:4]
        far_out = refs[-4]
        far_out[0] = add(a[...], b[...])
        far_out[1] = add(c[...], d[...])
        refs = refs[4:-4] + refs[-3:]
    gb_ref = refs[0]
    halves = Halves(refs[1], refs[2] if split else None, flags[0])
    sums, low, sems = refs[2 + split :]
    step = pl.program_id(0)
    dv = dv_ref[0]
    more = [dot_tn(m_ref[0], dk_ref[0]), dot_tn(m_ref[0], dv)]

    @pl.when(step == 0)
    def _():
        for which in (0, 1):
            sums[which] = more[which]
        gb_ref[...] = jnp.broadcast_to(rowsum(dv), gb_ref.shape)

    @pl.when(step > 0)
    def _():
        for which in (0, 1):
            sums[which] += more[which]
        gb_ref[...] += jnp.broadcast_to(rowsum(dv), gb_ref.shape)

    def leave(which, act):
        start = (1 + which) * D - QUERY_HEAD
        for number, (done, pair, offset, length) in enumerate(pieces(start, D, halves.keep.shape[-2])):
            piece = low.at[which, pl.ds(done, length)]
            getattr(halves, act)(piece, pair, offset, length, sems.at[which, number])

    @pl.when(step == pl.num_programs(0) - 1)
    def _():
        for which in (0, 1):
            low[which] = sums[which].astype(BF16)
            leave(which, "start")
        for which in (0, 1):
            leave(which, "wait")


def memory_weights(flags, cross, memory, dk, dv, far, split):
    images, tokens, _ = memory.shape
    block = pl.BlockSpec((1, tokens, D), lambda i, _: (i, 0, 0))
    anywhere = pl.BlockSpec(memory_space=pl.ANY)
    far = [blocks_of(part) for part in far]
    part = D // images
    sources, far_specs, far_out, far_shape = [], [], [], []
    if split:
        rows = far[0].shape[-2]
        for r in (0, 1):
            for array in far:
                sources.append(array)
                far_specs.append(
                    pl.BlockSpec((None, None, None, rows, part), lambda i, f, r=r: (r, 1 - f[2], f[1], 0, i))
                )
        far_out = [pl.BlockSpec((2, rows, part), lambda i, f: (0, 0, i))]
        far_shape = [jax.ShapeDtypeStruct((2, rows, D), BF16)]
    return pl.pallas_call(
        partial(memory_weights_kernel, split),
        grid_spec=pltpu.PrefetchScalarGridSpec(
            num_scalar_prefetch=1,
            grid=(images,),
            in_specs=[anywhere] * (1 + split) + [block, block, block] + far_specs,
            out_specs=[whole((8, D))] + [anywhere] * (1 + split) + far_out,
            scratch_shapes=[
                pltpu.VMEM((2, D, D), F32),
                pltpu.VMEM((2, D, D), BF16),
                pltpu.SemaphoreType.DMA((2, 2)),
            ],
        ),
        out_shape=[jax.ShapeDtypeStruct((8, D), F32)] + halves_shape(cross[0].shape, split) + far_shape,
        input_output_aliases={1 + n: 1 + n for n in range(1 + split)},
        cost_estimate=cost(4 * images * tokens * D * D, images * tokens * D * 6),
        compiler_params=params(60),
        name="memory_weights",
    )(flags, *cross, memory, dk, dv, *sources)


def memory_grads_kernel(dk_ref, dv_ref, ck, cv, gm_ref):
    gm_ref[0] = dot_nt(dk_ref[0], ck[...]) + dot_nt(dv_ref[0], cv[...])


def memory_grads(dk, dv, w):
    images, tokens, _ = dk.shape
    block = pl.BlockSpec((1, tokens, D), lambda i: (i, 0, 0))
    return pl.pallas_call(
        memory_grads_kernel,
        grid=(images,),
        in_specs=[block, block, weight_block(5), weight_block(6)],
        out_specs=block,
        out_shape=jax.ShapeDtypeStruct(dk.shape, F32),
        cost_estimate=pl.CostEstimate(
            flops=4 * images * tokens * D * D, bytes_accessed=images * tokens * D * 8, transcendentals=0
        ),
        compiler_params=params(60),
        name="memory_grads",
    )(dk, dv, w, w)


class Loads:
    def __init__(self, pairs, sems):
        self.copies = [(pltpu.make_async_copy(source, target, sems.at[n]), target) for n, (source, target) in enumerate(pairs)]
        self.ready = set()
        for copy, _ in self.copies:
            copy.start()

    def __call__(self, number):
        copy, target = self.copies[number]
        if number not in self.ready:
            copy.wait()
            self.ready.add(number)
        return target[...]


def query_backward_kernel(parts, split, flags, *refs):
    sources, vec = refs[1 + split : 4 + split + parts], refs[4 + split + parts]
    refs = refs[5 + split + parts :]
    da_ref, gq_head_ref, dvec_ref = refs[:3]
    halves = Halves(refs[3], refs[4] if split else None, flags[0])
    refs = refs[4 + split :]
    targets, staged, load_sems, sems = refs[: 3 + parts], refs[3 + parts], refs[4 + parts], refs[5 + parts]
    w_hbm = sources[-1]
    sources = [*sources[:-1], w_hbm.at[pl.ds(4 * D, D)]]
    get = Loads(list(zip(sources, targets)), load_sems)

    def leave(act):
        for number, (done, pair, offset, length) in enumerate(pieces(0, D - QUERY_HEAD, halves.keep.shape[-2])):
            piece = staged.at[pl.ds(done + QUERY_HEAD, length)]
            getattr(halves, act)(piece, pair, offset, length, sems.at[number])

    total = get(0).astype(F32)
    for number in range(1, parts):
        total = total + get(number).astype(F32)
    dq = total.astype(BF16) * SCALE
    hat, inverse = norm_parts(get(parts))
    gain = vec[11:12, :]
    x1b = (hat * gain + vec[12:13, :]).astype(BF16)
    gcq = dot_tn(x1b, dq).astype(BF16)
    staged[...] = gcq
    leave("start")
    gq_head_ref[...] = gcq[:QUERY_HEAD]
    dvec_ref[...] = jnp.zeros_like(dvec_ref)
    dvec_ref[3:4, :] = rowsum(dq)
    dy = get(parts + 1) + dot_nt(dq, get(parts + 2))
    dvec_ref[11:12, :] = rowsum(dy * hat)
    dvec_ref[12:13, :] = rowsum(dy)
    da = norm_back(dy, hat, inverse, gain)
    da_ref[...] = da
    dvec_ref[2:3, :] = rowsum(da.astype(BF16))
    leave("wait")


def query_backward(flags, cross, y1, db, dq_parts, w, vec, split):
    rows = y1.shape[0]
    parts = len(dq_parts)
    full = whole((rows, D))
    anywhere = pl.BlockSpec(memory_space=pl.ANY)
    return pl.pallas_call(
        partial(query_backward_kernel, parts, split),
        grid_spec=pltpu.PrefetchScalarGridSpec(
            num_scalar_prefetch=1,
            grid=(1,),
            in_specs=[anywhere] * (4 + split + parts) + [whole((VECS, D))],
            out_specs=[full, whole((QUERY_HEAD, D)), whole((VECS, D))] + [anywhere] * (1 + split),
            scratch_shapes=[pltpu.VMEM((rows, D), BF16)] * parts
            + [pltpu.VMEM((rows, D), F32)] * 2
            + [pltpu.VMEM((D, D), BF16)] * 2
            + [pltpu.SemaphoreType.DMA((parts + 3,)), pltpu.SemaphoreType.DMA((2,))],
        ),
        out_shape=[
            jax.ShapeDtypeStruct((rows, D), F32),
            jax.ShapeDtypeStruct((QUERY_HEAD, D), BF16),
            jax.ShapeDtypeStruct((VECS, D), F32),
        ]
        + halves_shape(cross[0].shape, split),
        input_output_aliases={1 + n: 3 + n for n in range(1 + split)},
        cost_estimate=cost(4 * rows * D * D, rows * D * 16),
        compiler_params=params(60),
        name="query_backward",
    )(flags, *cross, *[part.reshape(rows, D) for part in dq_parts], y1, db, w, vec)


def self_backward_kernel(queries, split, *refs):
    flags, os_hbm, da_hbm, qs_hbm, ks_hbm, vs_hbm, x_hbm, w_hbm, gq_ref, gx_ref, dvec_ref, keep_ref = refs[:12]
    halves = Halves(keep_ref, refs[12] if split else None, flags[0])
    sq, sk, sv, g_ref, os_ref, da_ref, ao, qs, ks, vs, x_ref, aq, ak, av, sems, load_sems = refs[12 + split :]
    size = keep_ref.shape[-2]
    matrices = [w_hbm.at[pl.ds(block * D, D)] for block in range(4)]
    get = Loads(
        [(os_hbm, os_ref), (da_hbm, da_ref), (matrices[3], ao), (qs_hbm, qs), (ks_hbm, ks), (vs_hbm, vs)]
        + [(x_hbm, x_ref), (matrices[0], aq), (matrices[1], ak), (matrices[2], av)],
        load_sems,
    )

    def leave(pair, act):
        getattr(halves, act)(g_ref.at[pl.ds(pair * size, size)], pair, 0, size, sems.at[pair])

    pairs = g_ref.shape[0] // size
    images = x_ref.shape[0] // QP
    dvec_ref[...] = jnp.zeros_like(dvec_ref)
    os = get(0)
    da = get(1)
    low = da.astype(BF16)
    g_ref[4 * D :, :] = gq_ref[...]
    g_ref[3 * D : 4 * D, :] = dot_tn(os, low).astype(BF16)
    dos = dot_nt(low, get(2)).astype(BF16)
    for number in (3, 4, 5):
        get(number)
    masks = head_masks()
    real = lax.broadcasted_iota(jnp.int32, (QP, 2 * QP), 0) < queries
    for image in range(images):
        rows = slice(image * QP, (image + 1) * QP)
        for pair in range(PAIRS):
            lanes = slice(pair * LANES, (pair + 1) * LANES)
            key, value = ks[rows, lanes], vs[rows, lanes]
            query = two_heads(qs[rows, lanes], masks)
            dout = two_heads(dos[rows, lanes], masks)
            scores = jnp.where(real, dot_nt(key, query), NEG)
            probs = jnp.exp(scores - jnp.max(scores, axis=0, keepdims=True))
            probs = probs / jnp.sum(probs, axis=0, keepdims=True)
            dprobs = dot_nt(value, dout)
            dscores = (probs * (dprobs - jnp.sum(probs * dprobs, axis=0, keepdims=True))).astype(BF16)
            sv[rows, lanes] = dot_nn(probs.astype(BF16), dout).astype(BF16)
            sk[rows, lanes] = dot_nn(dscores, query).astype(BF16)
            sq[rows, lanes] = join_heads(dot_tn(key, dscores).T).astype(BF16) * SCALE
    dvec_ref[0:1, :] = rowsum(sq[...])
    dvec_ref[1:2, :] = rowsum(sv[...])
    xb = get(6)
    g_ref[2 * D : 3 * D, :] = dot_tn(xb, sv[...]).astype(BF16)
    for pair in range(2, pairs):
        leave(pair, "start")
    g_ref[D : 2 * D, :] = dot_tn(xb, sk[...]).astype(BF16)
    for pair in range(1, min(2, pairs)):
        leave(pair, "start")
    g_ref[0:D, :] = dot_tn(xb, sq[...]).astype(BF16)
    leave(0, "start")
    gx = da + dot_nt(sq[...], get(7)) + dot_nt(sk[...], get(8)) + dot_nt(sv[...], get(9))
    for image in range(images):
        gx_ref[image] = gx[image * QP : (image + 1) * QP]
    for pair in range(pairs):
        leave(pair, "wait")


def self_backward(flags, xb, qs, ks, vs, os, da, gq_head, w, queries, shape, split):
    rows = xb.shape[0]
    images = rows // QP
    anywhere = pl.BlockSpec(memory_space=pl.ANY)
    return pl.pallas_call(
        partial(self_backward_kernel, queries, split),
        grid_spec=pltpu.PrefetchScalarGridSpec(
            num_scalar_prefetch=1,
            grid=(1,),
            in_specs=[anywhere] * 7 + [whole((QUERY_HEAD, D))],
            out_specs=[whole((images, QP, D)), whole((VECS, D))] + [anywhere] * (1 + split),
            scratch_shapes=[pltpu.VMEM((rows, D), BF16)] * 3
            + [pltpu.VMEM((4 * D + QUERY_HEAD, D), BF16), pltpu.VMEM((rows, D), BF16), pltpu.VMEM((rows, D), F32)]
            + [pltpu.VMEM((D, D), BF16)]
            + [pltpu.VMEM((rows, D), BF16)] * 4
            + [pltpu.VMEM((D, D), BF16)] * 3
            + [pltpu.SemaphoreType.DMA((4,)), pltpu.SemaphoreType.DMA((10,))],
        ),
        out_shape=[
            jax.ShapeDtypeStruct((images, QP, D), F32),
            jax.ShapeDtypeStruct((VECS, D), F32),
        ]
        + halves_shape(shape, split),
        cost_estimate=cost(16 * rows * D * D * 2, 8 * D * D * 2),
        compiler_params=params(60),
        name="self_backward",
    )(flags, os, da, qs, ks, vs, xb, w, gq_head)


class Place:
    def __init__(self):
        place = lax.axis_index("dp")
        self.x = lax.axis_index("seq")
        self.c = lax.rem(place, 2)
        self.y = lax.rem(place // 2, 2)
        self.z = place // 4


def pick(array, index, axis):
    return lax.dynamic_index_in_dim(array, index, axis, keepdims=False)


def over_core(v):
    return lax.ppermute(v, "dp", [(i, i ^ 1) for i in range(16)])


def over_y(v):
    return lax.ppermute(v, "dp", [(i, i ^ 2) for i in range(16)])


def over_x(v):
    return lax.ppermute(v, "seq", [(0, 1), (1, 0)])


def over_z(v, hops):
    return lax.ppermute(v, "dp", [(4 * a + i, 4 * b + i) for a, b in hops for i in range(4)])


def over_far(v):
    return over_z(v, [(0, 2), (2, 0), (1, 3), (3, 1)])


def over_near(v):
    return over_z(v, SWAP_ONE)


def spread(own):
    x, y, z = over_x(own), over_y(own), over_near(own)
    xy, yz, zx = over_x(y), over_y(z), over_near(x)
    return own, x, y, z, xy, yz, zx


def gather(at, rows):
    low = at.x == 0
    edge = over_x(jnp.where(low, rows[-8:], rows[:8]))
    own = jnp.where(low, jnp.concatenate([rows, edge]), jnp.concatenate([edge, rows]))
    other = over_far(own)
    here, there = spread(own), spread(other)
    found = [*here, over_x(here[5]), *there, over_y(there[6])]
    return found + [over_core(part) for part in found]


def tie(*values):
    return lax.optimization_barrier(values)


def add(kept, came):
    return (kept.astype(F32) + came.astype(F32)).astype(BF16)


def own_half(pairs, x):
    half = pairs.shape[-2] // 2
    return pick(pairs.reshape(*pairs.shape[:-2], 2, half, D), x, pairs.ndim - 2)


def blocks_of(pairs):
    return pairs.reshape(*pairs.shape[:-2], 2, pairs.shape[-2] // 2, D)


def picked(pairs, half, x):
    return pick(pick(pairs, half, 0), x, 0)


def merge(body, flags, sources, out_rows, name):
    parts = 3
    specs = []
    for array, where in sources:
        lead = (None,) * (array.ndim - 2)
        shape = (*lead, array.shape[-2], D // parts)
        specs.append(pl.BlockSpec(shape, lambda i, f, where=where: (*where(f), 0, i)))
    return pl.pallas_call(
        body,
        grid_spec=pltpu.PrefetchScalarGridSpec(
            num_scalar_prefetch=1,
            grid=(parts,),
            in_specs=specs,
            out_specs=[
                pl.BlockSpec((*rows, D // parts), lambda i, f, n=len(rows): (*[0] * n, i)) for rows in out_rows
            ],
        ),
        out_shape=[jax.ShapeDtypeStruct((*rows, D), BF16) for rows in out_rows],
        cost_estimate=cost(0, 0),
        compiler_params=params(60),
        name=name,
    )(flags, *[array for array, _ in sources])


def core_merge_kernel(flags, *refs):
    ins, outs = refs[:14], refs[14:]
    for number in range(2):
        first, second, third = ins[3 * number : 3 * number + 3]
        outs[number][...] = (first[...].astype(F32) + second[...].astype(F32) + third[...].astype(F32)).astype(BF16)
    outs[2][...] = add(ins[6][...], ins[7][...])
    outs[3][...] = add(ins[8][...], ins[9][...])
    message = outs[4]
    block = ins[10].shape[0]
    message[:block, :] = add(ins[10][...], ins[11][...])
    spill = message.shape[0] - (block + 8)
    total = ins[12][...].astype(F32) + ins[13][...].astype(F32)
    message[block:, :] = jnp.concatenate([jnp.zeros((8, total.shape[1]), F32), total[block - spill :]]).astype(BF16)


def core_merge(flags, far, far_came, far_last, cross, cross_came):
    far, far_came, cross, cross_came = [blocks_of(v) for v in (far, far_came, cross, cross_came)]
    block = cross.shape[-2]
    spill = 2 * block - (D - QUERY_HEAD)
    sources = []
    for r in (lambda f: 1 - f[3] % 2, lambda f: f[3] % 2):
        sources += [(part, lambda f, r=r: (r(f), f[2], f[1])) for part in (far, far_came)]
        sources += [(far_last, lambda f, r=r: (r(f),))]
    chosen = [
        lambda f: (0, f[1]),
        lambda f: (1, f[1]),
        lambda f: (1 - f[0], 1 - f[1]),
        lambda f: (0, 1 - f[1]),
    ]
    for where in chosen:
        sources += [(cross, where), (cross_came, where)]
    return merge(core_merge_kernel, flags, sources, [(block,)] * 4 + [(block + 8 + spill,)], "core_merge")


def cross_second(at, mine, came):
    start = D - QUERY_HEAD
    block = mine[0].shape[-2]
    spill = 2 * block - start
    main = came[:block].astype(F32)
    tall = jnp.concatenate([jnp.zeros((block - spill, D), F32), came[block + 8 :].astype(F32)])
    ids = (at.c * 2 + at.x) * block + jnp.arange(block)[:, None]

    def half(index, y):
        part = jnp.where((at.c == 0) & (y == 0), tall, main)
        place = ids + y * 4 * block
        shared = (place >= start) & (place < start + 2 * D)
        own = jnp.where(index == 0, mine[0], mine[1]).astype(F32)
        return (own + jnp.where(shared, part, 0.0)).astype(BF16)

    return half(1 - at.y, 1 - at.y), half(at.y, at.y)


SWAP_ONE = [(0, 1), (1, 0), (2, 3), (3, 2)]
SWAP_TWO = [(0, 2), (2, 0), (1, 3), (3, 1)]


def finish(at, flags, block, far, far_last, near, near_send, cross, cross_came, vec_rows, extra):
    near_came = over_core(near_send)
    vec_came = over_core(vec_rows)
    far_out, far, low, high, message = core_merge(flags, *far, far_last, cross, cross_came)
    near_came, message, far_out, low, high, far = tie(near_came, message, far_out, low, high, far)
    came, far_came = over_x(message), over_z(far_out, SWAP_ONE)
    near, near_came = blocks_of(near), blocks_of(near_came)
    near_send = add(picked(near, 1 - at.y, at.x), picked(near_came, 1 - at.y, at.x))
    near = add(picked(near, at.y, at.x), picked(near_came, at.y, at.x))
    vec_rows = vec_rows + vec_came
    near_send, near, vec_rows, dk, dv, w = tie(near_send, near, vec_rows, *extra)
    near_came, vec_came = over_y(near_send), over_y(vec_rows)
    gm = memory_grads(dk, dv, w)
    gm, came = tie(gm, came)
    send, cross = cross_second(at, (low, high), came)
    send, near_came, far_came, cross = tie(send, near_came, far_came, cross)

    near = add(near, near_came)
    far = add(far, far_came)
    vec_rows = vec_rows + vec_came
    near, far, vec_rows, send = tie(near, far, vec_rows, send)
    cross_came, near_came = over_y(send), over_z(near, [(3, 2), (1, 0)])
    cut = block // 16 * 8
    far_top, vec_came = over_z(far[:cut], [(0, 2), (1, 3)]), over_z(vec_rows, SWAP_ONE)
    cross = add(cross, cross_came)
    near = add(near, near_came)
    vec_rows = vec_rows + vec_came
    near, cross, vec_rows, far_top, far = tie(near, cross, vec_rows, far_top, far)

    cross_came, near_came = over_z(cross, [(3, 2), (0, 1)]), over_z(near, [(2, 0)])
    far_low, vec_came = over_z(far[cut:], [(0, 2), (1, 3)]), over_z(vec_rows, SWAP_TWO)
    cross = add(cross, cross_came)
    vec_rows = vec_rows + vec_came
    near_came, cross, vec_rows, far_low = tie(near_came, cross, vec_rows, far_low)

    cross_came = over_z(cross, [(2, 1)])
    far_came = jnp.concatenate([far_top, far_low])
    kept = jnp.where(at.z >= 2, far, jnp.where(at.z == 0, near, cross))
    came = jnp.where(at.z >= 2, far_came, jnp.where(at.z == 0, near_came, cross_came))
    grad_rows = kept.astype(F32) + came.astype(F32)
    start = VEC_ROW - 31 * block
    last = jnp.concatenate([grad_rows[:start], vec_rows, jnp.zeros((block - start - VECS, D), F32)])
    is_last = (lax.axis_index("dp") == 15) & (at.x == 1)
    return jnp.where(is_last, last, grad_rows), gm


def shards(custom, inputs, memory, lengths, matched, cotangent, weights):
    axes = ("dp", "seq")
    share = 1.0 / lax.axis_size("seq")
    images, queries, _ = inputs.shape
    tokens = memory.shape[1]
    block = weights.shape[1]
    at = Place()
    left = lengths - at.x * tokens
    flags = jnp.stack([at.c if custom else 0, at.x, at.y, at.z]).astype(jnp.int32)

    def parts_of(value):
        if custom:
            return [value, over_x(value)]
        gathered = lax.all_gather(value, "seq")
        return [gathered[n] for n in range(gathered.shape[0])]

    if custom:
        bufs = gather(at, weights[0])
    else:
        bufs = [lax.all_gather(weights[0], axes, axis=0, tiled=True)]
    xb = jnp.pad(inputs, ((0, 0), (0, QP - queries), (0, 0))).reshape(images * QP, D)
    qs, ks, vs, os, y1, qc, key, value, mixed, stat, *w = forward(left, flags, xb, memory, bufs, queries)
    w = w[0] if custom else bufs[0]
    vec = w[VEC_ROW : VEC_ROW + VECS].astype(F32)
    near_rows = 4 * D + QUERY_HEAD
    far_rows = 2 * FF - HEAD_ROWS + TAIL
    cross_rows = 4 * D - QUERY_HEAD + HEAD_ROWS
    far_shape = (2, 2, 2 * block, D) if custom else (far_rows, D)
    near_shape = (2, 2 * block, D) if custom else (near_rows, D)
    cross_shape = (2, 2 * block, D) if custom else (cross_rows, D)
    out, *grads, db, doc, tot, dvec_mid = middle(
        flags, y1, parts_of(mixed), parts_of(stat), w, vec, cotangent, matched, far_shape, cross_shape, custom
    )
    far, cross = grads[: 1 + custom], grads[1 + custom :]
    if custom:
        far_came = over_core(far[1])
    dq, dk, dv = cross_backward(left, qc, key, value, doc, tot)
    dq_parts = parts_of(dq)
    if custom:
        far = [far[0], far_came]
    dcv_row, *cross = memory_weights(flags, cross, memory, dk, dv, far, custom)
    if custom:
        dcv_row = dcv_row + over_x(dcv_row)
        dq_parts[1], message = tie(dq_parts[1], cross.pop())
        far_last = over_y(message)
    da, gq_head, dvec_query, *cross = query_backward(flags, cross, y1, db, dq_parts, w, vec, custom)
    if custom:
        cross_came = over_core(cross[1])
    gq_head, dcv_row = tie(gq_head, dcv_row)
    gx, dvec_self, *near = self_backward(
        flags, xb, qs, ks, vs, os, da, gq_head, w, queries, near_shape, custom
    )
    vec_rows = (dvec_mid + dvec_query + dvec_self) * (1.0 if custom else share)
    is_value_bias = jnp.arange(VECS)[:, None] == 4
    vec_rows = jnp.where(is_value_bias, dcv_row[0:1], vec_rows)
    if custom:
        far_last, near_send = tie(far_last, near[1])
        grad_rows, gm = finish(
            at, flags, block, far, far_last, near[0], near_send, cross[0], cross_came, vec_rows, (dk, dv, w)
        )
    else:
        gm = memory_grads(dk, dv, w)
        low_share = jnp.asarray(share, BF16)
        pad = lax.axis_size(axes) * block - VEC_ROW - VECS
        last = 2 * FF - HEAD_ROWS
        memory_rows = slice(D - QUERY_HEAD, 3 * D - QUERY_HEAD)
        grads = jnp.concatenate(
            [near[0] * low_share, cross[0][: memory_rows.start] * low_share, cross[0][memory_rows]]
            + [cross[0][memory_rows.stop :] * low_share, far[0][:last] * low_share]
            + [vec_rows.astype(BF16), jnp.zeros((pad, D), BF16)]
        )
        grad_rows = lax.psum_scatter(grads, axes, scatter_dimension=0, tiled=True).astype(F32)
    return out[:, :queries], gx[:, :queries], gm, grad_rows[None]


def solution(mesh):
    placed = (
        P("dp", None, None),
        P("dp", "seq", None),
        P("dp"),
        P("dp", None),
        P("dp", None, None),
        P(None, ("dp", "seq"), None),
    )
    custom = dict(mesh.shape) == {"dp": 16, "seq": 2}
    return jax.shard_map(
        partial(shards, custom),
        mesh=mesh,
        in_specs=placed,
        out_specs=(
            P("dp", None, None),
            P("dp", None, None),
            P("dp", "seq", None),
            P(None, ("dp", "seq"), None),
        ),
        check_vma=False,
    )
```

```python
from functools import partial

import jax
import jax.numpy as jnp
from jax import lax
from jax.experimental import pallas as pl
from jax.experimental.pallas import tpu as pltpu
from jax.sharding import PartitionSpec as P

D = 768
H = 12
HEAD = 64
FF = 3072
PAIRS = H // 2
LANES = 2 * HEAD
QP = 112
VEC_ROW = 8 * D + 2 * FF
VECS = 24
TAIL = 256
HEAD_ROWS = 128
QUERY_HEAD = 64
SCALE = HEAD ** (-0.5)
EPS = 1e-05
NEG = -1e30
F32 = jnp.float32
BF16 = jnp.bfloat16
MIB = 1024 * 1024


def dot_nn(a, b):
    return lax.dot_general(a, b, (((1,), (0,)), ((), ())), preferred_element_type=F32)


def dot_nt(a, b):
    return lax.dot_general(a, b, (((1,), (1,)), ((), ())), preferred_element_type=F32)


def dot_tn(a, b):
    return lax.dot_general(a, b, (((0,), (0,)), ((), ())), preferred_element_type=F32)


def norm_parts(v):
    center = v - jnp.mean(v, axis=-1, keepdims=True)
    inverse = lax.rsqrt(jnp.mean(center * center, axis=-1, keepdims=True) + EPS)
    return center * inverse, inverse


def norm_back(dy, hat, inverse, gain):
    scaled = dy * gain
    mean_one = jnp.mean(scaled, axis=-1, keepdims=True)
    mean_two = jnp.mean(scaled * hat, axis=-1, keepdims=True)
    return inverse * (scaled - mean_one - hat * mean_two)


def rowsum(v):
    return jnp.sum(v.astype(F32), axis=0, keepdims=True)


def head_masks():
    lane = lax.broadcasted_iota(jnp.int32, (1, LANES), 1)
    first = jnp.where(lane < HEAD, 1.0, 0.0)
    return first.astype(BF16), (1.0 - first).astype(BF16)


def two_heads(block, masks):
    return jnp.concatenate([block * masks[0], block * masks[1]], axis=0)


def join_heads(stacked):
    lane = lax.broadcasted_iota(jnp.int32, (QP, LANES), 1)
    return jnp.where(lane < HEAD, stacked[:QP], stacked[QP:])


def weight_block(index):
    return pl.BlockSpec((D, D), lambda *_: (index, 0))


def whole(shape):
    return pl.BlockSpec(shape, lambda *_: (0,) * len(shape))


def params(mib):
    return pltpu.CompilerParams(vmem_limit_bytes=mib * MIB)


def cost(flops, moved):
    return pl.CostEstimate(flops=flops // 1000, bytes_accessed=moved // 1000, transcendentals=0)


FIRST_BLOCKS = (0, 1, 2, 5, 6, 3, 4)
SPREAD = ((0, 0, 0), (0, 0, 1), (0, 1, 0), (1, 0, 0), (0, 1, 1), (1, 1, 0), (1, 0, 1), (1, 1, 1))
PAIR_ROWS = 784
HOLDER = (3, 1, 1, 1)


class Assembly:
    def __init__(self, flags, bufs, weights, sems, vec_low, vec_sem):
        self.core, self.x, self.y, self.z = flags[0], flags[1], flags[2], flags[3]
        self.bufs, self.weights, self.sems = bufs, weights, sems
        self.vec_low, self.vec_sem = vec_low, vec_sem
        self.ready = set()

    def buf(self, dc, dz2, spread):
        return self.bufs[dc * 16 + dz2 * 8 + SPREAD.index(spread)]

    def start_vec(self):
        first = VEC_ROW - 15 * PAIR_ROWS - 384
        for dc in (0, 1):
            for dz2 in (0, 1):
                for dz1, dy, dx in SPREAD:
                    here = (self.z ^ (2 * dz2 + dz1), self.y ^ dy, self.core ^ dc, self.x ^ dx)
                    hit = (here[0] == HOLDER[0]) & (here[1] == HOLDER[1]) & (here[2] == HOLDER[2]) & (here[3] == HOLDER[3])

                    @pl.when(hit)
                    def _(source=self.buf(dc, dz2, (dz1, dy, dx))):
                        pltpu.make_async_copy(source.at[pl.ds(first, 32)], self.vec_low, self.vec_sem).start()

    def wait_vec(self):
        pltpu.make_async_copy(self.weights.at[pl.ds(0, 32)], self.vec_low, self.vec_sem).wait()

    def start_group(self, dz2):
        def rows(start, count):
            return pl.ds(pl.multiple_of(start, 16), count)

        for dz1 in (0, 1):
            for dy in (0, 1):
                for dc in (0, 1):
                    pair = (self.z ^ (2 * dz2 + dz1)) * 4 + (self.y ^ dy) * 2 + (self.core ^ dc)
                    base, sem = pair * PAIR_ROWS, self.sems.at[pair]
                    near, far = self.buf(dc, dz2, (dz1, dy, 0)), self.buf(dc, dz2, (dz1, dy, 1))
                    for source, x in ((near, self.x), (far, 1 - self.x)):
                        target = self.weights.at[rows(base + 400 * x, 384)]
                        pltpu.make_async_copy(source.at[rows(16 * x, 384)], target, sem).start()
                    target = self.weights.at[rows(base + 384, 16)]
                    pltpu.make_async_copy(near.at[rows(384 * (1 - self.x), 16)], target, sem).start()

    def start(self):
        self.start_vec()
        for low in (True, False):

            @pl.when((self.z < 2) == low)
            def _(low=low):
                for dz2 in (0, 1) if low else (1, 0):
                    self.start_group(dz2)

    def wait(self, pair):
        if pair not in self.ready:
            self.ready.add(pair)
            rows = self.weights.at[pl.ds(pair * PAIR_ROWS, PAIR_ROWS)]
            pltpu.make_async_copy(rows, rows, self.sems.at[pair]).wait()

    def block(self, number):
        for pair in range(number * D // PAIR_ROWS, (number * D + D - 1) // PAIR_ROWS + 1):
            self.wait(pair)


class Direct:
    def __init__(self, w_hbm, weights, sems, vec_low, vec_sem):
        self.copies = {}
        for number in FIRST_BLOCKS:
            rows = pl.ds(number * D, D)
            self.copies[number] = pltpu.make_async_copy(w_hbm.at[rows], weights.at[rows], sems.at[number])
        self.vec = pltpu.make_async_copy(w_hbm.at[pl.ds(VEC_ROW, 32)], vec_low, vec_sem)
        self.ready = set()

    def start(self):
        self.vec.start()
        for number in FIRST_BLOCKS:
            self.copies[number].start()

    def wait_vec(self):
        self.vec.wait()

    def block(self, number):
        if number not in self.ready:
            self.ready.add(number)
            self.copies[number].wait()


def forward_kernel(queries, custom, left_ref, flags, xb_ref, m_hbm, *refs):
    count = 32 if custom else 1
    bufs, refs = refs[:count], refs[count:]
    qs_out, ks_out, vs_out, os_out, y1_out, qc_out, k_out, v_out, o_out, stat_ref = refs[:10]
    w_out = refs[10] if custom else None
    weights, m_ref, qs_ref, ks_ref, vs_ref, os_ref, y1_ref, qc_ref, k_ref, v_ref, o_ref, vec_low = refs[10 + custom : 22 + custom]
    w_sems, m_sems, out_sems, kv_sems, vec_sem, all_sems = refs[22 + custom :]
    images = m_ref.shape[0]
    tokens = m_ref.shape[1]
    if custom:
        feed = Assembly(flags, bufs, weights, w_sems, vec_low, vec_sem)
    else:
        feed = Direct(bufs[0], weights, w_sems, vec_low, vec_sem)

    def load_memory(image):
        return pltpu.make_async_copy(m_hbm.at[image], m_ref.at[image], m_sems.at[image])

    def matrix(block):
        feed.block(block)
        return weights[block * D : (block + 1) * D, :]

    def leave_weights(half):
        rows = pl.ds(half * 8 * PAIR_ROWS, 8 * PAIR_ROWS)
        return pltpu.make_async_copy(weights.at[rows], w_out.at[rows], all_sems.at[half])

    small = [(qs_ref, qs_out), (ks_ref, ks_out), (vs_ref, vs_out), (os_ref, os_out), (y1_ref, y1_out), (qc_ref, qc_out)]

    def leave(number):
        return pltpu.make_async_copy(*small[number], out_sems.at[number])

    def leave_image(image, number):
        source, target = [(k_ref, k_out), (v_ref, v_out), (o_ref, o_out)][number]
        return pltpu.make_async_copy(source.at[image], target.at[image], kv_sems.at[image, number])

    feed.start()
    for image in range(images):
        load_memory(image).start()
    feed.wait_vec()
    vec = vec_low[...].astype(F32)
    xb = xb_ref[...]
    qs_ref[...] = ((dot_nn(xb, matrix(0)) + vec[0:1, :]) * SCALE).astype(BF16)
    leave(0).start()
    ks_ref[...] = dot_nn(xb, matrix(1)).astype(BF16)
    leave(1).start()
    vs_ref[...] = (dot_nn(xb, matrix(2)) + vec[1:2, :]).astype(BF16)
    leave(2).start()
    masks = head_masks()
    real = lax.broadcasted_iota(jnp.int32, (2 * QP, QP), 1) < queries
    places = [(slice(i * QP, (i + 1) * QP), slice(p * LANES, (p + 1) * LANES)) for i in range(images) for p in range(PAIRS)]

    def raw_self(place):
        return dot_nt(two_heads(qs_ref[place], masks), ks_ref[place])

    following = raw_self(places[0])
    for number, place in enumerate(places):
        scores = following
        if number + 1 < len(places):
            following = raw_self(places[number + 1])
        scores = jnp.where(real, scores, NEG)
        probs = jnp.exp(scores - jnp.max(scores, axis=-1, keepdims=True))
        probs = probs / jnp.sum(probs, axis=-1, keepdims=True)
        os_ref[place] = join_heads(dot_nn(probs.astype(BF16), vs_ref[place])).astype(BF16)
    leave(3).start()
    y1 = xb.astype(F32) + (dot_nn(os_ref[...], matrix(3)) + vec[2:3, :])
    y1_ref[...] = y1
    leave(4).start()
    hat, _ = norm_parts(y1)
    x1 = hat * vec[11:12, :] + vec[12:13, :]
    qc_ref[...] = ((dot_nn(x1.astype(BF16), matrix(4)) + vec[3:4, :]) * SCALE).astype(BF16)
    leave(5).start()

    feed.block(5)
    feed.block(6)
    if custom:
        for pair in range(8):
            feed.wait(pair)
        leave_weights(0).start()
    column = lax.broadcasted_iota(jnp.int32, (2 * QP, 128), 1)
    for image in range(images):
        load_memory(image).wait()
        rows = slice(image * QP, (image + 1) * QP)
        k_ref[image] = dot_nn(m_ref[image], matrix(5)).astype(BF16)
        v_ref[image] = (dot_nn(m_ref[image], matrix(6)) + vec[4:5, :]).astype(BF16)
        leave_image(image, 0).start()
        leave_image(image, 1).start()
        valid = lax.broadcasted_iota(jnp.int32, (2 * QP, tokens), 1) < left_ref[image]
        stat = jnp.zeros((2 * QP, 128), F32)
        def raw(pair):
            lanes = slice(pair * LANES, (pair + 1) * LANES)
            return dot_nt(two_heads(qc_ref[rows, lanes], masks), k_ref[image, :, lanes])

        following = raw(0)
        for pair in range(PAIRS):
            lanes = slice(pair * LANES, (pair + 1) * LANES)
            scores = following
            if pair + 1 < PAIRS:
                following = raw(pair + 1)
            scores = jnp.where(valid, scores, NEG)
            top = jnp.max(scores, axis=-1, keepdims=True)
            probs = jnp.exp(scores - top)
            total = jnp.sum(probs, axis=-1, keepdims=True)
            mixed = dot_nn(probs.astype(BF16), v_ref[image, :, lanes]) / total
            o_ref[image, :, lanes] = join_heads(mixed).astype(BF16)
            stat = jnp.where(column == pair, top + jnp.log(total), stat)
        stat_ref[image] = jnp.where(left_ref[image] > 0, stat.T[:8], NEG)
        leave_image(image, 2).start()
        if custom and image == 0:
            for pair in range(8, 16):
                feed.wait(pair)
            leave_weights(1).start()
    for number in range(len(small)):
        leave(number).wait()
    for image in range(images):
        for number in range(3):
            leave_image(image, number).wait()
    if custom:
        leave_weights(0).wait()
        leave_weights(1).wait()


def forward(left, flags, xb, memory, bufs, queries):
    custom = len(bufs) > 1
    rows = xb.shape[0]
    images, tokens, _ = memory.shape
    narrow = jax.ShapeDtypeStruct((rows, D), BF16)
    tall = jax.ShapeDtypeStruct(memory.shape, BF16)
    anywhere = pl.BlockSpec(memory_space=pl.ANY)
    small = pltpu.VMEM((rows, D), BF16)
    large = pltpu.VMEM(memory.shape, BF16)
    held = 16 * PAIR_ROWS if custom else 7 * D
    return pl.pallas_call(
        partial(forward_kernel, queries, custom),
        grid_spec=pltpu.PrefetchScalarGridSpec(
            num_scalar_prefetch=2,
            grid=(1,),
            in_specs=[whole((rows, D)), anywhere] + [anywhere] * len(bufs),
            out_specs=[anywhere] * 9 + [whole((images, 8, 2 * QP))] + [anywhere] * custom,
            scratch_shapes=[
                pltpu.VMEM((held, D), BF16),
                large, small, small, small, small,
                pltpu.VMEM((rows, D), F32),
                small, large, large,
                pltpu.VMEM((images, QP, D), BF16),
                pltpu.VMEM((32, D), BF16),
                pltpu.SemaphoreType.DMA((16,)),
                pltpu.SemaphoreType.DMA((images,)),
                pltpu.SemaphoreType.DMA((6,)),
                pltpu.SemaphoreType.DMA((images, 3)),
                pltpu.SemaphoreType.DMA(()),
                pltpu.SemaphoreType.DMA((2,)),
            ],
        ),
        out_shape=[
            narrow, narrow, narrow, narrow,
            jax.ShapeDtypeStruct((rows, D), F32),
            narrow, tall, tall,
            jax.ShapeDtypeStruct((images, QP, D), BF16),
            jax.ShapeDtypeStruct((images, 8, 2 * QP), F32),
        ]
        + [jax.ShapeDtypeStruct((held, D), BF16)] * custom,
        cost_estimate=cost(0, 0),
        compiler_params=params(60),
        name="forward",
    )(left, flags, xb, memory, *bufs)


def pieces(start, count, size):
    found = []
    done = 0
    while done < count:
        pair, offset = divmod(start + done, size)
        length = min(count - done, size - offset)
        found.append((done, pair, offset, length))
        done += length
    return found


class Halves:
    def __init__(self, keep, send, my_core):
        self.keep, self.send, self.my_core = keep, send, my_core

    def copy(self, target, source, pair, offset, length, sem):
        place = pair // self.cores()
        index = []
        for extent in reversed(target.shape[:-2]):
            index.insert(0, place % extent)
            place = place // extent
        return pltpu.make_async_copy(source, target.at[(*index, pl.ds(offset, length))], sem)

    def cores(self):
        return 1 if self.send is None else 2

    def start(self, source, pair, offset, length, sem):
        if self.send is None:
            self.copy(self.keep, source, pair, offset, length, sem).start()
            return

        @pl.when(self.my_core == pair % 2)
        def _():
            self.copy(self.keep, source, pair, offset, length, sem).start()

        @pl.when(self.my_core != pair % 2)
        def _():
            self.copy(self.send, source, pair, offset, length, sem).start()

    def wait(self, source, pair, offset, length, sem):
        self.copy(self.keep, source, pair, offset, length, sem).wait()


def middle_kernel(parts, split, *refs):
    flags, y1_ref = refs[:2]
    o_refs, stat_refs = refs[2 : 2 + parts], refs[2 + parts : 2 + 2 * parts]
    refs = refs[2 + 2 * parts :]
    w_hbm, vec, cot_ref, match_ref, out_hbm = refs[:5]
    halves = Halves(refs[5], refs[6] if split else None, flags[0])
    refs = refs[6 + split :]
    cross_halves = Halves(refs[0], refs[1] if split else None, flags[0])
    refs = refs[1 + split :]
    db_ref, doc_ref, tot_ref, dvec_ref = refs[:4]
    ocf, ocb, y2, x2b, u, slope, acc, e3b, staged, blank, out_ref, dco_ref, co, feed = refs[4:18]
    sems, blank_sem, out_sem, side_sems, w_sems = refs[18:]
    phase, step = pl.program_id(0), pl.program_id(1)
    steps = FF // D
    images = match_ref.shape[0]
    column = lax.broadcasted_iota(jnp.int32, (2 * QP, 128), 1)
    lane = lax.broadcasted_iota(jnp.int32, (QP, LANES), 1)
    size = halves.keep.shape[-2]
    side = cross_halves.keep.shape[-2]

    def load(block):
        target = co if block == 7 else feed.at[block - 8]
        return pltpu.make_async_copy(w_hbm.at[pl.ds(block * D, D)], target, w_sems.at[block - 7])

    def leave_out():
        return pltpu.make_async_copy(out_ref, out_hbm, out_sem)

    def leave_side(act):
        starts = [(dco_ref, 3 * D - QUERY_HEAD, D), (staged.at[0, 0], 4 * D - QUERY_HEAD, HEAD_ROWS)]
        for which, (source, start, count) in enumerate(starts):
            if (which == 0) != (act[0] == "o"):
                continue
            for number, (done, pair, offset, length) in enumerate(pieces(start, count, side)):
                piece = source.at[pl.ds(done, length)]
                getattr(cross_halves, act[1])(piece, pair, offset, length, side_sems.at[which, number])

    def leave(which, at, act):
        skip = HEAD_ROWS if which + at == 0 else 0
        start = which * FF + at * D + skip - HEAD_ROWS
        for number, (done, pair, offset, length) in enumerate(pieces(start, D - skip, size)):
            source = staged.at[at % 2, which, pl.ds(done + skip, length)]
            getattr(halves, act)(source, pair, offset, length, sems.at[at, which, number])

    def leave_blank(act):
        for _, pair, offset, length in pieces(2 * FF - HEAD_ROWS, TAIL, size):
            getattr(halves, act)(blank, pair, offset, length, blank_sem)

    def ordered(first, second):
        if parts != 2:
            return first, second
        swap = flags[1] != 0
        return jnp.where(swap, second, first), jnp.where(swap, first, second)

    @pl.when((phase == 0) & (step == 0))
    def _():
        load(7).start()
        for at in range(steps):
            load(8 + at).start()
            load(8 + steps + at).start()
        for image in range(images):
            rows = slice(image * QP, (image + 1) * QP)
            stats = [ref[image] for ref in stat_refs]
            if parts == 2:
                stats = ordered(*stats)
            top = stats[0]
            for n in range(1, parts):
                top = jnp.maximum(top, stats[n])
            mass = [jnp.exp(stats[n] - top) for n in range(parts)]
            total = mass[0]
            for n in range(1, parts):
                total = total + mass[n]
            tot_ref[image, 0:8, :] = top + jnp.log(total)
            shares = [jnp.concatenate([m / total, jnp.zeros((120, 2 * QP), F32)], axis=0).T for m in mass]
            for pair in range(PAIRS):
                lanes = slice(pair * LANES, (pair + 1) * LANES)
                values = [ref[image, :, lanes].astype(F32) for ref in o_refs]
                if parts == 2:
                    values = ordered(*values)
                mixed = jnp.zeros((QP, LANES), F32)
                for n in range(parts):
                    share = shares[n][:, pair : pair + 1]
                    mixed = mixed + values[n] * jnp.where(lane < HEAD, share[:QP], share[QP:])
                ocf[rows, lanes] = mixed
        ocb[...] = ocf[...].astype(BF16)
        hat, _ = norm_parts(y1_ref[...])
        x1 = hat * vec[11:12, :] + vec[12:13, :]
        load(7).wait()
        total = x1 + (dot_nn(ocb[...], co[...]) + vec[5:6, :])
        y2[...] = total
        hat, _ = norm_parts(total)
        x2 = hat * vec[13:14, :] + vec[14:15, :]
        x2b[...] = x2.astype(BF16)
        acc[...] = x2 + vec[6:7, :]

    for at in range(steps):

        @pl.when((phase == 0) & (step == at))
        def _(at=at):
            load(8 + at).wait()
            load(8 + steps + at).wait()

    f1, f2 = feed.at[step], feed.at[steps + step]

    @pl.when(phase == 0)
    def _():
        h = dot_nt(x2b[...], f1[...]) + vec[pl.ds(7 + step, 1), :]
        root = 0.7978845608028654
        square = h * h
        t = jnp.tanh(root * (h + 0.044715 * (h * square)))
        half = 0.5 * (1.0 + t)
        slope[step] = half + (0.5 * root) * h * (1.0 - t * t) * (1.0 + 0.134145 * square)
        active = (h * half).astype(BF16)
        u[step] = active
        acc[...] += dot_nn(active, f2[...])

    @pl.when((phase == 1) & (step == 0))
    def _():
        blank[...] = jnp.zeros_like(blank)
        leave_blank("start")
        dvec_ref[...] = jnp.zeros_like(dvec_ref)
        hat, inverse = norm_parts(acc[...])
        out = hat * vec[15:16, :] + vec[16:17, :]
        grads = []
        for image in range(images):
            out_ref[image] = out[image * QP : (image + 1) * QP]
            matched = match_ref[image]
            hit = lax.broadcasted_iota(jnp.int32, (QP, matched.shape[1]), 0) == matched
            grads.append(dot_nn(jnp.where(hit, 1.0, 0.0).astype(BF16), cot_ref[image]))
        leave_out().start()
        dy = jnp.concatenate(grads, axis=0)
        dvec_ref[15:16, :] = rowsum(dy * hat)
        dvec_ref[16:17, :] = rowsum(dy)
        dc = norm_back(dy, hat, inverse, vec[15:16, :])
        low = dc.astype(BF16)
        e3b[...] = low
        dvec_ref[6:7, :] = rowsum(low)
        acc[...] = dc

    for at in range(2, steps):

        @pl.when((phase == 1) & (step == at))
        def _(at=at):
            leave(0, at - 2, "wait")
            leave(1, at - 2, "wait")
            if at == 2:
                leave_side(("f", "wait"))

    @pl.when(phase == 1)
    def _():
        du = dot_nt(e3b[...], f2[...])
        dh = (du * slope[step]).astype(BF16)
        slot = lax.rem(step, 2)
        staged[slot, 1] = dot_tn(u[step], e3b[...]).astype(BF16)
        staged[slot, 0] = dot_tn(dh, x2b[...]).astype(BF16)

        @pl.when(step == 0)
        def _():
            leave_side(("f", "start"))

        for at in range(steps):

            @pl.when(step == at)
            def _(at=at):
                leave(0, at, "start")
                leave(1, at, "start")

        dvec_ref[pl.ds(7 + step, 1), :] = rowsum(dh)
        acc[...] += dot_nn(dh, f1[...])

    @pl.when((phase == 1) & (step == steps - 1))
    def _():
        hat, inverse = norm_parts(y2[...])
        dy = acc[...]
        dvec_ref[13:14, :] = rowsum(dy * hat)
        dvec_ref[14:15, :] = rowsum(dy)
        db = norm_back(dy, hat, inverse, vec[13:14, :])
        db_ref[...] = db
        low = db.astype(BF16)
        dvec_ref[5:6, :] = rowsum(low)
        dco_ref[...] = dot_tn(ocb[...], low).astype(BF16)
        leave_side(("o", "start"))
        doc = dot_nt(low, co[...]).astype(BF16)
        doc_ref[...] = doc
        both = doc.astype(F32) * ocf[...]
        for image in range(images):
            rows = slice(image * QP, (image + 1) * QP)
            tot = jnp.zeros((2 * QP, 128), F32)
            for pair in range(PAIRS):
                piece = both[rows, pair * LANES : (pair + 1) * LANES]
                one = jnp.sum(jnp.where(lane < HEAD, piece, 0.0), axis=-1, keepdims=True)
                two = jnp.sum(jnp.where(lane < HEAD, 0.0, piece), axis=-1, keepdims=True)
                tot = jnp.where(column == pair, jnp.concatenate([one, two], axis=0), tot)
            tot_ref[image, 8:16, :] = tot.T[:8]
        leave_blank("wait")
        leave_out().wait()
        leave_side(("o", "wait"))
        for which in (0, 1):
            leave(which, steps - 2, "wait")
            leave(which, steps - 1, "wait")


def halves_shape(shape, split):
    return [jax.ShapeDtypeStruct(shape, BF16)] * (1 + split)


def middle(flags, y1, o_parts, stat_parts, w, vec, cot, matched, far_shape, cross_shape, split):
    rows = y1.shape[0]
    images = cot.shape[0]
    steps = FF // D
    parts = len(o_parts)
    anywhere = pl.BlockSpec(memory_space=pl.ANY)
    return pl.pallas_call(
        partial(middle_kernel, parts, split),
        grid_spec=pltpu.PrefetchScalarGridSpec(
            num_scalar_prefetch=1,
            grid=(2, steps),
            in_specs=[whole(y1.shape)]
            + [whole(o_parts[0].shape)] * parts
            + [whole(stat_parts[0].shape)] * parts
            + [anywhere, whole((VECS, D)), whole(cot.shape), whole((images, 1, matched.shape[1]))],
            out_specs=[anywhere] * (3 + 2 * split)
            + [
                whole((rows, D)),
                whole((rows, D)),
                whole((images, 16, 2 * QP)),
                whole((VECS, D)),
            ],
            scratch_shapes=[
                pltpu.VMEM((rows, D), F32),
                pltpu.VMEM((rows, D), BF16),
                pltpu.VMEM((rows, D), F32),
                pltpu.VMEM((rows, D), BF16),
                pltpu.VMEM((steps, rows, D), BF16),
                pltpu.VMEM((steps, rows, D), F32),
                pltpu.VMEM((rows, D), F32),
                pltpu.VMEM((rows, D), BF16),
                pltpu.VMEM((2, 2, D, D), BF16),
                pltpu.VMEM((TAIL, D), BF16),
                pltpu.VMEM((images, QP, D), F32),
                pltpu.VMEM((D, D), BF16),
                pltpu.VMEM((D, D), BF16),
                pltpu.VMEM((2 * steps, D, D), BF16),
                pltpu.SemaphoreType.DMA((steps, 2, 2)),
                pltpu.SemaphoreType.DMA(()),
                pltpu.SemaphoreType.DMA(()),
                pltpu.SemaphoreType.DMA((2, 2)),
                pltpu.SemaphoreType.DMA((1 + 2 * steps,)),
            ],
        ),
        out_shape=[jax.ShapeDtypeStruct((images, QP, D), F32)]
        + halves_shape(far_shape, split)
        + halves_shape(cross_shape, split)
        + [
            jax.ShapeDtypeStruct((rows, D), F32),
            jax.ShapeDtypeStruct((rows, D), BF16),
            jax.ShapeDtypeStruct((images, 16, 2 * QP), F32),
            jax.ShapeDtypeStruct((VECS, D), F32),
        ],
        cost_estimate=cost(2 * rows * D * (6 * FF + 3 * D), 2 * FF * D * 6),
        compiler_params=params(60),
        name="middle",
    )(flags, y1, *o_parts, *stat_parts, w, vec, cot, matched[:, None, :])


def cross_backward_kernel(left_ref, q_ref, k_ref, v_ref, do_ref, tot_ref, dq_ref, dk_ref, dv_ref):
    tokens = k_ref.shape[1]
    masks = head_masks()
    valid = lax.broadcasted_iota(jnp.int32, (tokens, 2 * QP), 0) < left_ref[pl.program_id(0)]
    def raw(pair):
        lanes = slice(pair * LANES, (pair + 1) * LANES)
        query = two_heads(q_ref[0, :, lanes], masks)
        dout = two_heads(do_ref[0, :, lanes], masks)
        return query, dout, dot_nt(k_ref[0, :, lanes], query), dot_nt(v_ref[0, :, lanes], dout)

    following = raw(0)
    for pair in range(PAIRS):
        lanes = slice(pair * LANES, (pair + 1) * LANES)
        query, dout, scores, dprobs = following
        if pair + 1 < PAIRS:
            following = raw(pair + 1)
        probs = jnp.where(valid, jnp.exp(scores - tot_ref[0, pair : pair + 1, :]), 0.0)
        dscores = (probs * (dprobs - tot_ref[0, 8 + pair : 9 + pair, :])).astype(BF16)
        dv_ref[0, :, lanes] = dot_nn(probs.astype(BF16), dout).astype(BF16)
        dk_ref[0, :, lanes] = dot_nn(dscores, query).astype(BF16)
        dq_ref[0, :, lanes] = join_heads(dot_tn(k_ref[0, :, lanes], dscores).T).astype(BF16)


def cross_backward(left, qc, key, value, doc, tot):
    images, tokens, _ = key.shape
    q_block = pl.BlockSpec((1, QP, D), lambda i, _: (i, 0, 0))
    m_block = pl.BlockSpec((1, tokens, D), lambda i, _: (i, 0, 0))
    s_block = pl.BlockSpec((1, 16, 2 * QP), lambda i, _: (i, 0, 0))
    return pl.pallas_call(
        cross_backward_kernel,
        grid_spec=pltpu.PrefetchScalarGridSpec(
            num_scalar_prefetch=1,
            grid=(images,),
            in_specs=[q_block, m_block, m_block, q_block, s_block],
            out_specs=[q_block, m_block, m_block],
        ),
        out_shape=[
            jax.ShapeDtypeStruct((images, QP, D), BF16),
            jax.ShapeDtypeStruct(key.shape, BF16),
            jax.ShapeDtypeStruct(key.shape, BF16),
        ],
        cost_estimate=cost(4 * images * 2 * QP * tokens * D // 3, images * tokens * D * 8),
        compiler_params=params(60),
        name="cross_backward",
    )(left, qc.reshape(images, QP, D), key, value, doc.reshape(images, QP, D), tot)


def memory_weights_kernel(split, flags, *refs):
    m_ref, dk_ref, dv_ref = refs[1 + split : 4 + split]
    refs = refs[4 + split :]
    gb_ref = refs[0]
    halves = Halves(refs[1], refs[2] if split else None, flags[0])
    sums, low, sems = refs[2 + split :]
    step = pl.program_id(0)
    dv = dv_ref[0]
    more = [dot_tn(m_ref[0], dk_ref[0]), dot_tn(m_ref[0], dv)]

    @pl.when(step == 0)
    def _():
        for which in (0, 1):
            sums[which] = more[which]
        gb_ref[...] = jnp.broadcast_to(rowsum(dv), gb_ref.shape)

    @pl.when(step > 0)
    def _():
        for which in (0, 1):
            sums[which] += more[which]
        gb_ref[...] += jnp.broadcast_to(rowsum(dv), gb_ref.shape)

    def leave(which, act):
        start = (1 + which) * D - QUERY_HEAD
        for number, (done, pair, offset, length) in enumerate(pieces(start, D, halves.keep.shape[-2])):
            piece = low.at[which, pl.ds(done, length)]
            getattr(halves, act)(piece, pair, offset, length, sems.at[which, number])

    @pl.when(step == pl.num_programs(0) - 1)
    def _():
        for which in (0, 1):
            low[which] = sums[which].astype(BF16)
            leave(which, "start")
        for which in (0, 1):
            leave(which, "wait")


def memory_weights(flags, cross, memory, dk, dv, split):
    images, tokens, _ = memory.shape
    block = pl.BlockSpec((1, tokens, D), lambda i, _: (i, 0, 0))
    anywhere = pl.BlockSpec(memory_space=pl.ANY)
    return pl.pallas_call(
        partial(memory_weights_kernel, split),
        grid_spec=pltpu.PrefetchScalarGridSpec(
            num_scalar_prefetch=1,
            grid=(images,),
            in_specs=[anywhere] * (1 + split) + [block, block, block],
            out_specs=[whole((8, D))] + [anywhere] * (1 + split),
            scratch_shapes=[
                pltpu.VMEM((2, D, D), F32),
                pltpu.VMEM((2, D, D), BF16),
                pltpu.SemaphoreType.DMA((2, 2)),
            ],
        ),
        out_shape=[jax.ShapeDtypeStruct((8, D), F32)] + halves_shape(cross[0].shape, split),
        input_output_aliases={1 + n: 1 + n for n in range(1 + split)},
        cost_estimate=cost(4 * images * tokens * D * D, images * tokens * D * 6),
        compiler_params=params(60),
        name="memory_weights",
    )(flags, *cross, memory, dk, dv)


def memory_grads_kernel(dk_ref, dv_ref, ck, cv, gm_ref):
    gm_ref[0] = dot_nt(dk_ref[0], ck[...]) + dot_nt(dv_ref[0], cv[...])


def memory_grads(dk, dv, w):
    images, tokens, _ = dk.shape
    block = pl.BlockSpec((1, tokens, D), lambda i: (i, 0, 0))
    return pl.pallas_call(
        memory_grads_kernel,
        grid=(images,),
        in_specs=[block, block, weight_block(5), weight_block(6)],
        out_specs=block,
        out_shape=jax.ShapeDtypeStruct(dk.shape, F32),
        cost_estimate=pl.CostEstimate(
            flops=4 * images * tokens * D * D, bytes_accessed=images * tokens * D * 8, transcendentals=0
        ),
        compiler_params=params(60),
        name="memory_grads",
    )(dk, dv, w, w)


class Loads:
    def __init__(self, pairs, sems):
        self.copies = [(pltpu.make_async_copy(source, target, sems.at[n]), target) for n, (source, target) in enumerate(pairs)]
        self.ready = set()
        for copy, _ in self.copies:
            copy.start()

    def __call__(self, number):
        copy, target = self.copies[number]
        if number not in self.ready:
            copy.wait()
            self.ready.add(number)
        return target[...]


def query_backward_kernel(parts, split, flags, *refs):
    sources, vec = refs[1 + split : 4 + split + parts], refs[4 + split + parts]
    refs = refs[5 + split + parts :]
    da_ref, gq_head_ref, dvec_ref = refs[:3]
    halves = Halves(refs[3], refs[4] if split else None, flags[0])
    refs = refs[4 + split :]
    targets, staged, load_sems, sems = refs[: 3 + parts], refs[3 + parts], refs[4 + parts], refs[5 + parts]
    w_hbm = sources[-1]
    sources = [*sources[:-1], w_hbm.at[pl.ds(4 * D, D)]]
    get = Loads(list(zip(sources, targets)), load_sems)

    def leave(act):
        for number, (done, pair, offset, length) in enumerate(pieces(0, D - QUERY_HEAD, halves.keep.shape[-2])):
            piece = staged.at[pl.ds(done + QUERY_HEAD, length)]
            getattr(halves, act)(piece, pair, offset, length, sems.at[number])

    total = get(0).astype(F32)
    for number in range(1, parts):
        total = total + get(number).astype(F32)
    dq = total.astype(BF16) * SCALE
    hat, inverse = norm_parts(get(parts))
    gain = vec[11:12, :]
    x1b = (hat * gain + vec[12:13, :]).astype(BF16)
    gcq = dot_tn(x1b, dq).astype(BF16)
    staged[...] = gcq
    leave("start")
    gq_head_ref[...] = gcq[:QUERY_HEAD]
    dvec_ref[...] = jnp.zeros_like(dvec_ref)
    dvec_ref[3:4, :] = rowsum(dq)
    dy = get(parts + 1) + dot_nt(dq, get(parts + 2))
    dvec_ref[11:12, :] = rowsum(dy * hat)
    dvec_ref[12:13, :] = rowsum(dy)
    da = norm_back(dy, hat, inverse, gain)
    da_ref[...] = da
    dvec_ref[2:3, :] = rowsum(da.astype(BF16))
    leave("wait")


def query_backward(flags, cross, y1, db, dq_parts, w, vec, split):
    rows = y1.shape[0]
    parts = len(dq_parts)
    full = whole((rows, D))
    anywhere = pl.BlockSpec(memory_space=pl.ANY)
    return pl.pallas_call(
        partial(query_backward_kernel, parts, split),
        grid_spec=pltpu.PrefetchScalarGridSpec(
            num_scalar_prefetch=1,
            grid=(1,),
            in_specs=[anywhere] * (4 + split + parts) + [whole((VECS, D))],
            out_specs=[full, whole((QUERY_HEAD, D)), whole((VECS, D))] + [anywhere] * (1 + split),
            scratch_shapes=[pltpu.VMEM((rows, D), BF16)] * parts
            + [pltpu.VMEM((rows, D), F32)] * 2
            + [pltpu.VMEM((D, D), BF16)] * 2
            + [pltpu.SemaphoreType.DMA((parts + 3,)), pltpu.SemaphoreType.DMA((2,))],
        ),
        out_shape=[
            jax.ShapeDtypeStruct((rows, D), F32),
            jax.ShapeDtypeStruct((QUERY_HEAD, D), BF16),
            jax.ShapeDtypeStruct((VECS, D), F32),
        ]
        + halves_shape(cross[0].shape, split),
        input_output_aliases={1 + n: 3 + n for n in range(1 + split)},
        cost_estimate=cost(4 * rows * D * D, rows * D * 16),
        compiler_params=params(60),
        name="query_backward",
    )(flags, *cross, *[part.reshape(rows, D) for part in dq_parts], y1, db, w, vec)


def self_backward_kernel(queries, split, *refs):
    flags, os_hbm, da_hbm, qs_hbm, ks_hbm, vs_hbm, x_hbm, w_hbm, gq_ref, gx_ref, dvec_ref, keep_ref = refs[:12]
    halves = Halves(keep_ref, refs[12] if split else None, flags[0])
    sq, sk, sv, g_ref, os_ref, da_ref, ao, qs, ks, vs, x_ref, aq, ak, av, sems, load_sems = refs[12 + split :]
    size = keep_ref.shape[-2]
    matrices = [w_hbm.at[pl.ds(block * D, D)] for block in range(4)]
    get = Loads(
        [(os_hbm, os_ref), (da_hbm, da_ref), (matrices[3], ao), (qs_hbm, qs), (ks_hbm, ks), (vs_hbm, vs)]
        + [(x_hbm, x_ref), (matrices[0], aq), (matrices[1], ak), (matrices[2], av)],
        load_sems,
    )

    def leave(pair, act):
        getattr(halves, act)(g_ref.at[pl.ds(pair * size, size)], pair, 0, size, sems.at[pair])

    pairs = g_ref.shape[0] // size
    images = x_ref.shape[0] // QP
    dvec_ref[...] = jnp.zeros_like(dvec_ref)
    os = get(0)
    da = get(1)
    low = da.astype(BF16)
    g_ref[4 * D :, :] = gq_ref[...]
    g_ref[3 * D : 4 * D, :] = dot_tn(os, low).astype(BF16)
    dos = dot_nt(low, get(2)).astype(BF16)
    for number in (3, 4, 5):
        get(number)
    masks = head_masks()
    real = lax.broadcasted_iota(jnp.int32, (QP, 2 * QP), 0) < queries
    places = [(slice(i * QP, (i + 1) * QP), slice(p * LANES, (p + 1) * LANES)) for i in range(images) for p in range(PAIRS)]

    def raw(place):
        query = two_heads(qs[place], masks)
        dout = two_heads(dos[place], masks)
        return query, dout, dot_nt(ks[place], query), dot_nt(vs[place], dout)

    following = raw(places[0])
    for number, place in enumerate(places):
        query, dout, scores, dprobs = following
        if number + 1 < len(places):
            following = raw(places[number + 1])
        scores = jnp.where(real, scores, NEG)
        probs = jnp.exp(scores - jnp.max(scores, axis=0, keepdims=True))
        probs = probs / jnp.sum(probs, axis=0, keepdims=True)
        dscores = (probs * (dprobs - jnp.sum(probs * dprobs, axis=0, keepdims=True))).astype(BF16)
        sv[place] = dot_nn(probs.astype(BF16), dout).astype(BF16)
        sk[place] = dot_nn(dscores, query).astype(BF16)
        sq[place] = join_heads(dot_tn(ks[place], dscores).T).astype(BF16) * SCALE
    dvec_ref[0:1, :] = rowsum(sq[...])
    dvec_ref[1:2, :] = rowsum(sv[...])
    xb = get(6)
    g_ref[2 * D : 3 * D, :] = dot_tn(xb, sv[...]).astype(BF16)
    for pair in range(2, pairs):
        leave(pair, "start")
    g_ref[D : 2 * D, :] = dot_tn(xb, sk[...]).astype(BF16)
    for pair in range(1, min(2, pairs)):
        leave(pair, "start")
    g_ref[0:D, :] = dot_tn(xb, sq[...]).astype(BF16)
    leave(0, "start")
    gx = da + dot_nt(sq[...], get(7)) + dot_nt(sk[...], get(8)) + dot_nt(sv[...], get(9))
    for image in range(images):
        gx_ref[image] = gx[image * QP : (image + 1) * QP]
    for pair in range(pairs):
        leave(pair, "wait")


def self_backward(flags, xb, qs, ks, vs, os, da, gq_head, w, queries, shape, split):
    rows = xb.shape[0]
    images = rows // QP
    anywhere = pl.BlockSpec(memory_space=pl.ANY)
    return pl.pallas_call(
        partial(self_backward_kernel, queries, split),
        grid_spec=pltpu.PrefetchScalarGridSpec(
            num_scalar_prefetch=1,
            grid=(1,),
            in_specs=[anywhere] * 7 + [whole((QUERY_HEAD, D))],
            out_specs=[whole((images, QP, D)), whole((VECS, D))] + [anywhere] * (1 + split),
            scratch_shapes=[pltpu.VMEM((rows, D), BF16)] * 3
            + [pltpu.VMEM((4 * D + QUERY_HEAD, D), BF16), pltpu.VMEM((rows, D), BF16), pltpu.VMEM((rows, D), F32)]
            + [pltpu.VMEM((D, D), BF16)]
            + [pltpu.VMEM((rows, D), BF16)] * 4
            + [pltpu.VMEM((D, D), BF16)] * 3
            + [pltpu.SemaphoreType.DMA((4,)), pltpu.SemaphoreType.DMA((10,))],
        ),
        out_shape=[
            jax.ShapeDtypeStruct((images, QP, D), F32),
            jax.ShapeDtypeStruct((VECS, D), F32),
        ]
        + halves_shape(shape, split),
        cost_estimate=cost(16 * rows * D * D * 2, 8 * D * D * 2),
        compiler_params=params(60),
        name="self_backward",
    )(flags, os, da, qs, ks, vs, xb, w, gq_head)


class Place:
    def __init__(self):
        place = lax.axis_index("dp")
        self.x = lax.axis_index("seq")
        self.c = lax.rem(place, 2)
        self.y = lax.rem(place // 2, 2)
        self.z = place // 4


def pick(array, index, axis):
    return lax.dynamic_index_in_dim(array, index, axis, keepdims=False)


def over_core(v):
    return lax.ppermute(v, "dp", [(i, i ^ 1) for i in range(16)])


def over_y(v):
    return lax.ppermute(v, "dp", [(i, i ^ 2) for i in range(16)])


def over_x(v):
    return lax.ppermute(v, "seq", [(0, 1), (1, 0)])


def over_z(v, hops):
    return lax.ppermute(v, "dp", [(4 * a + i, 4 * b + i) for a, b in hops for i in range(4)])


def over_far(v):
    return over_z(v, [(0, 2), (2, 0), (1, 3), (3, 1)])


def over_near(v):
    return over_z(v, SWAP_ONE)


def spread(own):
    x, y, z = over_x(own), over_y(own), over_near(own)
    xy, yz, zx = over_x(y), over_y(z), over_near(x)
    return own, x, y, z, xy, yz, zx


def gather(at, rows):
    low = at.x == 0
    edge = over_x(jnp.where(low, rows[-8:], rows[:8]))
    own = jnp.where(low, jnp.concatenate([rows, edge]), jnp.concatenate([edge, rows]))
    other = over_far(own)
    here, there = spread(own), spread(other)
    found = [*here, over_x(here[5]), *there, over_y(there[6])]
    return found + [over_core(part) for part in found]


def tie(*values):
    return lax.optimization_barrier(values)


def add(kept, came):
    return (kept.astype(F32) + came.astype(F32)).astype(BF16)


def own_half(pairs, x):
    half = pairs.shape[-2] // 2
    return pick(pairs.reshape(*pairs.shape[:-2], 2, half, D), x, pairs.ndim - 2)


def blocks_of(pairs):
    return pairs.reshape(*pairs.shape[:-2], 2, pairs.shape[-2] // 2, D)


def picked(pairs, half, x):
    return pick(pick(pairs, half, 0), x, 0)


def merge(body, flags, sources, out_rows, name):
    parts = 3
    specs = []
    for array, where in sources:
        lead = (None,) * (array.ndim - 2)
        shape = (*lead, array.shape[-2], D // parts)
        specs.append(pl.BlockSpec(shape, lambda i, f, where=where: (*where(f), 0, i)))
    return pl.pallas_call(
        body,
        grid_spec=pltpu.PrefetchScalarGridSpec(
            num_scalar_prefetch=1,
            grid=(parts,),
            in_specs=specs,
            out_specs=[
                pl.BlockSpec((*rows, D // parts), lambda i, f, n=len(rows): (*[0] * n, i)) for rows in out_rows
            ],
        ),
        out_shape=[jax.ShapeDtypeStruct((*rows, D), BF16) for rows in out_rows],
        cost_estimate=cost(0, 0),
        compiler_params=params(60),
        name=name,
    )(flags, *[array for array, _ in sources])


def far_send_kernel(flags, a, b, c, d, out):
    out[0] = add(a[...], b[...])
    out[1] = add(c[...], d[...])


def far_send(flags, kept, came):
    kept, came = blocks_of(kept), blocks_of(came)
    sources = []
    for r in (0, 1):
        sources += [(part, lambda f, r=r: (r, 1 - f[2], f[1])) for part in (kept, came)]
    return merge(far_send_kernel, flags, sources, [(2, kept.shape[-2])], "far_send")[0]


def core_merge_kernel(flags, *refs):
    ins, outs = refs[:14], refs[14:]
    for number in range(2):
        first, second, third = ins[3 * number : 3 * number + 3]
        outs[number][...] = (first[...].astype(F32) + second[...].astype(F32) + third[...].astype(F32)).astype(BF16)
    outs[2][...] = add(ins[6][...], ins[7][...])
    outs[3][...] = add(ins[8][...], ins[9][...])
    message = outs[4]
    block = ins[10].shape[0]
    message[:block, :] = add(ins[10][...], ins[11][...])
    spill = message.shape[0] - (block + 8)
    total = ins[12][...].astype(F32) + ins[13][...].astype(F32)
    message[block:, :] = jnp.concatenate([jnp.zeros((8, total.shape[1]), F32), total[block - spill :]]).astype(BF16)


def core_merge(flags, far, far_came, far_last, cross, cross_came):
    far, far_came, cross, cross_came = [blocks_of(v) for v in (far, far_came, cross, cross_came)]
    block = cross.shape[-2]
    spill = 2 * block - (D - QUERY_HEAD)
    sources = []
    for r in (lambda f: 1 - f[3] % 2, lambda f: f[3] % 2):
        sources += [(part, lambda f, r=r: (r(f), f[2], f[1])) for part in (far, far_came)]
        sources += [(far_last, lambda f, r=r: (r(f),))]
    chosen = [
        lambda f: (0, f[1]),
        lambda f: (1, f[1]),
        lambda f: (1 - f[0], 1 - f[1]),
        lambda f: (0, 1 - f[1]),
    ]
    for where in chosen:
        sources += [(cross, where), (cross_came, where)]
    return merge(core_merge_kernel, flags, sources, [(block,)] * 4 + [(block + 8 + spill,)], "core_merge")


def cross_second(at, mine, came):
    start = D - QUERY_HEAD
    block = mine[0].shape[-2]
    spill = 2 * block - start
    main = came[:block].astype(F32)
    tall = jnp.concatenate([jnp.zeros((block - spill, D), F32), came[block + 8 :].astype(F32)])
    ids = (at.c * 2 + at.x) * block + jnp.arange(block)[:, None]

    def half(index, y):
        part = jnp.where((at.c == 0) & (y == 0), tall, main)
        place = ids + y * 4 * block
        shared = (place >= start) & (place < start + 2 * D)
        own = jnp.where(index == 0, mine[0], mine[1]).astype(F32)
        return (own + jnp.where(shared, part, 0.0)).astype(BF16)

    return half(1 - at.y, 1 - at.y), half(at.y, at.y)


SWAP_ONE = [(0, 1), (1, 0), (2, 3), (3, 2)]
SWAP_TWO = [(0, 2), (2, 0), (1, 3), (3, 1)]


def finish(at, flags, block, far, far_last, near, near_send, cross, cross_came, vec_rows, extra):
    near_came = over_core(near_send)
    vec_came = over_core(vec_rows)
    far_out, far, low, high, message = core_merge(flags, *far, far_last, cross, cross_came)
    near_came, message, far_out, low, high, far = tie(near_came, message, far_out, low, high, far)
    came, far_came = over_x(message), over_z(far_out, SWAP_ONE)
    near, near_came = blocks_of(near), blocks_of(near_came)
    near_send = add(picked(near, 1 - at.y, at.x), picked(near_came, 1 - at.y, at.x))
    near = add(picked(near, at.y, at.x), picked(near_came, at.y, at.x))
    vec_rows = vec_rows + vec_came
    near_send, near, vec_rows, dk, dv, w = tie(near_send, near, vec_rows, *extra)
    near_came, vec_came = over_y(near_send), over_y(vec_rows)
    gm = memory_grads(dk, dv, w)
    gm, came = tie(gm, came)
    send, cross = cross_second(at, (low, high), came)
    send, near_came, far_came, cross = tie(send, near_came, far_came, cross)

    near = add(near, near_came)
    far = add(far, far_came)
    vec_rows = vec_rows + vec_came
    near, far, vec_rows, send = tie(near, far, vec_rows, send)
    cross_came, near_came = over_y(send), over_z(near, [(3, 2), (1, 0)])
    cut = block // 16 * 8
    far_top, vec_came = over_z(far[:cut], [(0, 2), (1, 3)]), over_z(vec_rows, SWAP_ONE)
    cross = add(cross, cross_came)
    near = add(near, near_came)
    vec_rows = vec_rows + vec_came
    near, cross, vec_rows, far_top, far = tie(near, cross, vec_rows, far_top, far)

    cross_came, near_came = over_z(cross, [(3, 2), (0, 1)]), over_z(near, [(2, 0)])
    far_low, vec_came = over_z(far[cut:], [(0, 2), (1, 3)]), over_z(vec_rows, SWAP_TWO)
    cross = add(cross, cross_came)
    vec_rows = vec_rows + vec_came
    near_came, cross, vec_rows, far_low = tie(near_came, cross, vec_rows, far_low)

    cross_came = over_z(cross, [(2, 1)])
    far_came = jnp.concatenate([far_top, far_low])
    kept = jnp.where(at.z >= 2, far, jnp.where(at.z == 0, near, cross))
    came = jnp.where(at.z >= 2, far_came, jnp.where(at.z == 0, near_came, cross_came))
    grad_rows = kept.astype(F32) + came.astype(F32)
    start = VEC_ROW - 31 * block
    last = jnp.concatenate([grad_rows[:start], vec_rows, jnp.zeros((block - start - VECS, D), F32)])
    is_last = (lax.axis_index("dp") == 15) & (at.x == 1)
    return jnp.where(is_last, last, grad_rows), gm


def shards(custom, inputs, memory, lengths, matched, cotangent, weights):
    axes = ("dp", "seq")
    share = 1.0 / lax.axis_size("seq")
    images, queries, _ = inputs.shape
    tokens = memory.shape[1]
    block = weights.shape[1]
    at = Place()
    left = lengths - at.x * tokens
    flags = jnp.stack([at.c if custom else 0, at.x, at.y, at.z]).astype(jnp.int32)

    def parts_of(value):
        if custom:
            return [value, over_x(value)]
        gathered = lax.all_gather(value, "seq")
        return [gathered[n] for n in range(gathered.shape[0])]

    if custom:
        bufs = gather(at, weights[0])
    else:
        bufs = [lax.all_gather(weights[0], axes, axis=0, tiled=True)]
    xb = jnp.pad(inputs, ((0, 0), (0, QP - queries), (0, 0))).reshape(images * QP, D)
    qs, ks, vs, os, y1, qc, key, value, mixed, stat, *w = forward(left, flags, xb, memory, bufs, queries)
    w = w[0] if custom else bufs[0]
    vec = w[VEC_ROW : VEC_ROW + VECS].astype(F32)
    near_rows = 4 * D + QUERY_HEAD
    far_rows = 2 * FF - HEAD_ROWS + TAIL
    cross_rows = 4 * D - QUERY_HEAD + HEAD_ROWS
    far_shape = (2, 2, 2 * block, D) if custom else (far_rows, D)
    near_shape = (2, 2 * block, D) if custom else (near_rows, D)
    cross_shape = (2, 2 * block, D) if custom else (cross_rows, D)
    out, *grads, db, doc, tot, dvec_mid = middle(
        flags, y1, parts_of(mixed), parts_of(stat), w, vec, cotangent, matched, far_shape, cross_shape, custom
    )
    far, cross = grads[: 1 + custom], grads[1 + custom :]
    if custom:
        far_came = over_core(far[1])
    dq, dk, dv = cross_backward(left, qc, key, value, doc, tot)
    dq_parts = parts_of(dq)
    if custom:
        far = [far[0], far_came]
        dk, message = tie(dk, far_send(flags, *far))
        far_last = over_y(message)
    dcv_row, *cross = memory_weights(flags, cross, memory, dk, dv, custom)
    if custom:
        dcv_row = dcv_row + over_x(dcv_row)
    da, gq_head, dvec_query, *cross = query_backward(flags, cross, y1, db, dq_parts, w, vec, custom)
    if custom:
        cross_came = over_core(cross[1])
    gq_head, dcv_row = tie(gq_head, dcv_row)
    gx, dvec_self, *near = self_backward(
        flags, xb, qs, ks, vs, os, da, gq_head, w, queries, near_shape, custom
    )
    vec_rows = (dvec_mid + dvec_query + dvec_self) * (1.0 if custom else share)
    is_value_bias = jnp.arange(VECS)[:, None] == 4
    vec_rows = jnp.where(is_value_bias, dcv_row[0:1], vec_rows)
    if custom:
        far_last, near_send = tie(far_last, near[1])
        grad_rows, gm = finish(
            at, flags, block, far, far_last, near[0], near_send, cross[0], cross_came, vec_rows, (dk, dv, w)
        )
    else:
        gm = memory_grads(dk, dv, w)
        low_share = jnp.asarray(share, BF16)
        pad = lax.axis_size(axes) * block - VEC_ROW - VECS
        last = 2 * FF - HEAD_ROWS
        memory_rows = slice(D - QUERY_HEAD, 3 * D - QUERY_HEAD)
        grads = jnp.concatenate(
            [near[0] * low_share, cross[0][: memory_rows.start] * low_share, cross[0][memory_rows]]
            + [cross[0][memory_rows.stop :] * low_share, far[0][:last] * low_share]
            + [vec_rows.astype(BF16), jnp.zeros((pad, D), BF16)]
        )
        grad_rows = lax.psum_scatter(grads, axes, scatter_dimension=0, tiled=True).astype(F32)
    return out[:, :queries], gx[:, :queries], gm, grad_rows[None]


def solution(mesh):
    placed = (
        P("dp", None, None),
        P("dp", "seq", None),
        P("dp"),
        P("dp", None),
        P("dp", None, None),
        P(None, ("dp", "seq"), None),
    )
    custom = dict(mesh.shape) == {"dp": 16, "seq": 2}
    return jax.shard_map(
        partial(shards, custom),
        mesh=mesh,
        in_specs=placed,
        out_specs=(
            P("dp", None, None),
            P("dp", None, None),
            P("dp", "seq", None),
            P(None, ("dp", "seq"), None),
        ),
        check_vma=False,
    )
```

```python
from functools import partial

import jax
import jax.numpy as jnp
from jax import lax
from jax.experimental import pallas as pl
from jax.experimental.pallas import tpu as pltpu
from jax.sharding import PartitionSpec as P

D = 768
H = 12
HEAD = 64
FF = 3072
PAIRS = H // 2
LANES = 2 * HEAD
QP = 112
VEC_ROW = 8 * D + 2 * FF
VECS = 24
TAIL = 256
HEAD_ROWS = 128
QUERY_HEAD = 64
SCALE = HEAD ** (-0.5)
EPS = 1e-05
NEG = -1e30
F32 = jnp.float32
BF16 = jnp.bfloat16
MIB = 1024 * 1024


def dot_nn(a, b):
    return lax.dot_general(a, b, (((1,), (0,)), ((), ())), preferred_element_type=F32)


def dot_nt(a, b):
    return lax.dot_general(a, b, (((1,), (1,)), ((), ())), preferred_element_type=F32)


def dot_tn(a, b):
    return lax.dot_general(a, b, (((0,), (0,)), ((), ())), preferred_element_type=F32)


def norm_parts(v):
    center = v - jnp.mean(v, axis=-1, keepdims=True)
    inverse = lax.rsqrt(jnp.mean(center * center, axis=-1, keepdims=True) + EPS)
    return center * inverse, inverse


def norm_back(dy, hat, inverse, gain):
    scaled = dy * gain
    mean_one = jnp.mean(scaled, axis=-1, keepdims=True)
    mean_two = jnp.mean(scaled * hat, axis=-1, keepdims=True)
    return inverse * (scaled - mean_one - hat * mean_two)


def rowsum(v):
    return jnp.sum(v.astype(F32), axis=0, keepdims=True)


def head_masks():
    lane = lax.broadcasted_iota(jnp.int32, (1, LANES), 1)
    first = jnp.where(lane < HEAD, 1.0, 0.0)
    return first.astype(BF16), (1.0 - first).astype(BF16)


def two_heads(block, masks):
    return jnp.concatenate([block * masks[0], block * masks[1]], axis=0)


def join_heads(stacked):
    lane = lax.broadcasted_iota(jnp.int32, (QP, LANES), 1)
    return jnp.where(lane < HEAD, stacked[:QP], stacked[QP:])


def weight_block(index):
    return pl.BlockSpec((D, D), lambda *_: (index, 0))


def whole(shape):
    return pl.BlockSpec(shape, lambda *_: (0,) * len(shape))


def params(mib):
    return pltpu.CompilerParams(vmem_limit_bytes=mib * MIB)


def cost(flops, moved):
    return pl.CostEstimate(flops=flops // 1000, bytes_accessed=moved // 1000, transcendentals=0)


FIRST_BLOCKS = (0, 1, 2, 5, 6, 3, 4)
SPREAD = ((0, 0, 0), (0, 0, 1), (0, 1, 0), (1, 0, 0), (0, 1, 1), (1, 1, 0), (1, 0, 1), (1, 1, 1))
PAIR_ROWS = 784
HOLDER = (3, 1, 1, 1)


class Assembly:
    def __init__(self, flags, bufs, weights, seams, sems, vec_low, vec_sem):
        self.core, self.x, self.y, self.z = flags[0], flags[1], flags[2], flags[3]
        self.bufs, self.weights, self.seams, self.sems = bufs, weights, seams, sems
        self.vec_low, self.vec_sem = vec_low, vec_sem
        self.ready = set()

    def buf(self, dc, dz2, spread):
        return self.bufs[dc * 16 + dz2 * 8 + SPREAD.index(spread)]

    def start_vec(self):
        first = VEC_ROW - 15 * PAIR_ROWS - 400
        for dc in (0, 1):
            for dz2 in (0, 1):
                for dz1, dy, dx in SPREAD:
                    here = (self.z ^ (2 * dz2 + dz1), self.y ^ dy, self.core ^ dc, self.x ^ dx)
                    hit = (here[0] == HOLDER[0]) & (here[1] == HOLDER[1]) & (here[2] == HOLDER[2]) & (here[3] == HOLDER[3])

                    @pl.when(hit)
                    def _(source=self.buf(dc, dz2, (dz1, dy, dx))):
                        pltpu.make_async_copy(source.at[pl.ds(first, 32)], self.vec_low, self.vec_sem).start()

    def wait_vec(self):
        pltpu.make_async_copy(self.weights.at[pl.ds(0, 32)], self.vec_low, self.vec_sem).wait()

    def start_group(self, dz2):
        def rows(start, count):
            return pl.ds(pl.multiple_of(start, 16), count)

        for dz1 in (0, 1):
            for dy in (0, 1):
                for dc in (0, 1):
                    pair = (self.z ^ (2 * dz2 + dz1)) * 4 + (self.y ^ dy) * 2 + (self.core ^ dc)
                    base, sem = pair * PAIR_ROWS, self.sems.at[pair]
                    near, far = self.buf(dc, dz2, (dz1, dy, 0)), self.buf(dc, dz2, (dz1, dy, 1))
                    for source, x in ((near, self.x), (far, 1 - self.x)):
                        target = self.weights.at[rows(base + 400 * x, 384)]
                        pltpu.make_async_copy(source.at[pl.ds(0, 384)], target, sem).start()
                        pltpu.make_async_copy(source.at[pl.ds(384, 16)], self.seams.at[pair, x], sem).start()

    def start(self):
        self.start_vec()
        for low in (True, False):

            @pl.when((self.z < 2) == low)
            def _(low=low):
                for dz2 in (0, 1) if low else (1, 0):
                    self.start_group(dz2)

    def wait(self, pair):
        if pair not in self.ready:
            self.ready.add(pair)
            rows = self.weights.at[pl.ds(0, PAIR_ROWS + 16)]
            pltpu.make_async_copy(rows, rows, self.sems.at[pair]).wait()
            halves = [self.seams[pair, x].astype(F32)[:8] for x in (0, 1)]
            seam = pl.ds(pair * PAIR_ROWS + 384, 16)
            self.weights[seam, :] = jnp.concatenate(halves, axis=0).astype(BF16)

    def block(self, number):
        for pair in range(number * D // PAIR_ROWS, (number * D + D - 1) // PAIR_ROWS + 1):
            self.wait(pair)


class Direct:
    def __init__(self, w_hbm, weights, sems, vec_low, vec_sem):
        self.copies = {}
        for number in FIRST_BLOCKS:
            rows = pl.ds(number * D, D)
            self.copies[number] = pltpu.make_async_copy(w_hbm.at[rows], weights.at[rows], sems.at[number])
        self.vec = pltpu.make_async_copy(w_hbm.at[pl.ds(VEC_ROW, 32)], vec_low, vec_sem)
        self.ready = set()

    def start(self):
        self.vec.start()
        for number in FIRST_BLOCKS:
            self.copies[number].start()

    def wait_vec(self):
        self.vec.wait()

    def block(self, number):
        if number not in self.ready:
            self.ready.add(number)
            self.copies[number].wait()


def forward_kernel(queries, custom, left_ref, flags, xb_ref, m_hbm, *refs):
    count = 32 if custom else 1
    bufs, refs = refs[:count], refs[count:]
    qs_out, ks_out, vs_out, os_out, y1_out, qc_out, k_out, v_out, o_out, stat_ref = refs[:10]
    w_out = refs[10] if custom else None
    weights, m_ref, qs_ref, ks_ref, vs_ref, os_ref, y1_ref, qc_ref, k_ref, v_ref, o_ref, vec_low = refs[10 + custom : 22 + custom]
    seams, w_sems, m_sems, out_sems, kv_sems, vec_sem, all_sems = refs[22 + custom :]
    images = m_ref.shape[0]
    tokens = m_ref.shape[1]
    if custom:
        feed = Assembly(flags, bufs, weights, seams, w_sems, vec_low, vec_sem)
    else:
        feed = Direct(bufs[0], weights, w_sems, vec_low, vec_sem)

    def load_memory(image):
        return pltpu.make_async_copy(m_hbm.at[image], m_ref.at[image], m_sems.at[image])

    def matrix(block):
        feed.block(block)
        return weights[block * D : (block + 1) * D, :]

    def leave_weights(half):
        rows = pl.ds(half * 8 * PAIR_ROWS, 8 * PAIR_ROWS)
        return pltpu.make_async_copy(weights.at[rows], w_out.at[rows], all_sems.at[half])

    small = [(qs_ref, qs_out), (ks_ref, ks_out), (vs_ref, vs_out), (os_ref, os_out), (y1_ref, y1_out), (qc_ref, qc_out)]

    def leave(number):
        return pltpu.make_async_copy(*small[number], out_sems.at[number])

    def leave_image(image, number):
        source, target = [(k_ref, k_out), (v_ref, v_out), (o_ref, o_out)][number]
        return pltpu.make_async_copy(source.at[image], target.at[image], kv_sems.at[image, number])

    feed.start()
    for image in range(images):
        load_memory(image).start()
    feed.wait_vec()
    vec = vec_low[...].astype(F32)
    xb = xb_ref[...]
    qs_ref[...] = ((dot_nn(xb, matrix(0)) + vec[0:1, :]) * SCALE).astype(BF16)
    leave(0).start()
    ks_ref[...] = dot_nn(xb, matrix(1)).astype(BF16)
    leave(1).start()
    vs_ref[...] = (dot_nn(xb, matrix(2)) + vec[1:2, :]).astype(BF16)
    leave(2).start()
    masks = head_masks()
    real = lax.broadcasted_iota(jnp.int32, (2 * QP, QP), 1) < queries
    places = [(slice(i * QP, (i + 1) * QP), slice(p * LANES, (p + 1) * LANES)) for i in range(images) for p in range(PAIRS)]

    def raw_self(place):
        return dot_nt(two_heads(qs_ref[place], masks), ks_ref[place])

    following = raw_self(places[0])
    for number, place in enumerate(places):
        scores = following
        if number + 1 < len(places):
            following = raw_self(places[number + 1])
        scores = jnp.where(real, scores, NEG)
        probs = jnp.exp(scores - jnp.max(scores, axis=-1, keepdims=True))
        probs = probs / jnp.sum(probs, axis=-1, keepdims=True)
        os_ref[place] = join_heads(dot_nn(probs.astype(BF16), vs_ref[place])).astype(BF16)
    leave(3).start()
    y1 = xb.astype(F32) + (dot_nn(os_ref[...], matrix(3)) + vec[2:3, :])
    y1_ref[...] = y1
    leave(4).start()
    hat, _ = norm_parts(y1)
    x1 = hat * vec[11:12, :] + vec[12:13, :]
    qc_ref[...] = ((dot_nn(x1.astype(BF16), matrix(4)) + vec[3:4, :]) * SCALE).astype(BF16)
    leave(5).start()

    feed.block(5)
    feed.block(6)
    if custom:
        for pair in range(8):
            feed.wait(pair)
        leave_weights(0).start()
    column = lax.broadcasted_iota(jnp.int32, (2 * QP, 128), 1)
    for image in range(images):
        load_memory(image).wait()
        rows = slice(image * QP, (image + 1) * QP)
        k_ref[image] = dot_nn(m_ref[image], matrix(5)).astype(BF16)
        v_ref[image] = (dot_nn(m_ref[image], matrix(6)) + vec[4:5, :]).astype(BF16)
        leave_image(image, 0).start()
        leave_image(image, 1).start()
        valid = lax.broadcasted_iota(jnp.int32, (2 * QP, tokens), 1) < left_ref[image]
        stat = jnp.zeros((2 * QP, 128), F32)
        def raw(pair):
            lanes = slice(pair * LANES, (pair + 1) * LANES)
            return dot_nt(two_heads(qc_ref[rows, lanes], masks), k_ref[image, :, lanes])

        following = raw(0)
        for pair in range(PAIRS):
            lanes = slice(pair * LANES, (pair + 1) * LANES)
            scores = following
            if pair + 1 < PAIRS:
                following = raw(pair + 1)
            scores = jnp.where(valid, scores, NEG)
            top = jnp.max(scores, axis=-1, keepdims=True)
            probs = jnp.exp(scores - top)
            total = jnp.sum(probs, axis=-1, keepdims=True)
            mixed = dot_nn(probs.astype(BF16), v_ref[image, :, lanes]) / total
            o_ref[image, :, lanes] = join_heads(mixed).astype(BF16)
            stat = jnp.where(column == pair, top + jnp.log(total), stat)
        stat_ref[image] = jnp.where(left_ref[image] > 0, stat.T[:8], NEG)
        leave_image(image, 2).start()
        if custom and image == 0:
            for pair in range(8, 16):
                feed.wait(pair)
            leave_weights(1).start()
    for number in range(len(small)):
        leave(number).wait()
    for image in range(images):
        for number in range(3):
            leave_image(image, number).wait()
    if custom:
        leave_weights(0).wait()
        leave_weights(1).wait()


def forward(left, flags, xb, memory, bufs, queries):
    custom = len(bufs) > 1
    rows = xb.shape[0]
    images, tokens, _ = memory.shape
    narrow = jax.ShapeDtypeStruct((rows, D), BF16)
    tall = jax.ShapeDtypeStruct(memory.shape, BF16)
    anywhere = pl.BlockSpec(memory_space=pl.ANY)
    small = pltpu.VMEM((rows, D), BF16)
    large = pltpu.VMEM(memory.shape, BF16)
    held = 16 * PAIR_ROWS if custom else 7 * D
    return pl.pallas_call(
        partial(forward_kernel, queries, custom),
        grid_spec=pltpu.PrefetchScalarGridSpec(
            num_scalar_prefetch=2,
            grid=(1,),
            in_specs=[whole((rows, D)), anywhere] + [anywhere] * len(bufs),
            out_specs=[anywhere] * 9 + [whole((images, 8, 2 * QP))] + [anywhere] * custom,
            scratch_shapes=[
                pltpu.VMEM((held, D), BF16),
                large, small, small, small, small,
                pltpu.VMEM((rows, D), F32),
                small, large, large,
                pltpu.VMEM((images, QP, D), BF16),
                pltpu.VMEM((32, D), BF16),
                pltpu.VMEM((16, 2, 16, D), BF16),
                pltpu.SemaphoreType.DMA((16,)),
                pltpu.SemaphoreType.DMA((images,)),
                pltpu.SemaphoreType.DMA((6,)),
                pltpu.SemaphoreType.DMA((images, 3)),
                pltpu.SemaphoreType.DMA(()),
                pltpu.SemaphoreType.DMA((2,)),
            ],
        ),
        out_shape=[
            narrow, narrow, narrow, narrow,
            jax.ShapeDtypeStruct((rows, D), F32),
            narrow, tall, tall,
            jax.ShapeDtypeStruct((images, QP, D), BF16),
            jax.ShapeDtypeStruct((images, 8, 2 * QP), F32),
        ]
        + [jax.ShapeDtypeStruct((held, D), BF16)] * custom,
        cost_estimate=cost(0, 0),
        compiler_params=params(60),
        name="forward",
    )(left, flags, xb, memory, *bufs)


def pieces(start, count, size):
    found = []
    done = 0
    while done < count:
        pair, offset = divmod(start + done, size)
        length = min(count - done, size - offset)
        found.append((done, pair, offset, length))
        done += length
    return found


class Halves:
    def __init__(self, keep, send, my_core):
        self.keep, self.send, self.my_core = keep, send, my_core

    def copy(self, target, source, pair, offset, length, sem):
        place = pair // self.cores()
        index = []
        for extent in reversed(target.shape[:-2]):
            index.insert(0, place % extent)
            place = place // extent
        return pltpu.make_async_copy(source, target.at[(*index, pl.ds(offset, length))], sem)

    def cores(self):
        return 1 if self.send is None else 2

    def start(self, source, pair, offset, length, sem):
        if self.send is None:
            self.copy(self.keep, source, pair, offset, length, sem).start()
            return

        @pl.when(self.my_core == pair % 2)
        def _():
            self.copy(self.keep, source, pair, offset, length, sem).start()

        @pl.when(self.my_core != pair % 2)
        def _():
            self.copy(self.send, source, pair, offset, length, sem).start()

    def wait(self, source, pair, offset, length, sem):
        self.copy(self.keep, source, pair, offset, length, sem).wait()


def middle_kernel(parts, split, *refs):
    flags, y1_ref = refs[:2]
    o_refs, stat_refs = refs[2 : 2 + parts], refs[2 + parts : 2 + 2 * parts]
    refs = refs[2 + 2 * parts :]
    w_hbm, vec, cot_ref, match_ref, out_hbm = refs[:5]
    halves = Halves(refs[5], refs[6] if split else None, flags[0])
    refs = refs[6 + split :]
    cross_halves = Halves(refs[0], refs[1] if split else None, flags[0])
    refs = refs[1 + split :]
    db_ref, doc_ref, tot_ref, dvec_ref = refs[:4]
    ocf, ocb, y2, x2b, u, slope, acc, e3b, staged, blank, out_ref, dco_ref, co, feed = refs[4:18]
    sems, blank_sem, out_sem, side_sems, w_sems = refs[18:]
    phase, step = pl.program_id(0), pl.program_id(1)
    steps = FF // D
    images = match_ref.shape[0]
    column = lax.broadcasted_iota(jnp.int32, (2 * QP, 128), 1)
    lane = lax.broadcasted_iota(jnp.int32, (QP, LANES), 1)
    size = halves.keep.shape[-2]
    side = cross_halves.keep.shape[-2]

    def load(block):
        target = co if block == 7 else feed.at[block - 8]
        return pltpu.make_async_copy(w_hbm.at[pl.ds(block * D, D)], target, w_sems.at[block - 7])

    def leave_out():
        return pltpu.make_async_copy(out_ref, out_hbm, out_sem)

    def leave_side(act):
        starts = [(dco_ref, 3 * D - QUERY_HEAD, D), (staged.at[0, 0], 4 * D - QUERY_HEAD, HEAD_ROWS)]
        for which, (source, start, count) in enumerate(starts):
            if (which == 0) != (act[0] == "o"):
                continue
            for number, (done, pair, offset, length) in enumerate(pieces(start, count, side)):
                piece = source.at[pl.ds(done, length)]
                getattr(cross_halves, act[1])(piece, pair, offset, length, side_sems.at[which, number])

    def leave(which, at, act):
        skip = HEAD_ROWS if which + at == 0 else 0
        start = which * FF + at * D + skip - HEAD_ROWS
        for number, (done, pair, offset, length) in enumerate(pieces(start, D - skip, size)):
            source = staged.at[at % 2, which, pl.ds(done + skip, length)]
            getattr(halves, act)(source, pair, offset, length, sems.at[at, which, number])

    def leave_blank(act):
        for _, pair, offset, length in pieces(2 * FF - HEAD_ROWS, TAIL, size):
            getattr(halves, act)(blank, pair, offset, length, blank_sem)

    def ordered(first, second):
        if parts != 2:
            return first, second
        swap = flags[1] != 0
        return jnp.where(swap, second, first), jnp.where(swap, first, second)

    @pl.when((phase == 0) & (step == 0))
    def _():
        load(7).start()
        for at in range(steps):
            load(8 + at).start()
            load(8 + steps + at).start()
        for image in range(images):
            rows = slice(image * QP, (image + 1) * QP)
            stats = [ref[image] for ref in stat_refs]
            if parts == 2:
                stats = ordered(*stats)
            top = stats[0]
            for n in range(1, parts):
                top = jnp.maximum(top, stats[n])
            mass = [jnp.exp(stats[n] - top) for n in range(parts)]
            total = mass[0]
            for n in range(1, parts):
                total = total + mass[n]
            tot_ref[image, 0:8, :] = top + jnp.log(total)
            shares = [jnp.concatenate([m / total, jnp.zeros((120, 2 * QP), F32)], axis=0).T for m in mass]
            for pair in range(PAIRS):
                lanes = slice(pair * LANES, (pair + 1) * LANES)
                values = [ref[image, :, lanes].astype(F32) for ref in o_refs]
                if parts == 2:
                    values = ordered(*values)
                mixed = jnp.zeros((QP, LANES), F32)
                for n in range(parts):
                    share = shares[n][:, pair : pair + 1]
                    mixed = mixed + values[n] * jnp.where(lane < HEAD, share[:QP], share[QP:])
                ocf[rows, lanes] = mixed
        ocb[...] = ocf[...].astype(BF16)
        hat, _ = norm_parts(y1_ref[...])
        x1 = hat * vec[11:12, :] + vec[12:13, :]
        load(7).wait()
        total = x1 + (dot_nn(ocb[...], co[...]) + vec[5:6, :])
        y2[...] = total
        hat, _ = norm_parts(total)
        x2 = hat * vec[13:14, :] + vec[14:15, :]
        x2b[...] = x2.astype(BF16)
        acc[...] = x2 + vec[6:7, :]

    for at in range(steps):

        @pl.when((phase == 0) & (step == at))
        def _(at=at):
            load(8 + at).wait()
            load(8 + steps + at).wait()

    f1, f2 = feed.at[step], feed.at[steps + step]

    @pl.when(phase == 0)
    def _():
        h = dot_nt(x2b[...], f1[...]) + vec[pl.ds(7 + step, 1), :]
        root = 0.7978845608028654
        square = h * h
        t = jnp.tanh(root * (h + 0.044715 * (h * square)))
        half = 0.5 * (1.0 + t)
        slope[step] = half + (0.5 * root) * h * (1.0 - t * t) * (1.0 + 0.134145 * square)
        active = (h * half).astype(BF16)
        u[step] = active
        acc[...] += dot_nn(active, f2[...])

    @pl.when((phase == 1) & (step == 0))
    def _():
        blank[...] = jnp.zeros_like(blank)
        leave_blank("start")
        dvec_ref[...] = jnp.zeros_like(dvec_ref)
        hat, inverse = norm_parts(acc[...])
        out = hat * vec[15:16, :] + vec[16:17, :]
        grads = []
        for image in range(images):
            out_ref[image] = out[image * QP : (image + 1) * QP]
            matched = match_ref[image]
            hit = lax.broadcasted_iota(jnp.int32, (QP, matched.shape[1]), 0) == matched
            grads.append(dot_nn(jnp.where(hit, 1.0, 0.0).astype(BF16), cot_ref[image]))
        leave_out().start()
        dy = jnp.concatenate(grads, axis=0)
        dvec_ref[15:16, :] = rowsum(dy * hat)
        dvec_ref[16:17, :] = rowsum(dy)
        dc = norm_back(dy, hat, inverse, vec[15:16, :])
        low = dc.astype(BF16)
        e3b[...] = low
        dvec_ref[6:7, :] = rowsum(low)
        acc[...] = dc

    for at in range(2, steps):

        @pl.when((phase == 1) & (step == at))
        def _(at=at):
            leave(0, at - 2, "wait")
            leave(1, at - 2, "wait")
            if at == 2:
                leave_side(("f", "wait"))

    @pl.when(phase == 1)
    def _():
        du = dot_nt(e3b[...], f2[...])
        dh = (du * slope[step]).astype(BF16)
        slot = lax.rem(step, 2)
        staged[slot, 1] = dot_tn(u[step], e3b[...]).astype(BF16)
        staged[slot, 0] = dot_tn(dh, x2b[...]).astype(BF16)

        @pl.when(step == 0)
        def _():
            leave_side(("f", "start"))

        for at in range(steps):

            @pl.when(step == at)
            def _(at=at):
                leave(0, at, "start")
                leave(1, at, "start")

        dvec_ref[pl.ds(7 + step, 1), :] = rowsum(dh)
        acc[...] += dot_nn(dh, f1[...])

    @pl.when((phase == 1) & (step == steps - 1))
    def _():
        hat, inverse = norm_parts(y2[...])
        dy = acc[...]
        dvec_ref[13:14, :] = rowsum(dy * hat)
        dvec_ref[14:15, :] = rowsum(dy)
        db = norm_back(dy, hat, inverse, vec[13:14, :])
        db_ref[...] = db
        low = db.astype(BF16)
        dvec_ref[5:6, :] = rowsum(low)
        dco_ref[...] = dot_tn(ocb[...], low).astype(BF16)
        leave_side(("o", "start"))
        doc = dot_nt(low, co[...]).astype(BF16)
        doc_ref[...] = doc
        both = doc.astype(F32) * ocf[...]
        for image in range(images):
            rows = slice(image * QP, (image + 1) * QP)
            tot = jnp.zeros((2 * QP, 128), F32)
            for pair in range(PAIRS):
                piece = both[rows, pair * LANES : (pair + 1) * LANES]
                one = jnp.sum(jnp.where(lane < HEAD, piece, 0.0), axis=-1, keepdims=True)
                two = jnp.sum(jnp.where(lane < HEAD, 0.0, piece), axis=-1, keepdims=True)
                tot = jnp.where(column == pair, jnp.concatenate([one, two], axis=0), tot)
            tot_ref[image, 8:16, :] = tot.T[:8]
        leave_blank("wait")
        leave_out().wait()
        leave_side(("o", "wait"))
        for which in (0, 1):
            leave(which, steps - 2, "wait")
            leave(which, steps - 1, "wait")


def halves_shape(shape, split):
    return [jax.ShapeDtypeStruct(shape, BF16)] * (1 + split)


def middle(flags, y1, o_parts, stat_parts, w, vec, cot, matched, far_shape, cross_shape, split):
    rows = y1.shape[0]
    images = cot.shape[0]
    steps = FF // D
    parts = len(o_parts)
    anywhere = pl.BlockSpec(memory_space=pl.ANY)
    return pl.pallas_call(
        partial(middle_kernel, parts, split),
        grid_spec=pltpu.PrefetchScalarGridSpec(
            num_scalar_prefetch=1,
            grid=(2, steps),
            in_specs=[whole(y1.shape)]
            + [whole(o_parts[0].shape)] * parts
            + [whole(stat_parts[0].shape)] * parts
            + [anywhere, whole((VECS, D)), whole(cot.shape), whole((images, 1, matched.shape[1]))],
            out_specs=[anywhere] * (3 + 2 * split)
            + [
                whole((rows, D)),
                whole((rows, D)),
                whole((images, 16, 2 * QP)),
                whole((VECS, D)),
            ],
            scratch_shapes=[
                pltpu.VMEM((rows, D), F32),
                pltpu.VMEM((rows, D), BF16),
                pltpu.VMEM((rows, D), F32),
                pltpu.VMEM((rows, D), BF16),
                pltpu.VMEM((steps, rows, D), BF16),
                pltpu.VMEM((steps, rows, D), F32),
                pltpu.VMEM((rows, D), F32),
                pltpu.VMEM((rows, D), BF16),
                pltpu.VMEM((2, 2, D, D), BF16),
                pltpu.VMEM((TAIL, D), BF16),
                pltpu.VMEM((images, QP, D), F32),
                pltpu.VMEM((D, D), BF16),
                pltpu.VMEM((D, D), BF16),
                pltpu.VMEM((2 * steps, D, D), BF16),
                pltpu.SemaphoreType.DMA((steps, 2, 2)),
                pltpu.SemaphoreType.DMA(()),
                pltpu.SemaphoreType.DMA(()),
                pltpu.SemaphoreType.DMA((2, 2)),
                pltpu.SemaphoreType.DMA((1 + 2 * steps,)),
            ],
        ),
        out_shape=[jax.ShapeDtypeStruct((images, QP, D), F32)]
        + halves_shape(far_shape, split)
        + halves_shape(cross_shape, split)
        + [
            jax.ShapeDtypeStruct((rows, D), F32),
            jax.ShapeDtypeStruct((rows, D), BF16),
            jax.ShapeDtypeStruct((images, 16, 2 * QP), F32),
            jax.ShapeDtypeStruct((VECS, D), F32),
        ],
        cost_estimate=cost(2 * rows * D * (6 * FF + 3 * D), 2 * FF * D * 6),
        compiler_params=params(60),
        name="middle",
    )(flags, y1, *o_parts, *stat_parts, w, vec, cot, matched[:, None, :])


def cross_backward_kernel(left_ref, q_ref, k_ref, v_ref, do_ref, tot_ref, dq_ref, dk_ref, dv_ref):
    tokens = k_ref.shape[1]
    masks = head_masks()
    valid = lax.broadcasted_iota(jnp.int32, (tokens, 2 * QP), 0) < left_ref[pl.program_id(0)]
    def raw(pair):
        lanes = slice(pair * LANES, (pair + 1) * LANES)
        query = two_heads(q_ref[0, :, lanes], masks)
        dout = two_heads(do_ref[0, :, lanes], masks)
        return query, dout, dot_nt(k_ref[0, :, lanes], query), dot_nt(v_ref[0, :, lanes], dout)

    following = raw(0)
    for pair in range(PAIRS):
        lanes = slice(pair * LANES, (pair + 1) * LANES)
        query, dout, scores, dprobs = following
        if pair + 1 < PAIRS:
            following = raw(pair + 1)
        probs = jnp.where(valid, jnp.exp(scores - tot_ref[0, pair : pair + 1, :]), 0.0)
        dscores = (probs * (dprobs - tot_ref[0, 8 + pair : 9 + pair, :])).astype(BF16)
        dv_ref[0, :, lanes] = dot_nn(probs.astype(BF16), dout).astype(BF16)
        dk_ref[0, :, lanes] = dot_nn(dscores, query).astype(BF16)
        dq_ref[0, :, lanes] = join_heads(dot_tn(k_ref[0, :, lanes], dscores).T).astype(BF16)


def cross_backward(left, qc, key, value, doc, tot):
    images, tokens, _ = key.shape
    q_block = pl.BlockSpec((1, QP, D), lambda i, _: (i, 0, 0))
    m_block = pl.BlockSpec((1, tokens, D), lambda i, _: (i, 0, 0))
    s_block = pl.BlockSpec((1, 16, 2 * QP), lambda i, _: (i, 0, 0))
    return pl.pallas_call(
        cross_backward_kernel,
        grid_spec=pltpu.PrefetchScalarGridSpec(
            num_scalar_prefetch=1,
            grid=(images,),
            in_specs=[q_block, m_block, m_block, q_block, s_block],
            out_specs=[q_block, m_block, m_block],
        ),
        out_shape=[
            jax.ShapeDtypeStruct((images, QP, D), BF16),
            jax.ShapeDtypeStruct(key.shape, BF16),
            jax.ShapeDtypeStruct(key.shape, BF16),
        ],
        cost_estimate=cost(4 * images * 2 * QP * tokens * D // 3, images * tokens * D * 8),
        compiler_params=params(60),
        name="cross_backward",
    )(left, qc.reshape(images, QP, D), key, value, doc.reshape(images, QP, D), tot)


def memory_weights_kernel(split, flags, *refs):
    m_ref, dk_ref, dv_ref = refs[1 + split : 4 + split]
    refs = refs[4 + split :]
    gb_ref = refs[0]
    halves = Halves(refs[1], refs[2] if split else None, flags[0])
    low, sems = refs[2 + split :]
    def leave(which, act):
        start = (1 + which) * D - QUERY_HEAD
        for number, (done, pair, offset, length) in enumerate(pieces(start, D, halves.keep.shape[-2])):
            piece = low.at[which, pl.ds(done, length)]
            getattr(halves, act)(piece, pair, offset, length, sems.at[which, number])

    tall = m_ref[...].reshape(-1, D)
    for which, ref in ((0, dk_ref), (1, dv_ref)):
        low[which] = dot_tn(tall, ref[...].reshape(-1, D)).astype(BF16)
        leave(which, "start")
    gb_ref[...] = jnp.broadcast_to(rowsum(dv_ref[...].reshape(-1, D)), gb_ref.shape)
    for which in (0, 1):
        leave(which, "wait")


def memory_weights(flags, cross, memory, dk, dv, split):
    images, tokens, _ = memory.shape
    block = whole(memory.shape)
    anywhere = pl.BlockSpec(memory_space=pl.ANY)
    return pl.pallas_call(
        partial(memory_weights_kernel, split),
        grid_spec=pltpu.PrefetchScalarGridSpec(
            num_scalar_prefetch=1,
            grid=(1,),
            in_specs=[anywhere] * (1 + split) + [block, block, block],
            out_specs=[whole((8, D))] + [anywhere] * (1 + split),
            scratch_shapes=[
                pltpu.VMEM((2, D, D), BF16),
                pltpu.SemaphoreType.DMA((2, 2)),
            ],
        ),
        out_shape=[jax.ShapeDtypeStruct((8, D), F32)] + halves_shape(cross[0].shape, split),
        input_output_aliases={1 + n: 1 + n for n in range(1 + split)},
        cost_estimate=cost(4 * images * tokens * D * D, images * tokens * D * 6),
        compiler_params=params(60),
        name="memory_weights",
    )(flags, *cross, memory, dk, dv)


def memory_grads_kernel(dk_ref, dv_ref, ck, cv, gm_ref):
    gm_ref[0] = dot_nt(dk_ref[0], ck[...]) + dot_nt(dv_ref[0], cv[...])


def memory_grads(dk, dv, w):
    images, tokens, _ = dk.shape
    block = pl.BlockSpec((1, tokens, D), lambda i: (i, 0, 0))
    return pl.pallas_call(
        memory_grads_kernel,
        grid=(images,),
        in_specs=[block, block, weight_block(5), weight_block(6)],
        out_specs=block,
        out_shape=jax.ShapeDtypeStruct(dk.shape, F32),
        cost_estimate=pl.CostEstimate(
            flops=4 * images * tokens * D * D, bytes_accessed=images * tokens * D * 8, transcendentals=0
        ),
        compiler_params=params(60),
        name="memory_grads",
    )(dk, dv, w, w)


class Loads:
    def __init__(self, pairs, sems):
        self.copies = [(pltpu.make_async_copy(source, target, sems.at[n]), target) for n, (source, target) in enumerate(pairs)]
        self.ready = set()
        for copy, _ in self.copies:
            copy.start()

    def __call__(self, number):
        copy, target = self.copies[number]
        if number not in self.ready:
            copy.wait()
            self.ready.add(number)
        return target[...]


def query_backward_kernel(parts, split, flags, *refs):
    sources, vec = refs[1 + split : 4 + split + parts], refs[4 + split + parts]
    refs = refs[5 + split + parts :]
    da_ref, gq_head_ref, dvec_ref = refs[:3]
    halves = Halves(refs[3], refs[4] if split else None, flags[0])
    refs = refs[4 + split :]
    targets, staged, load_sems, sems = refs[: 3 + parts], refs[3 + parts], refs[4 + parts], refs[5 + parts]
    w_hbm = sources[-1]
    sources = [*sources[:-1], w_hbm.at[pl.ds(4 * D, D)]]
    get = Loads(list(zip(sources, targets)), load_sems)

    def leave(act):
        for number, (done, pair, offset, length) in enumerate(pieces(0, D - QUERY_HEAD, halves.keep.shape[-2])):
            piece = staged.at[pl.ds(done + QUERY_HEAD, length)]
            getattr(halves, act)(piece, pair, offset, length, sems.at[number])

    total = get(0).astype(F32)
    for number in range(1, parts):
        total = total + get(number).astype(F32)
    dq = total.astype(BF16) * SCALE
    hat, inverse = norm_parts(get(parts))
    gain = vec[11:12, :]
    x1b = (hat * gain + vec[12:13, :]).astype(BF16)
    gcq = dot_tn(x1b, dq).astype(BF16)
    staged[...] = gcq
    leave("start")
    gq_head_ref[...] = gcq[:QUERY_HEAD]
    dvec_ref[...] = jnp.zeros_like(dvec_ref)
    dvec_ref[3:4, :] = rowsum(dq)
    dy = get(parts + 1) + dot_nt(dq, get(parts + 2))
    dvec_ref[11:12, :] = rowsum(dy * hat)
    dvec_ref[12:13, :] = rowsum(dy)
    da = norm_back(dy, hat, inverse, gain)
    da_ref[...] = da
    dvec_ref[2:3, :] = rowsum(da.astype(BF16))
    leave("wait")


def query_backward(flags, cross, y1, db, dq_parts, w, vec, split):
    rows = y1.shape[0]
    parts = len(dq_parts)
    full = whole((rows, D))
    anywhere = pl.BlockSpec(memory_space=pl.ANY)
    return pl.pallas_call(
        partial(query_backward_kernel, parts, split),
        grid_spec=pltpu.PrefetchScalarGridSpec(
            num_scalar_prefetch=1,
            grid=(1,),
            in_specs=[anywhere] * (4 + split + parts) + [whole((VECS, D))],
            out_specs=[full, whole((QUERY_HEAD, D)), whole((VECS, D))] + [anywhere] * (1 + split),
            scratch_shapes=[pltpu.VMEM((rows, D), BF16)] * parts
            + [pltpu.VMEM((rows, D), F32)] * 2
            + [pltpu.VMEM((D, D), BF16)] * 2
            + [pltpu.SemaphoreType.DMA((parts + 3,)), pltpu.SemaphoreType.DMA((2,))],
        ),
        out_shape=[
            jax.ShapeDtypeStruct((rows, D), F32),
            jax.ShapeDtypeStruct((QUERY_HEAD, D), BF16),
            jax.ShapeDtypeStruct((VECS, D), F32),
        ]
        + halves_shape(cross[0].shape, split),
        input_output_aliases={1 + n: 3 + n for n in range(1 + split)},
        cost_estimate=cost(4 * rows * D * D, rows * D * 16),
        compiler_params=params(60),
        name="query_backward",
    )(flags, *cross, *[part.reshape(rows, D) for part in dq_parts], y1, db, w, vec)


def self_backward_kernel(queries, split, *refs):
    flags, os_hbm, da_hbm, qs_hbm, ks_hbm, vs_hbm, x_hbm, w_hbm, gq_ref, gx_ref, dvec_ref, keep_ref = refs[:12]
    halves = Halves(keep_ref, refs[12] if split else None, flags[0])
    sq, sk, sv, g_ref, os_ref, da_ref, ao, qs, ks, vs, x_ref, aq, ak, av, sems, load_sems = refs[12 + split :]
    size = keep_ref.shape[-2]
    matrices = [w_hbm.at[pl.ds(block * D, D)] for block in range(4)]
    get = Loads(
        [(os_hbm, os_ref), (da_hbm, da_ref), (matrices[3], ao), (qs_hbm, qs), (ks_hbm, ks), (vs_hbm, vs)]
        + [(x_hbm, x_ref), (matrices[0], aq), (matrices[1], ak), (matrices[2], av)],
        load_sems,
    )

    def leave(pair, act):
        getattr(halves, act)(g_ref.at[pl.ds(pair * size, size)], pair, 0, size, sems.at[pair])

    pairs = g_ref.shape[0] // size
    images = x_ref.shape[0] // QP
    dvec_ref[...] = jnp.zeros_like(dvec_ref)
    os = get(0)
    da = get(1)
    low = da.astype(BF16)
    g_ref[4 * D :, :] = gq_ref[...]
    g_ref[3 * D : 4 * D, :] = dot_tn(os, low).astype(BF16)
    dos = dot_nt(low, get(2)).astype(BF16)
    for number in (3, 4, 5):
        get(number)
    masks = head_masks()
    real = lax.broadcasted_iota(jnp.int32, (QP, 2 * QP), 0) < queries
    places = [(slice(i * QP, (i + 1) * QP), slice(p * LANES, (p + 1) * LANES)) for i in range(images) for p in range(PAIRS)]

    def raw(place):
        query = two_heads(qs[place], masks)
        dout = two_heads(dos[place], masks)
        return query, dout, dot_nt(ks[place], query), dot_nt(vs[place], dout)

    following = raw(places[0])
    for number, place in enumerate(places):
        query, dout, scores, dprobs = following
        if number + 1 < len(places):
            following = raw(places[number + 1])
        scores = jnp.where(real, scores, NEG)
        probs = jnp.exp(scores - jnp.max(scores, axis=0, keepdims=True))
        probs = probs / jnp.sum(probs, axis=0, keepdims=True)
        dscores = (probs * (dprobs - jnp.sum(probs * dprobs, axis=0, keepdims=True))).astype(BF16)
        sv[place] = dot_nn(probs.astype(BF16), dout).astype(BF16)
        sk[place] = dot_nn(dscores, query).astype(BF16)
        sq[place] = join_heads(dot_tn(ks[place], dscores).T).astype(BF16) * SCALE
    dvec_ref[0:1, :] = rowsum(sq[...])
    dvec_ref[1:2, :] = rowsum(sv[...])
    xb = get(6)
    g_ref[2 * D : 3 * D, :] = dot_tn(xb, sv[...]).astype(BF16)
    for pair in range(2, pairs):
        leave(pair, "start")
    g_ref[D : 2 * D, :] = dot_tn(xb, sk[...]).astype(BF16)
    for pair in range(1, min(2, pairs)):
        leave(pair, "start")
    g_ref[0:D, :] = dot_tn(xb, sq[...]).astype(BF16)
    leave(0, "start")
    gx = da + dot_nt(sq[...], get(7)) + dot_nt(sk[...], get(8)) + dot_nt(sv[...], get(9))
    for image in range(images):
        gx_ref[image] = gx[image * QP : (image + 1) * QP]
    for pair in range(pairs):
        leave(pair, "wait")


def self_backward(flags, xb, qs, ks, vs, os, da, gq_head, w, queries, shape, split):
    rows = xb.shape[0]
    images = rows // QP
    anywhere = pl.BlockSpec(memory_space=pl.ANY)
    return pl.pallas_call(
        partial(self_backward_kernel, queries, split),
        grid_spec=pltpu.PrefetchScalarGridSpec(
            num_scalar_prefetch=1,
            grid=(1,),
            in_specs=[anywhere] * 7 + [whole((QUERY_HEAD, D))],
            out_specs=[whole((images, QP, D)), whole((VECS, D))] + [anywhere] * (1 + split),
            scratch_shapes=[pltpu.VMEM((rows, D), BF16)] * 3
            + [pltpu.VMEM((4 * D + QUERY_HEAD, D), BF16), pltpu.VMEM((rows, D), BF16), pltpu.VMEM((rows, D), F32)]
            + [pltpu.VMEM((D, D), BF16)]
            + [pltpu.VMEM((rows, D), BF16)] * 4
            + [pltpu.VMEM((D, D), BF16)] * 3
            + [pltpu.SemaphoreType.DMA((4,)), pltpu.SemaphoreType.DMA((10,))],
        ),
        out_shape=[
            jax.ShapeDtypeStruct((images, QP, D), F32),
            jax.ShapeDtypeStruct((VECS, D), F32),
        ]
        + halves_shape(shape, split),
        cost_estimate=cost(16 * rows * D * D * 2, 8 * D * D * 2),
        compiler_params=params(60),
        name="self_backward",
    )(flags, os, da, qs, ks, vs, xb, w, gq_head)


class Place:
    def __init__(self):
        place = lax.axis_index("dp")
        self.x = lax.axis_index("seq")
        self.c = lax.rem(place, 2)
        self.y = lax.rem(place // 2, 2)
        self.z = place // 4


def pick(array, index, axis):
    return lax.dynamic_index_in_dim(array, index, axis, keepdims=False)


def over_core(v):
    return lax.ppermute(v, "dp", [(i, i ^ 1) for i in range(16)])


def over_y(v):
    return lax.ppermute(v, "dp", [(i, i ^ 2) for i in range(16)])


def over_x(v):
    return lax.ppermute(v, "seq", [(0, 1), (1, 0)])


def over_z(v, hops):
    return lax.ppermute(v, "dp", [(4 * a + i, 4 * b + i) for a, b in hops for i in range(4)])


def over_far(v):
    return over_z(v, [(0, 2), (2, 0), (1, 3), (3, 1)])


def over_near(v):
    return over_z(v, SWAP_ONE)


def spread(own):
    x, y, z = over_x(own), over_y(own), over_near(own)
    xy, yz, zx = over_x(y), over_y(z), over_near(x)
    return own, x, y, z, xy, yz, zx


def gather(at, rows):
    rest = jnp.zeros((8, D), BF16)
    own = jnp.where(at.x == 0, jnp.concatenate([rows, rest]), jnp.concatenate([rows[8:], rows[:8], rest]))
    other = over_far(own)
    here, there = spread(own), spread(other)
    found = [*here, over_x(here[5]), *there, over_y(there[6])]
    return found + [over_core(part) for part in found]


def tie(*values):
    return lax.optimization_barrier(values)


def add(kept, came):
    return (kept.astype(F32) + came.astype(F32)).astype(BF16)


def own_half(pairs, x):
    half = pairs.shape[-2] // 2
    return pick(pairs.reshape(*pairs.shape[:-2], 2, half, D), x, pairs.ndim - 2)


def blocks_of(pairs):
    return pairs.reshape(*pairs.shape[:-2], 2, pairs.shape[-2] // 2, D)


def picked(pairs, half, x):
    return pick(pick(pairs, half, 0), x, 0)


def merge(body, flags, sources, out_rows, name):
    parts = 2
    specs = []
    for array, where in sources:
        lead = (None,) * (array.ndim - 2)
        shape = (*lead, array.shape[-2], D // parts)
        specs.append(pl.BlockSpec(shape, lambda i, f, where=where: (*where(f), 0, i)))
    return pl.pallas_call(
        body,
        grid_spec=pltpu.PrefetchScalarGridSpec(
            num_scalar_prefetch=1,
            grid=(parts,),
            in_specs=specs,
            out_specs=[
                pl.BlockSpec((*rows, D // parts), lambda i, f, n=len(rows): (*[0] * n, i)) for rows in out_rows
            ],
        ),
        out_shape=[jax.ShapeDtypeStruct((*rows, D), BF16) for rows in out_rows],
        cost_estimate=cost(0, 0),
        compiler_params=params(60),
        name=name,
    )(flags, *[array for array, _ in sources])


def far_send_kernel(flags, a, b, c, d, out):
    out[0] = add(a[...], b[...])
    out[1] = add(c[...], d[...])


def far_send(flags, kept, came):
    kept, came = blocks_of(kept), blocks_of(came)
    sources = []
    for r in (0, 1):
        sources += [(part, lambda f, r=r: (r, 1 - f[2], f[1])) for part in (kept, came)]
    return merge(far_send_kernel, flags, sources, [(2, kept.shape[-2])], "far_send")[0]


def core_merge_kernel(flags, *refs):
    ins, outs = refs[:14], refs[14:]
    for number in range(2):
        first, second, third = ins[3 * number : 3 * number + 3]
        outs[number][...] = (first[...].astype(F32) + second[...].astype(F32) + third[...].astype(F32)).astype(BF16)
    outs[2][...] = add(ins[6][...], ins[7][...])
    outs[3][...] = add(ins[8][...], ins[9][...])
    message = outs[4]
    block = ins[10].shape[0]
    message[:block, :] = add(ins[10][...], ins[11][...])
    spill = message.shape[0] - (block + 8)
    total = ins[12][...].astype(F32) + ins[13][...].astype(F32)
    message[block:, :] = jnp.concatenate([jnp.zeros((8, total.shape[1]), F32), total[block - spill :]]).astype(BF16)


def core_merge(flags, far, far_came, far_last, cross, cross_came):
    far, far_came, cross, cross_came = [blocks_of(v) for v in (far, far_came, cross, cross_came)]
    block = cross.shape[-2]
    spill = 2 * block - (D - QUERY_HEAD)
    sources = []
    for r in (lambda f: 1 - f[3] % 2, lambda f: f[3] % 2):
        sources += [(part, lambda f, r=r: (r(f), f[2], f[1])) for part in (far, far_came)]
        sources += [(far_last, lambda f, r=r: (r(f),))]
    chosen = [
        lambda f: (0, f[1]),
        lambda f: (1, f[1]),
        lambda f: (1 - f[0], 1 - f[1]),
        lambda f: (0, 1 - f[1]),
    ]
    for where in chosen:
        sources += [(cross, where), (cross_came, where)]
    return merge(core_merge_kernel, flags, sources, [(block,)] * 4 + [(block + 8 + spill,)], "core_merge")


def cross_second(at, mine, came):
    start = D - QUERY_HEAD
    block = mine[0].shape[-2]
    spill = 2 * block - start
    main = came[:block].astype(F32)
    tall = jnp.concatenate([jnp.zeros((block - spill, D), F32), came[block + 8 :].astype(F32)])
    ids = (at.c * 2 + at.x) * block + jnp.arange(block)[:, None]

    def half(index, y):
        part = jnp.where((at.c == 0) & (y == 0), tall, main)
        place = ids + y * 4 * block
        shared = (place >= start) & (place < start + 2 * D)
        own = jnp.where(index == 0, mine[0], mine[1]).astype(F32)
        return (own + jnp.where(shared, part, 0.0)).astype(BF16)

    return half(1 - at.y, 1 - at.y), half(at.y, at.y)


SWAP_ONE = [(0, 1), (1, 0), (2, 3), (3, 2)]
SWAP_TWO = [(0, 2), (2, 0), (1, 3), (3, 1)]


def with_rows(message, vec_rows):
    return jnp.concatenate([message, vec_rows.astype(BF16)])


def finish(at, flags, block, far, far_last, near, near_send, cross, cross_came, vec_rows, extra):
    near_came = over_core(near_send)
    vec_came = over_core(vec_rows)
    far_out, far, low, high, message = core_merge(flags, *far, far_last, cross, cross_came)
    near_came, message, far_out, low, high, far = tie(near_came, message, far_out, low, high, far)
    came = over_x(message)
    near, near_came = blocks_of(near), blocks_of(near_came)
    near_send = add(picked(near, 1 - at.y, at.x), picked(near_came, 1 - at.y, at.x))
    near = add(picked(near, at.y, at.x), picked(near_came, at.y, at.x))
    vec_rows = vec_rows + vec_came
    near_send, near, vec_rows, dk, dv, w = tie(near_send, near, vec_rows, *extra)
    near_came, far_came = over_y(near_send), over_z(with_rows(far_out, vec_rows), SWAP_ONE)
    gm = memory_grads(dk, dv, w)
    gm, came = tie(gm, came)
    send, cross = cross_second(at, (low, high), came)
    send, near_came, far_came, cross = tie(send, near_came, far_came, cross)

    near = add(near, near_came)
    far = add(far, far_came[:block])
    vec_rows = vec_rows + far_came[block:].astype(F32)
    near, far, vec_rows, send = tie(near, far, vec_rows, send)
    cross_came, near_came = over_y(with_rows(send, vec_rows)), over_z(near, [(3, 2), (1, 0)])
    cut = block // 16 * 8
    far_top = over_z(far[:cut], [(0, 2), (1, 3)])
    cross = add(cross, cross_came[:block])
    near = add(near, near_came)
    vec_rows = vec_rows + cross_came[block:].astype(F32)
    near, cross, vec_rows, far_top, far = tie(near, cross, vec_rows, far_top, far)

    cross_came, near_came = over_z(cross, [(3, 2), (0, 1)]), over_z(near, [(2, 0)])
    cross = add(cross, cross_came)
    near_came, cross, far, vec_rows = tie(near_came, cross, far, vec_rows)

    cross_came, far_low = over_z(cross, [(2, 1)]), over_z(with_rows(far[cut:], vec_rows), [(0, 2), (1, 3)])
    far_came = jnp.concatenate([far_top, far_low[: block - cut]])
    vec_rows = vec_rows + far_low[block - cut :].astype(F32)
    kept = jnp.where(at.z >= 2, far, jnp.where(at.z == 0, near, cross))
    came = jnp.where(at.z >= 2, far_came, jnp.where(at.z == 0, near_came, cross_came))
    grad_rows = kept.astype(F32) + came.astype(F32)
    start = VEC_ROW - 31 * block
    last = jnp.concatenate([grad_rows[:start], vec_rows, jnp.zeros((block - start - VECS, D), F32)])
    is_last = (lax.axis_index("dp") == 15) & (at.x == 1)
    return jnp.where(is_last, last, grad_rows), gm


def shards(custom, inputs, memory, lengths, matched, cotangent, weights):
    axes = ("dp", "seq")
    share = 1.0 / lax.axis_size("seq")
    images, queries, _ = inputs.shape
    tokens = memory.shape[1]
    block = weights.shape[1]
    at = Place()
    left = lengths - at.x * tokens
    flags = jnp.stack([at.c if custom else 0, at.x, at.y, at.z]).astype(jnp.int32)

    def parts_of(value):
        if custom:
            return [value, over_x(value)]
        gathered = lax.all_gather(value, "seq")
        return [gathered[n] for n in range(gathered.shape[0])]

    if custom:
        bufs = gather(at, weights[0])
    else:
        bufs = [lax.all_gather(weights[0], axes, axis=0, tiled=True)]
    xb = jnp.pad(inputs, ((0, 0), (0, QP - queries), (0, 0))).reshape(images * QP, D)
    qs, ks, vs, os, y1, qc, key, value, mixed, stat, *w = forward(left, flags, xb, memory, bufs, queries)
    w = w[0] if custom else bufs[0]
    vec = w[VEC_ROW : VEC_ROW + VECS].astype(F32)
    near_rows = 4 * D + QUERY_HEAD
    far_rows = 2 * FF - HEAD_ROWS + TAIL
    cross_rows = 4 * D - QUERY_HEAD + HEAD_ROWS
    far_shape = (2, 2, 2 * block, D) if custom else (far_rows, D)
    near_shape = (2, 2 * block, D) if custom else (near_rows, D)
    cross_shape = (2, 2 * block, D) if custom else (cross_rows, D)
    out, *grads, db, doc, tot, dvec_mid = middle(
        flags, y1, parts_of(mixed), parts_of(stat), w, vec, cotangent, matched, far_shape, cross_shape, custom
    )
    far, cross = grads[: 1 + custom], grads[1 + custom :]
    if custom:
        far_came = over_core(far[1])
    dq, dk, dv = cross_backward(left, qc, key, value, doc, tot)
    dq_parts = parts_of(dq)
    if custom:
        far = [far[0], far_came]
        dk, message = tie(dk, far_send(flags, *far))
        far_last = over_y(message)
    dcv_row, *cross = memory_weights(flags, cross, memory, dk, dv, custom)
    if custom:
        dcv_row = dcv_row + over_x(dcv_row)
    da, gq_head, dvec_query, *cross = query_backward(flags, cross, y1, db, dq_parts, w, vec, custom)
    if custom:
        cross_came = over_core(cross[1])
    gq_head, dcv_row = tie(gq_head, dcv_row)
    gx, dvec_self, *near = self_backward(
        flags, xb, qs, ks, vs, os, da, gq_head, w, queries, near_shape, custom
    )
    vec_rows = (dvec_mid + dvec_query + dvec_self) * (1.0 if custom else share)
    is_value_bias = jnp.arange(VECS)[:, None] == 4
    vec_rows = jnp.where(is_value_bias, dcv_row[0:1], vec_rows)
    if custom:
        far_last, near_send = tie(far_last, near[1])
        grad_rows, gm = finish(
            at, flags, block, far, far_last, near[0], near_send, cross[0], cross_came, vec_rows, (dk, dv, w)
        )
    else:
        gm = memory_grads(dk, dv, w)
        low_share = jnp.asarray(share, BF16)
        pad = lax.axis_size(axes) * block - VEC_ROW - VECS
        last = 2 * FF - HEAD_ROWS
        memory_rows = slice(D - QUERY_HEAD, 3 * D - QUERY_HEAD)
        grads = jnp.concatenate(
            [near[0] * low_share, cross[0][: memory_rows.start] * low_share, cross[0][memory_rows]]
            + [cross[0][memory_rows.stop :] * low_share, far[0][:last] * low_share]
            + [vec_rows.astype(BF16), jnp.zeros((pad, D), BF16)]
        )
        grad_rows = lax.psum_scatter(grads, axes, scatter_dimension=0, tiled=True).astype(F32)
    return out[:, :queries], gx[:, :queries], gm, grad_rows[None]


def solution(mesh):
    placed = (
        P("dp", None, None),
        P("dp", "seq", None),
        P("dp"),
        P("dp", None),
        P("dp", None, None),
        P(None, ("dp", "seq"), None),
    )
    custom = dict(mesh.shape) == {"dp": 16, "seq": 2}
    return jax.shard_map(
        partial(shards, custom),
        mesh=mesh,
        in_specs=placed,
        out_specs=(
            P("dp", None, None),
            P("dp", None, None),
            P("dp", "seq", None),
            P(None, ("dp", "seq"), None),
        ),
        check_vma=False,
    )
```

```python
from functools import partial

import jax
import jax.numpy as jnp
from jax import lax
from jax.experimental import pallas as pl
from jax.experimental.pallas import tpu as pltpu
from jax.sharding import PartitionSpec as P

D = 768
H = 12
HEAD = 64
FF = 3072
PAIRS = H // 2
LANES = 2 * HEAD
QP = 112
VEC_ROW = 8 * D + 2 * FF
VECS = 24
TAIL = 256
HEAD_ROWS = 128
QUERY_HEAD = 64
SCALE = HEAD ** (-0.5)
EPS = 1e-05
NEG = -1e30
F32 = jnp.float32
BF16 = jnp.bfloat16
MIB = 1024 * 1024


def dot_nn(a, b):
    return lax.dot_general(a, b, (((1,), (0,)), ((), ())), preferred_element_type=F32)


def dot_nt(a, b):
    return lax.dot_general(a, b, (((1,), (1,)), ((), ())), preferred_element_type=F32)


def dot_tn(a, b):
    return lax.dot_general(a, b, (((0,), (0,)), ((), ())), preferred_element_type=F32)


def norm_parts(v):
    center = v - jnp.mean(v, axis=-1, keepdims=True)
    inverse = lax.rsqrt(jnp.mean(center * center, axis=-1, keepdims=True) + EPS)
    return center * inverse, inverse


def norm_back(dy, hat, inverse, gain):
    scaled = dy * gain
    mean_one = jnp.mean(scaled, axis=-1, keepdims=True)
    mean_two = jnp.mean(scaled * hat, axis=-1, keepdims=True)
    return inverse * (scaled - mean_one - hat * mean_two)


def rowsum(v):
    return jnp.sum(v.astype(F32), axis=0, keepdims=True)


def head_masks():
    lane = lax.broadcasted_iota(jnp.int32, (1, LANES), 1)
    first = jnp.where(lane < HEAD, 1.0, 0.0)
    return first.astype(BF16), (1.0 - first).astype(BF16)


def two_heads(block, masks):
    return jnp.concatenate([block * masks[0], block * masks[1]], axis=0)


def join_heads(stacked):
    lane = lax.broadcasted_iota(jnp.int32, (QP, LANES), 1)
    return jnp.where(lane < HEAD, stacked[:QP], stacked[QP:])


def weight_block(index):
    return pl.BlockSpec((D, D), lambda *_: (index, 0))


def whole(shape):
    return pl.BlockSpec(shape, lambda *_: (0,) * len(shape))


def params(mib):
    return pltpu.CompilerParams(vmem_limit_bytes=mib * MIB)


def cost(flops, moved):
    return pl.CostEstimate(flops=flops // 1000, bytes_accessed=moved // 1000, transcendentals=0)


FIRST_BLOCKS = (0, 1, 2, 5, 6, 3, 4)
SPREAD = ((0, 0, 0), (0, 0, 1), (0, 1, 0), (1, 0, 0), (0, 1, 1), (1, 1, 0), (1, 0, 1), (1, 1, 1))
PAIR_ROWS = 784
HOLDER = (3, 1, 1, 1)


class Assembly:
    def __init__(self, flags, bufs, weights, seams, sems, vec_low, vec_sem):
        self.core, self.x, self.y, self.z = flags[0], flags[1], flags[2], flags[3]
        self.bufs, self.weights, self.seams, self.sems = bufs, weights, seams, sems
        self.vec_low, self.vec_sem = vec_low, vec_sem
        self.ready = set()

    def buf(self, dc, dz2, spread):
        return self.bufs[dc * 16 + dz2 * 8 + SPREAD.index(spread)]

    def start_vec(self):
        first = VEC_ROW - 15 * PAIR_ROWS - 400
        for dc in (0, 1):
            for dz2 in (0, 1):
                for dz1, dy, dx in SPREAD:
                    here = (self.z ^ (2 * dz2 + dz1), self.y ^ dy, self.core ^ dc, self.x ^ dx)
                    hit = (here[0] == HOLDER[0]) & (here[1] == HOLDER[1]) & (here[2] == HOLDER[2]) & (here[3] == HOLDER[3])

                    @pl.when(hit)
                    def _(source=self.buf(dc, dz2, (dz1, dy, dx))):
                        pltpu.make_async_copy(source.at[pl.ds(first, 32)], self.vec_low, self.vec_sem).start()

    def wait_vec(self):
        pltpu.make_async_copy(self.weights.at[pl.ds(0, 32)], self.vec_low, self.vec_sem).wait()

    def start_group(self, dz2):
        def rows(start, count):
            return pl.ds(pl.multiple_of(start, 16), count)

        for dz1 in (0, 1):
            for dy in (0, 1):
                for dc in (0, 1):
                    pair = (self.z ^ (2 * dz2 + dz1)) * 4 + (self.y ^ dy) * 2 + (self.core ^ dc)
                    base, sem = pair * PAIR_ROWS, self.sems.at[pair]
                    near, far = self.buf(dc, dz2, (dz1, dy, 0)), self.buf(dc, dz2, (dz1, dy, 1))
                    for source, x in ((near, self.x), (far, 1 - self.x)):
                        target = self.weights.at[rows(base + 400 * x, 384)]
                        pltpu.make_async_copy(source.at[pl.ds(0, 384)], target, sem).start()
                        pltpu.make_async_copy(source.at[pl.ds(384, 16)], self.seams.at[pair, x], sem).start()

    def start(self):
        self.start_vec()
        for low in (True, False):

            @pl.when((self.z < 2) == low)
            def _(low=low):
                for dz2 in (0, 1) if low else (1, 0):
                    self.start_group(dz2)

    def wait(self, pair):
        if pair not in self.ready:
            self.ready.add(pair)
            rows = self.weights.at[pl.ds(0, PAIR_ROWS + 16)]
            pltpu.make_async_copy(rows, rows, self.sems.at[pair]).wait()
            halves = [self.seams[pair, x].astype(F32)[:8] for x in (0, 1)]
            seam = pl.ds(pair * PAIR_ROWS + 384, 16)
            self.weights[seam, :] = jnp.concatenate(halves, axis=0).astype(BF16)

    def block(self, number):
        for pair in range(number * D // PAIR_ROWS, (number * D + D - 1) // PAIR_ROWS + 1):
            self.wait(pair)


class Direct:
    def __init__(self, w_hbm, weights, sems, vec_low, vec_sem):
        self.copies = {}
        for number in FIRST_BLOCKS:
            rows = pl.ds(number * D, D)
            self.copies[number] = pltpu.make_async_copy(w_hbm.at[rows], weights.at[rows], sems.at[number])
        self.vec = pltpu.make_async_copy(w_hbm.at[pl.ds(VEC_ROW, 32)], vec_low, vec_sem)
        self.ready = set()

    def start(self):
        self.vec.start()
        for number in FIRST_BLOCKS:
            self.copies[number].start()

    def wait_vec(self):
        self.vec.wait()

    def block(self, number):
        if number not in self.ready:
            self.ready.add(number)
            self.copies[number].wait()


def forward_kernel(queries, custom, left_ref, flags, xb_ref, m_hbm, *refs):
    count = 32 if custom else 1
    bufs, refs = refs[:count], refs[count:]
    qs_out, ks_out, vs_out, os_out, y1_out, qc_out, k_out, v_out, o_out, stat_ref = refs[:10]
    w_out = refs[10] if custom else None
    weights, m_ref, qs_ref, ks_ref, vs_ref, os_ref, y1_ref, qc_ref, k_ref, v_ref, o_ref, vec_low = refs[10 + custom : 22 + custom]
    seams, w_sems, m_sems, out_sems, kv_sems, vec_sem, all_sems = refs[22 + custom :]
    images = m_ref.shape[0]
    tokens = m_ref.shape[1]
    if custom:
        feed = Assembly(flags, bufs, weights, seams, w_sems, vec_low, vec_sem)
    else:
        feed = Direct(bufs[0], weights, w_sems, vec_low, vec_sem)

    def load_memory(image):
        return pltpu.make_async_copy(m_hbm.at[image], m_ref.at[image], m_sems.at[image])

    def matrix(block):
        feed.block(block)
        return weights[block * D : (block + 1) * D, :]

    def leave_weights(half):
        rows = pl.ds(half * 8 * PAIR_ROWS, 8 * PAIR_ROWS)
        return pltpu.make_async_copy(weights.at[rows], w_out.at[rows], all_sems.at[half])

    small = [(qs_ref, qs_out), (ks_ref, ks_out), (vs_ref, vs_out), (os_ref, os_out), (y1_ref, y1_out), (qc_ref, qc_out)]

    def leave(number):
        return pltpu.make_async_copy(*small[number], out_sems.at[number])

    def leave_image(image, number):
        source, target = [(k_ref, k_out), (v_ref, v_out), (o_ref, o_out)][number]
        return pltpu.make_async_copy(source.at[image], target.at[image], kv_sems.at[image, number])

    feed.start()
    for image in range(images):
        load_memory(image).start()
    feed.wait_vec()
    vec = vec_low[...].astype(F32)
    xb = xb_ref[...]
    qs_ref[...] = ((dot_nn(xb, matrix(0)) + vec[0:1, :]) * SCALE).astype(BF16)
    leave(0).start()
    ks_ref[...] = dot_nn(xb, matrix(1)).astype(BF16)
    leave(1).start()
    vs_ref[...] = (dot_nn(xb, matrix(2)) + vec[1:2, :]).astype(BF16)
    leave(2).start()
    masks = head_masks()
    real = lax.broadcasted_iota(jnp.int32, (2 * QP, QP), 1) < queries
    places = [(slice(i * QP, (i + 1) * QP), slice(p * LANES, (p + 1) * LANES)) for i in range(images) for p in range(PAIRS)]

    def raw_self(place):
        return dot_nt(two_heads(qs_ref[place], masks), ks_ref[place])

    following = raw_self(places[0])
    for number, place in enumerate(places):
        scores = following
        if number + 1 < len(places):
            following = raw_self(places[number + 1])
        scores = jnp.where(real, scores, NEG)
        probs = jnp.exp(scores - jnp.max(scores, axis=-1, keepdims=True))
        probs = probs / jnp.sum(probs, axis=-1, keepdims=True)
        os_ref[place] = join_heads(dot_nn(probs.astype(BF16), vs_ref[place])).astype(BF16)
    leave(3).start()
    y1 = xb.astype(F32) + (dot_nn(os_ref[...], matrix(3)) + vec[2:3, :])
    y1_ref[...] = y1
    leave(4).start()
    hat, _ = norm_parts(y1)
    x1 = hat * vec[11:12, :] + vec[12:13, :]
    qc_ref[...] = ((dot_nn(x1.astype(BF16), matrix(4)) + vec[3:4, :]) * SCALE).astype(BF16)
    leave(5).start()

    feed.block(5)
    feed.block(6)
    if custom:
        for pair in range(8):
            feed.wait(pair)
        leave_weights(0).start()
    column = lax.broadcasted_iota(jnp.int32, (2 * QP, 128), 1)
    for image in range(images):
        load_memory(image).wait()
        rows = slice(image * QP, (image + 1) * QP)
        k_ref[image] = dot_nn(m_ref[image], matrix(5)).astype(BF16)
        v_ref[image] = (dot_nn(m_ref[image], matrix(6)) + vec[4:5, :]).astype(BF16)
        leave_image(image, 0).start()
        leave_image(image, 1).start()
        valid = lax.broadcasted_iota(jnp.int32, (2 * QP, tokens), 1) < left_ref[image]
        stat = jnp.zeros((2 * QP, 128), F32)
        def raw(pair):
            lanes = slice(pair * LANES, (pair + 1) * LANES)
            return dot_nt(two_heads(qc_ref[rows, lanes], masks), k_ref[image, :, lanes])

        following = raw(0)
        for pair in range(PAIRS):
            lanes = slice(pair * LANES, (pair + 1) * LANES)
            scores = following
            if pair + 1 < PAIRS:
                following = raw(pair + 1)
            scores = jnp.where(valid, scores, NEG)
            top = jnp.max(scores, axis=-1, keepdims=True)
            probs = jnp.exp(scores - top)
            total = jnp.sum(probs, axis=-1, keepdims=True)
            mixed = dot_nn(probs.astype(BF16), v_ref[image, :, lanes]) / total
            o_ref[image, :, lanes] = join_heads(mixed).astype(BF16)
            stat = jnp.where(column == pair, top + jnp.log(total), stat)
        stat_ref[image] = jnp.where(left_ref[image] > 0, stat.T[:8], NEG)
        leave_image(image, 2).start()
        if custom and image == 0:
            for pair in range(8, 16):
                feed.wait(pair)
            leave_weights(1).start()
    for number in range(len(small)):
        leave(number).wait()
    for image in range(images):
        for number in range(3):
            leave_image(image, number).wait()
    if custom:
        leave_weights(0).wait()
        leave_weights(1).wait()


def forward(left, flags, xb, memory, bufs, queries):
    custom = len(bufs) > 1
    rows = xb.shape[0]
    images, tokens, _ = memory.shape
    narrow = jax.ShapeDtypeStruct((rows, D), BF16)
    tall = jax.ShapeDtypeStruct(memory.shape, BF16)
    anywhere = pl.BlockSpec(memory_space=pl.ANY)
    small = pltpu.VMEM((rows, D), BF16)
    large = pltpu.VMEM(memory.shape, BF16)
    held = 16 * PAIR_ROWS if custom else 7 * D
    return pl.pallas_call(
        partial(forward_kernel, queries, custom),
        grid_spec=pltpu.PrefetchScalarGridSpec(
            num_scalar_prefetch=2,
            grid=(1,),
            in_specs=[whole((rows, D)), anywhere] + [anywhere] * len(bufs),
            out_specs=[anywhere] * 9 + [whole((images, 8, 2 * QP))] + [anywhere] * custom,
            scratch_shapes=[
                pltpu.VMEM((held, D), BF16),
                large, small, small, small, small,
                pltpu.VMEM((rows, D), F32),
                small, large, large,
                pltpu.VMEM((images, QP, D), BF16),
                pltpu.VMEM((32, D), BF16),
                pltpu.VMEM((16, 2, 16, D), BF16),
                pltpu.SemaphoreType.DMA((16,)),
                pltpu.SemaphoreType.DMA((images,)),
                pltpu.SemaphoreType.DMA((6,)),
                pltpu.SemaphoreType.DMA((images, 3)),
                pltpu.SemaphoreType.DMA(()),
                pltpu.SemaphoreType.DMA((2,)),
            ],
        ),
        out_shape=[
            narrow, narrow, narrow, narrow,
            jax.ShapeDtypeStruct((rows, D), F32),
            narrow, tall, tall,
            jax.ShapeDtypeStruct((images, QP, D), BF16),
            jax.ShapeDtypeStruct((images, 8, 2 * QP), F32),
        ]
        + [jax.ShapeDtypeStruct((held, D), BF16)] * custom,
        cost_estimate=cost(0, 0),
        compiler_params=params(60),
        name="forward",
    )(left, flags, xb, memory, *bufs)


def pieces(start, count, size):
    found = []
    done = 0
    while done < count:
        pair, offset = divmod(start + done, size)
        length = min(count - done, size - offset)
        found.append((done, pair, offset, length))
        done += length
    return found


class Halves:
    def __init__(self, keep, send, my_core):
        self.keep, self.send, self.my_core = keep, send, my_core

    def copy(self, target, source, pair, offset, length, sem):
        place = pair // self.cores()
        index = []
        for extent in reversed(target.shape[:-2]):
            index.insert(0, place % extent)
            place = place // extent
        return pltpu.make_async_copy(source, target.at[(*index, pl.ds(offset, length))], sem)

    def cores(self):
        return 1 if self.send is None else 2

    def start(self, source, pair, offset, length, sem):
        if self.send is None:
            self.copy(self.keep, source, pair, offset, length, sem).start()
            return

        @pl.when(self.my_core == pair % 2)
        def _():
            self.copy(self.keep, source, pair, offset, length, sem).start()

        @pl.when(self.my_core != pair % 2)
        def _():
            self.copy(self.send, source, pair, offset, length, sem).start()

    def wait(self, source, pair, offset, length, sem):
        self.copy(self.keep, source, pair, offset, length, sem).wait()


def middle_kernel(parts, split, *refs):
    flags, y1_ref = refs[:2]
    o_refs, stat_refs = refs[2 : 2 + parts], refs[2 + parts : 2 + 2 * parts]
    refs = refs[2 + 2 * parts :]
    w_hbm, vec, cot_ref, match_ref, out_hbm = refs[:5]
    halves = Halves(refs[5], refs[6] if split else None, flags[0])
    refs = refs[6 + split :]
    cross_halves = Halves(refs[0], refs[1] if split else None, flags[0])
    refs = refs[1 + split :]
    db_ref, doc_ref, tot_ref, dvec_ref = refs[:4]
    ocf, ocb, y2, x2b, u, slope, acc, e3b, staged, blank, out_ref, dco_ref, co, feed = refs[4:18]
    sems, blank_sem, out_sem, side_sems, w_sems = refs[18:]
    phase, step = pl.program_id(0), pl.program_id(1)
    steps = FF // D
    images = match_ref.shape[0]
    column = lax.broadcasted_iota(jnp.int32, (2 * QP, 128), 1)
    lane = lax.broadcasted_iota(jnp.int32, (QP, LANES), 1)
    size = halves.keep.shape[-2]
    side = cross_halves.keep.shape[-2]

    def load(block):
        target = co if block == 7 else feed.at[block - 8]
        return pltpu.make_async_copy(w_hbm.at[pl.ds(block * D, D)], target, w_sems.at[block - 7])

    def leave_out():
        return pltpu.make_async_copy(out_ref, out_hbm, out_sem)

    def leave_side(act):
        starts = [(dco_ref, 3 * D - QUERY_HEAD, D), (staged.at[0, 0], 4 * D - QUERY_HEAD, HEAD_ROWS)]
        for which, (source, start, count) in enumerate(starts):
            if (which == 0) != (act[0] == "o"):
                continue
            for number, (done, pair, offset, length) in enumerate(pieces(start, count, side)):
                piece = source.at[pl.ds(done, length)]
                getattr(cross_halves, act[1])(piece, pair, offset, length, side_sems.at[which, number])

    def leave(which, at, act):
        skip = HEAD_ROWS if which + at == 0 else 0
        start = which * FF + at * D + skip - HEAD_ROWS
        for number, (done, pair, offset, length) in enumerate(pieces(start, D - skip, size)):
            source = staged.at[at % 2, which, pl.ds(done + skip, length)]
            getattr(halves, act)(source, pair, offset, length, sems.at[at, which, number])

    def leave_blank(act):
        for _, pair, offset, length in pieces(2 * FF - HEAD_ROWS, TAIL, size):
            getattr(halves, act)(blank, pair, offset, length, blank_sem)

    def ordered(first, second):
        if parts != 2:
            return first, second
        swap = flags[1] != 0
        return jnp.where(swap, second, first), jnp.where(swap, first, second)

    @pl.when((phase == 0) & (step == 0))
    def _():
        load(7).start()
        for at in range(steps):
            load(8 + at).start()
            load(8 + steps + at).start()
        for image in range(images):
            rows = slice(image * QP, (image + 1) * QP)
            stats = [ref[image] for ref in stat_refs]
            if parts == 2:
                stats = ordered(*stats)
            top = stats[0]
            for n in range(1, parts):
                top = jnp.maximum(top, stats[n])
            mass = [jnp.exp(stats[n] - top) for n in range(parts)]
            total = mass[0]
            for n in range(1, parts):
                total = total + mass[n]
            tot_ref[image, 0:8, :] = top + jnp.log(total)
            shares = [jnp.concatenate([m / total, jnp.zeros((120, 2 * QP), F32)], axis=0).T for m in mass]
            for pair in range(PAIRS):
                lanes = slice(pair * LANES, (pair + 1) * LANES)
                values = [ref[image, :, lanes].astype(F32) for ref in o_refs]
                if parts == 2:
                    values = ordered(*values)
                mixed = jnp.zeros((QP, LANES), F32)
                for n in range(parts):
                    share = shares[n][:, pair : pair + 1]
                    mixed = mixed + values[n] * jnp.where(lane < HEAD, share[:QP], share[QP:])
                ocf[rows, lanes] = mixed
        ocb[...] = ocf[...].astype(BF16)
        hat, _ = norm_parts(y1_ref[...])
        x1 = hat * vec[11:12, :] + vec[12:13, :]
        load(7).wait()
        total = x1 + (dot_nn(ocb[...], co[...]) + vec[5:6, :])
        y2[...] = total
        hat, _ = norm_parts(total)
        x2 = hat * vec[13:14, :] + vec[14:15, :]
        x2b[...] = x2.astype(BF16)
        acc[...] = x2 + vec[6:7, :]

    for at in range(steps):

        @pl.when((phase == 0) & (step == at))
        def _(at=at):
            load(8 + at).wait()
            load(8 + steps + at).wait()

    f1, f2 = feed.at[step], feed.at[steps + step]

    @pl.when(phase == 0)
    def _():
        h = dot_nt(x2b[...], f1[...]) + vec[pl.ds(7 + step, 1), :]
        root = 0.7978845608028654
        square = h * h
        t = jnp.tanh(root * (h + 0.044715 * (h * square)))
        half = 0.5 * (1.0 + t)
        slope[step] = half + (0.5 * root) * h * (1.0 - t * t) * (1.0 + 0.134145 * square)
        active = (h * half).astype(BF16)
        u[step] = active
        acc[...] += dot_nn(active, f2[...])

    @pl.when((phase == 1) & (step == 0))
    def _():
        blank[...] = jnp.zeros_like(blank)
        leave_blank("start")
        dvec_ref[...] = jnp.zeros_like(dvec_ref)
        hat, inverse = norm_parts(acc[...])
        out = hat * vec[15:16, :] + vec[16:17, :]
        grads = []
        for image in range(images):
            out_ref[image] = out[image * QP : (image + 1) * QP]
            matched = match_ref[image]
            hit = lax.broadcasted_iota(jnp.int32, (QP, matched.shape[1]), 0) == matched
            grads.append(dot_nn(jnp.where(hit, 1.0, 0.0).astype(BF16), cot_ref[image]))
        leave_out().start()
        dy = jnp.concatenate(grads, axis=0)
        dvec_ref[15:16, :] = rowsum(dy * hat)
        dvec_ref[16:17, :] = rowsum(dy)
        dc = norm_back(dy, hat, inverse, vec[15:16, :])
        low = dc.astype(BF16)
        e3b[...] = low
        dvec_ref[6:7, :] = rowsum(low)
        acc[...] = dc

    for at in range(2, steps):

        @pl.when((phase == 1) & (step == at))
        def _(at=at):
            leave(0, at - 2, "wait")
            leave(1, at - 2, "wait")
            if at == 2:
                leave_side(("f", "wait"))

    @pl.when(phase == 1)
    def _():
        du = dot_nt(e3b[...], f2[...])
        dh = (du * slope[step]).astype(BF16)
        slot = lax.rem(step, 2)
        staged[slot, 1] = dot_tn(u[step], e3b[...]).astype(BF16)
        staged[slot, 0] = dot_tn(dh, x2b[...]).astype(BF16)

        @pl.when(step == 0)
        def _():
            leave_side(("f", "start"))

        for at in range(steps):

            @pl.when(step == at)
            def _(at=at):
                leave(0, at, "start")
                leave(1, at, "start")

        dvec_ref[pl.ds(7 + step, 1), :] = rowsum(dh)
        acc[...] += dot_nn(dh, f1[...])

    @pl.when((phase == 1) & (step == steps - 1))
    def _():
        hat, inverse = norm_parts(y2[...])
        dy = acc[...]
        dvec_ref[13:14, :] = rowsum(dy * hat)
        dvec_ref[14:15, :] = rowsum(dy)
        db = norm_back(dy, hat, inverse, vec[13:14, :])
        db_ref[...] = db
        low = db.astype(BF16)
        dvec_ref[5:6, :] = rowsum(low)
        dco_ref[...] = dot_tn(ocb[...], low).astype(BF16)
        leave_side(("o", "start"))
        doc = dot_nt(low, co[...]).astype(BF16)
        doc_ref[...] = doc
        both = doc.astype(F32) * ocf[...]
        for image in range(images):
            rows = slice(image * QP, (image + 1) * QP)
            tot = jnp.zeros((2 * QP, 128), F32)
            for pair in range(PAIRS):
                piece = both[rows, pair * LANES : (pair + 1) * LANES]
                one = jnp.sum(jnp.where(lane < HEAD, piece, 0.0), axis=-1, keepdims=True)
                two = jnp.sum(jnp.where(lane < HEAD, 0.0, piece), axis=-1, keepdims=True)
                tot = jnp.where(column == pair, jnp.concatenate([one, two], axis=0), tot)
            tot_ref[image, 8:16, :] = tot.T[:8]
        leave_blank("wait")
        leave_out().wait()
        leave_side(("o", "wait"))
        for which in (0, 1):
            leave(which, steps - 2, "wait")
            leave(which, steps - 1, "wait")


def halves_shape(shape, split):
    return [jax.ShapeDtypeStruct(shape, BF16)] * (1 + split)


def middle(flags, y1, o_parts, stat_parts, w, vec, cot, matched, far_shape, cross_shape, split):
    rows = y1.shape[0]
    images = cot.shape[0]
    steps = FF // D
    parts = len(o_parts)
    anywhere = pl.BlockSpec(memory_space=pl.ANY)
    return pl.pallas_call(
        partial(middle_kernel, parts, split),
        grid_spec=pltpu.PrefetchScalarGridSpec(
            num_scalar_prefetch=1,
            grid=(2, steps),
            in_specs=[whole(y1.shape)]
            + [whole(o_parts[0].shape)] * parts
            + [whole(stat_parts[0].shape)] * parts
            + [anywhere, whole((VECS, D)), whole(cot.shape), whole((images, 1, matched.shape[1]))],
            out_specs=[anywhere] * (3 + 2 * split)
            + [
                whole((rows, D)),
                whole((rows, D)),
                whole((images, 16, 2 * QP)),
                whole((VECS, D)),
            ],
            scratch_shapes=[
                pltpu.VMEM((rows, D), F32),
                pltpu.VMEM((rows, D), BF16),
                pltpu.VMEM((rows, D), F32),
                pltpu.VMEM((rows, D), BF16),
                pltpu.VMEM((steps, rows, D), BF16),
                pltpu.VMEM((steps, rows, D), F32),
                pltpu.VMEM((rows, D), F32),
                pltpu.VMEM((rows, D), BF16),
                pltpu.VMEM((2, 2, D, D), BF16),
                pltpu.VMEM((TAIL, D), BF16),
                pltpu.VMEM((images, QP, D), F32),
                pltpu.VMEM((D, D), BF16),
                pltpu.VMEM((D, D), BF16),
                pltpu.VMEM((2 * steps, D, D), BF16),
                pltpu.SemaphoreType.DMA((steps, 2, 2)),
                pltpu.SemaphoreType.DMA(()),
                pltpu.SemaphoreType.DMA(()),
                pltpu.SemaphoreType.DMA((2, 2)),
                pltpu.SemaphoreType.DMA((1 + 2 * steps,)),
            ],
        ),
        out_shape=[jax.ShapeDtypeStruct((images, QP, D), F32)]
        + halves_shape(far_shape, split)
        + halves_shape(cross_shape, split)
        + [
            jax.ShapeDtypeStruct((rows, D), F32),
            jax.ShapeDtypeStruct((rows, D), BF16),
            jax.ShapeDtypeStruct((images, 16, 2 * QP), F32),
            jax.ShapeDtypeStruct((VECS, D), F32),
        ],
        cost_estimate=cost(2 * rows * D * (6 * FF + 3 * D), 2 * FF * D * 6),
        compiler_params=params(60),
        name="middle",
    )(flags, y1, *o_parts, *stat_parts, w, vec, cot, matched[:, None, :])


def cross_backward_kernel(left_ref, q_ref, k_ref, v_ref, do_ref, tot_ref, dq_ref, dk_ref, dv_ref):
    tokens = k_ref.shape[1]
    masks = head_masks()
    valid = lax.broadcasted_iota(jnp.int32, (tokens, 2 * QP), 0) < left_ref[pl.program_id(0)]
    def raw(pair):
        lanes = slice(pair * LANES, (pair + 1) * LANES)
        query = two_heads(q_ref[0, :, lanes], masks)
        dout = two_heads(do_ref[0, :, lanes], masks)
        return query, dout, dot_nt(k_ref[0, :, lanes], query), dot_nt(v_ref[0, :, lanes], dout)

    following = raw(0)
    for pair in range(PAIRS):
        lanes = slice(pair * LANES, (pair + 1) * LANES)
        query, dout, scores, dprobs = following
        if pair + 1 < PAIRS:
            following = raw(pair + 1)
        probs = jnp.where(valid, jnp.exp(scores - tot_ref[0, pair : pair + 1, :]), 0.0)
        dscores = (probs * (dprobs - tot_ref[0, 8 + pair : 9 + pair, :])).astype(BF16)
        dv_ref[0, :, lanes] = dot_nn(probs.astype(BF16), dout).astype(BF16)
        dk_ref[0, :, lanes] = dot_nn(dscores, query).astype(BF16)
        dq_ref[0, :, lanes] = join_heads(dot_tn(k_ref[0, :, lanes], dscores).T).astype(BF16)


def cross_backward(left, qc, key, value, doc, tot):
    images, tokens, _ = key.shape
    q_block = pl.BlockSpec((1, QP, D), lambda i, _: (i, 0, 0))
    m_block = pl.BlockSpec((1, tokens, D), lambda i, _: (i, 0, 0))
    s_block = pl.BlockSpec((1, 16, 2 * QP), lambda i, _: (i, 0, 0))
    return pl.pallas_call(
        cross_backward_kernel,
        grid_spec=pltpu.PrefetchScalarGridSpec(
            num_scalar_prefetch=1,
            grid=(images,),
            in_specs=[q_block, m_block, m_block, q_block, s_block],
            out_specs=[q_block, m_block, m_block],
        ),
        out_shape=[
            jax.ShapeDtypeStruct((images, QP, D), BF16),
            jax.ShapeDtypeStruct(key.shape, BF16),
            jax.ShapeDtypeStruct(key.shape, BF16),
        ],
        cost_estimate=cost(4 * images * 2 * QP * tokens * D // 3, images * tokens * D * 8),
        compiler_params=params(60),
        name="cross_backward",
    )(left, qc.reshape(images, QP, D), key, value, doc.reshape(images, QP, D), tot)


def memory_weights_kernel(split, flags, *refs):
    m_ref, dk_ref, dv_ref = refs[1 + split : 4 + split]
    refs = refs[4 + split :]
    gb_ref = refs[0]
    halves = Halves(refs[1], refs[2] if split else None, flags[0])
    low, sems = refs[2 + split :]
    def leave(which, act):
        start = (1 + which) * D - QUERY_HEAD
        for number, (done, pair, offset, length) in enumerate(pieces(start, D, halves.keep.shape[-2])):
            piece = low.at[which, pl.ds(done, length)]
            getattr(halves, act)(piece, pair, offset, length, sems.at[which, number])

    tall = m_ref[...].reshape(-1, D)
    for which, ref in ((0, dk_ref), (1, dv_ref)):
        low[which] = dot_tn(tall, ref[...].reshape(-1, D)).astype(BF16)
        leave(which, "start")
    gb_ref[...] = jnp.broadcast_to(rowsum(dv_ref[...].reshape(-1, D)), gb_ref.shape)
    for which in (0, 1):
        leave(which, "wait")


def memory_weights(flags, cross, memory, dk, dv, split):
    images, tokens, _ = memory.shape
    block = whole(memory.shape)
    anywhere = pl.BlockSpec(memory_space=pl.ANY)
    return pl.pallas_call(
        partial(memory_weights_kernel, split),
        grid_spec=pltpu.PrefetchScalarGridSpec(
            num_scalar_prefetch=1,
            grid=(1,),
            in_specs=[anywhere] * (1 + split) + [block, block, block],
            out_specs=[whole((8, D))] + [anywhere] * (1 + split),
            scratch_shapes=[
                pltpu.VMEM((2, D, D), BF16),
                pltpu.SemaphoreType.DMA((2, 2)),
            ],
        ),
        out_shape=[jax.ShapeDtypeStruct((8, D), F32)] + halves_shape(cross[0].shape, split),
        input_output_aliases={1 + n: 1 + n for n in range(1 + split)},
        cost_estimate=cost(4 * images * tokens * D * D, images * tokens * D * 6),
        compiler_params=params(60),
        name="memory_weights",
    )(flags, *cross, memory, dk, dv)


def memory_grads_kernel(dk_ref, dv_ref, ck, cv, gm_ref):
    gm_ref[0] = dot_nt(dk_ref[0], ck[...]) + dot_nt(dv_ref[0], cv[...])


def memory_grads(dk, dv, w):
    images, tokens, _ = dk.shape
    block = pl.BlockSpec((1, tokens, D), lambda i: (i, 0, 0))
    return pl.pallas_call(
        memory_grads_kernel,
        grid=(images,),
        in_specs=[block, block, weight_block(5), weight_block(6)],
        out_specs=block,
        out_shape=jax.ShapeDtypeStruct(dk.shape, F32),
        cost_estimate=pl.CostEstimate(
            flops=4 * images * tokens * D * D, bytes_accessed=images * tokens * D * 8, transcendentals=0
        ),
        compiler_params=params(60),
        name="memory_grads",
    )(dk, dv, w, w)


class Loads:
    def __init__(self, pairs, sems):
        self.copies = [(pltpu.make_async_copy(source, target, sems.at[n]), target) for n, (source, target) in enumerate(pairs)]
        self.ready = set()
        for copy, _ in self.copies:
            copy.start()

    def __call__(self, number):
        copy, target = self.copies[number]
        if number not in self.ready:
            copy.wait()
            self.ready.add(number)
        return target[...]


def query_backward_kernel(parts, split, flags, *refs):
    sources, vec = refs[1 + split : 4 + split + parts], refs[4 + split + parts]
    refs = refs[5 + split + parts :]
    da_ref, gq_head_ref, dvec_ref = refs[:3]
    halves = Halves(refs[3], refs[4] if split else None, flags[0])
    refs = refs[4 + split :]
    targets, staged, load_sems, sems = refs[: 3 + parts], refs[3 + parts], refs[4 + parts], refs[5 + parts]
    w_hbm = sources[-1]
    sources = [*sources[:-1], w_hbm.at[pl.ds(4 * D, D)]]
    get = Loads(list(zip(sources, targets)), load_sems)

    def leave(act):
        for number, (done, pair, offset, length) in enumerate(pieces(0, D - QUERY_HEAD, halves.keep.shape[-2])):
            piece = staged.at[pl.ds(done + QUERY_HEAD, length)]
            getattr(halves, act)(piece, pair, offset, length, sems.at[number])

    total = get(0).astype(F32)
    for number in range(1, parts):
        total = total + get(number).astype(F32)
    dq = total.astype(BF16) * SCALE
    hat, inverse = norm_parts(get(parts))
    gain = vec[11:12, :]
    x1b = (hat * gain + vec[12:13, :]).astype(BF16)
    gcq = dot_tn(x1b, dq).astype(BF16)
    staged[...] = gcq
    leave("start")
    gq_head_ref[...] = gcq[:QUERY_HEAD]
    dvec_ref[...] = jnp.zeros_like(dvec_ref)
    dvec_ref[3:4, :] = rowsum(dq)
    dy = get(parts + 1) + dot_nt(dq, get(parts + 2))
    dvec_ref[11:12, :] = rowsum(dy * hat)
    dvec_ref[12:13, :] = rowsum(dy)
    da = norm_back(dy, hat, inverse, gain)
    da_ref[...] = da
    dvec_ref[2:3, :] = rowsum(da.astype(BF16))
    leave("wait")


def query_backward(flags, cross, y1, db, dq_parts, w, vec, split):
    rows = y1.shape[0]
    parts = len(dq_parts)
    full = whole((rows, D))
    anywhere = pl.BlockSpec(memory_space=pl.ANY)
    return pl.pallas_call(
        partial(query_backward_kernel, parts, split),
        grid_spec=pltpu.PrefetchScalarGridSpec(
            num_scalar_prefetch=1,
            grid=(1,),
            in_specs=[anywhere] * (4 + split + parts) + [whole((VECS, D))],
            out_specs=[full, whole((QUERY_HEAD, D)), whole((VECS, D))] + [anywhere] * (1 + split),
            scratch_shapes=[pltpu.VMEM((rows, D), BF16)] * parts
            + [pltpu.VMEM((rows, D), F32)] * 2
            + [pltpu.VMEM((D, D), BF16)] * 2
            + [pltpu.SemaphoreType.DMA((parts + 3,)), pltpu.SemaphoreType.DMA((2,))],
        ),
        out_shape=[
            jax.ShapeDtypeStruct((rows, D), F32),
            jax.ShapeDtypeStruct((QUERY_HEAD, D), BF16),
            jax.ShapeDtypeStruct((VECS, D), F32),
        ]
        + halves_shape(cross[0].shape, split),
        input_output_aliases={1 + n: 3 + n for n in range(1 + split)},
        cost_estimate=cost(4 * rows * D * D, rows * D * 16),
        compiler_params=params(60),
        name="query_backward",
    )(flags, *cross, *[part.reshape(rows, D) for part in dq_parts], y1, db, w, vec)


def self_backward_kernel(queries, split, *refs):
    flags, os_hbm, da_hbm, qs_hbm, ks_hbm, vs_hbm, x_hbm, w_hbm, gq_ref, gx_ref, dvec_ref, keep_ref = refs[:12]
    halves = Halves(keep_ref, refs[12] if split else None, flags[0])
    sq, sk, sv, g_ref, os_ref, da_ref, ao, qs, ks, vs, x_ref, aq, ak, av, sems, load_sems = refs[12 + split :]
    size = keep_ref.shape[-2]
    matrices = [w_hbm.at[pl.ds(block * D, D)] for block in range(4)]
    get = Loads(
        [(os_hbm, os_ref), (da_hbm, da_ref), (matrices[3], ao), (qs_hbm, qs), (ks_hbm, ks), (vs_hbm, vs)]
        + [(x_hbm, x_ref), (matrices[0], aq), (matrices[1], ak), (matrices[2], av)],
        load_sems,
    )

    def leave(pair, act):
        getattr(halves, act)(g_ref.at[pl.ds(pair * size, size)], pair, 0, size, sems.at[pair])

    pairs = g_ref.shape[0] // size
    images = x_ref.shape[0] // QP
    dvec_ref[...] = jnp.zeros_like(dvec_ref)
    os = get(0)
    da = get(1)
    low = da.astype(BF16)
    g_ref[4 * D :, :] = gq_ref[...]
    g_ref[3 * D : 4 * D, :] = dot_tn(os, low).astype(BF16)
    dos = dot_nt(low, get(2)).astype(BF16)
    for number in (3, 4, 5):
        get(number)
    masks = head_masks()
    real = lax.broadcasted_iota(jnp.int32, (QP, 2 * QP), 0) < queries
    places = [(slice(i * QP, (i + 1) * QP), slice(p * LANES, (p + 1) * LANES)) for i in range(images) for p in range(PAIRS)]

    def raw(place):
        query = two_heads(qs[place], masks)
        dout = two_heads(dos[place], masks)
        return query, dout, dot_nt(ks[place], query), dot_nt(vs[place], dout)

    following = raw(places[0])
    for number, place in enumerate(places):
        query, dout, scores, dprobs = following
        if number + 1 < len(places):
            following = raw(places[number + 1])
        scores = jnp.where(real, scores, NEG)
        probs = jnp.exp(scores - jnp.max(scores, axis=0, keepdims=True))
        probs = probs / jnp.sum(probs, axis=0, keepdims=True)
        dscores = (probs * (dprobs - jnp.sum(probs * dprobs, axis=0, keepdims=True))).astype(BF16)
        sv[place] = dot_nn(probs.astype(BF16), dout).astype(BF16)
        sk[place] = dot_nn(dscores, query).astype(BF16)
        sq[place] = join_heads(dot_tn(ks[place], dscores).T).astype(BF16) * SCALE
    dvec_ref[0:1, :] = rowsum(sq[...])
    dvec_ref[1:2, :] = rowsum(sv[...])
    xb = get(6)
    g_ref[2 * D : 3 * D, :] = dot_tn(xb, sv[...]).astype(BF16)
    for pair in range(2, pairs):
        leave(pair, "start")
    g_ref[D : 2 * D, :] = dot_tn(xb, sk[...]).astype(BF16)
    for pair in range(1, min(2, pairs)):
        leave(pair, "start")
    g_ref[0:D, :] = dot_tn(xb, sq[...]).astype(BF16)
    leave(0, "start")
    gx = da + dot_nt(sq[...], get(7)) + dot_nt(sk[...], get(8)) + dot_nt(sv[...], get(9))
    for image in range(images):
        gx_ref[image] = gx[image * QP : (image + 1) * QP]
    for pair in range(pairs):
        leave(pair, "wait")


def self_backward(flags, xb, qs, ks, vs, os, da, gq_head, w, queries, shape, split):
    rows = xb.shape[0]
    images = rows // QP
    anywhere = pl.BlockSpec(memory_space=pl.ANY)
    return pl.pallas_call(
        partial(self_backward_kernel, queries, split),
        grid_spec=pltpu.PrefetchScalarGridSpec(
            num_scalar_prefetch=1,
            grid=(1,),
            in_specs=[anywhere] * 7 + [whole((QUERY_HEAD, D))],
            out_specs=[whole((images, QP, D)), whole((VECS, D))] + [anywhere] * (1 + split),
            scratch_shapes=[pltpu.VMEM((rows, D), BF16)] * 3
            + [pltpu.VMEM((4 * D + QUERY_HEAD, D), BF16), pltpu.VMEM((rows, D), BF16), pltpu.VMEM((rows, D), F32)]
            + [pltpu.VMEM((D, D), BF16)]
            + [pltpu.VMEM((rows, D), BF16)] * 4
            + [pltpu.VMEM((D, D), BF16)] * 3
            + [pltpu.SemaphoreType.DMA((4,)), pltpu.SemaphoreType.DMA((10,))],
        ),
        out_shape=[
            jax.ShapeDtypeStruct((images, QP, D), F32),
            jax.ShapeDtypeStruct((VECS, D), F32),
        ]
        + halves_shape(shape, split),
        cost_estimate=cost(16 * rows * D * D * 2, 8 * D * D * 2),
        compiler_params=params(60),
        name="self_backward",
    )(flags, os, da, qs, ks, vs, xb, w, gq_head)


class Place:
    def __init__(self):
        place = lax.axis_index("dp")
        self.x = lax.axis_index("seq")
        self.c = lax.rem(place, 2)
        self.y = lax.rem(place // 2, 2)
        self.z = place // 4


def pick(array, index, axis):
    return lax.dynamic_index_in_dim(array, index, axis, keepdims=False)


def over_core(v):
    return lax.ppermute(v, "dp", [(i, i ^ 1) for i in range(16)])


def over_y(v):
    return lax.ppermute(v, "dp", [(i, i ^ 2) for i in range(16)])


def over_x(v):
    return lax.ppermute(v, "seq", [(0, 1), (1, 0)])


def over_z(v, hops):
    return lax.ppermute(v, "dp", [(4 * a + i, 4 * b + i) for a, b in hops for i in range(4)])


def over_far(v):
    return over_z(v, [(0, 2), (2, 0), (1, 3), (3, 1)])


def over_near(v):
    return over_z(v, SWAP_ONE)


def spread(own):
    x, y, z = over_x(own), over_y(own), over_near(own)
    xy, yz, zx = over_x(y), over_y(z), over_near(x)
    return own, x, y, z, xy, yz, zx


def gather(at, rows):
    rest = jnp.zeros((8, D), BF16)
    own = jnp.where(at.x == 0, jnp.concatenate([rows, rest]), jnp.concatenate([rows[8:], rows[:8], rest]))
    other = over_far(own)
    here, there = spread(own), spread(other)
    found = [*here, over_x(here[5]), *there, over_y(there[6])]
    return found + [over_core(part) for part in found]


def tie(*values):
    return lax.optimization_barrier(values)


def add(kept, came):
    return (kept.astype(F32) + came.astype(F32)).astype(BF16)


def own_half(pairs, x):
    half = pairs.shape[-2] // 2
    return pick(pairs.reshape(*pairs.shape[:-2], 2, half, D), x, pairs.ndim - 2)


def blocks_of(pairs):
    return pairs.reshape(*pairs.shape[:-2], 2, pairs.shape[-2] // 2, D)


def picked(pairs, half, x):
    return pick(pick(pairs, half, 0), x, 0)


def merge(body, flags, sources, out_rows, name):
    parts = 2
    specs = []
    for array, where in sources:
        lead = (None,) * (array.ndim - 2)
        shape = (*lead, array.shape[-2], D // parts)
        specs.append(pl.BlockSpec(shape, lambda i, f, where=where: (*where(f), 0, i)))
    return pl.pallas_call(
        body,
        grid_spec=pltpu.PrefetchScalarGridSpec(
            num_scalar_prefetch=1,
            grid=(parts,),
            in_specs=specs,
            out_specs=[
                pl.BlockSpec((*rows, D // parts), lambda i, f, n=len(rows): (*[0] * n, i)) for rows in out_rows
            ],
        ),
        out_shape=[jax.ShapeDtypeStruct((*rows, D), BF16) for rows in out_rows],
        cost_estimate=cost(0, 0),
        compiler_params=params(60),
        name=name,
    )(flags, *[array for array, _ in sources])


def far_send_kernel(flags, a, b, c, d, out):
    out[0] = add(a[...], b[...])
    out[1] = add(c[...], d[...])


def far_send(flags, kept, came):
    kept, came = blocks_of(kept), blocks_of(came)
    sources = []
    for r in (0, 1):
        sources += [(part, lambda f, r=r: (r, 1 - f[2], f[1])) for part in (kept, came)]
    return merge(far_send_kernel, flags, sources, [(2, kept.shape[-2])], "far_send")[0]


def cross_merge_kernel(flags, *refs):
    ins, outs = refs[:8], refs[8:]
    outs[0][...] = add(ins[0][...], ins[1][...])
    outs[1][...] = add(ins[2][...], ins[3][...])
    message = outs[2]
    block = ins[4].shape[0]
    message[:block, :] = add(ins[4][...], ins[5][...])
    spill = message.shape[0] - (block + 8)
    total = ins[6][...].astype(F32) + ins[7][...].astype(F32)
    message[block:, :] = jnp.concatenate([jnp.zeros((8, total.shape[1]), F32), total[block - spill :]]).astype(BF16)


def cross_merge(flags, cross, cross_came):
    cross, cross_came = blocks_of(cross), blocks_of(cross_came)
    block = cross.shape[-2]
    spill = 2 * block - (D - QUERY_HEAD)
    chosen = [
        lambda f: (0, f[1]),
        lambda f: (1, f[1]),
        lambda f: (1 - f[0], 1 - f[1]),
        lambda f: (0, 1 - f[1]),
    ]
    sources = []
    for where in chosen:
        sources += [(cross, where), (cross_came, where)]
    return merge(cross_merge_kernel, flags, sources, [(block,)] * 2 + [(block + 8 + spill,)], "cross_merge")


def far_merge_kernel(flags, *refs):
    ins, outs = refs[:6], refs[6:]
    for number in range(2):
        first, second, third = ins[3 * number : 3 * number + 3]
        outs[number][...] = (first[...].astype(F32) + second[...].astype(F32) + third[...].astype(F32)).astype(BF16)


def far_merge(flags, far, far_came, far_last):
    far, far_came = blocks_of(far), blocks_of(far_came)
    sources = []
    for r in (lambda f: 1 - f[3] % 2, lambda f: f[3] % 2):
        sources += [(part, lambda f, r=r: (r(f), f[2], f[1])) for part in (far, far_came)]
        sources += [(far_last, lambda f, r=r: (r(f),))]
    return merge(far_merge_kernel, flags, sources, [(far.shape[-2],)] * 2, "far_merge")


def cross_second(at, mine, came):
    start = D - QUERY_HEAD
    block = mine[0].shape[-2]
    spill = 2 * block - start
    main = came[:block].astype(F32)
    tall = jnp.concatenate([jnp.zeros((block - spill, D), F32), came[block + 8 :].astype(F32)])
    ids = (at.c * 2 + at.x) * block + jnp.arange(block)[:, None]

    def half(index, y):
        part = jnp.where((at.c == 0) & (y == 0), tall, main)
        place = ids + y * 4 * block
        shared = (place >= start) & (place < start + 2 * D)
        own = jnp.where(index == 0, mine[0], mine[1]).astype(F32)
        return (own + jnp.where(shared, part, 0.0)).astype(BF16)

    return half(1 - at.y, 1 - at.y), half(at.y, at.y)


SWAP_ONE = [(0, 1), (1, 0), (2, 3), (3, 2)]
SWAP_TWO = [(0, 2), (2, 0), (1, 3), (3, 1)]


def with_rows(message, vec_rows):
    return jnp.concatenate([message, vec_rows.astype(BF16)])


def finish(at, flags, block, far, far_last, near, near_send, cross, cross_came, vec_rows, extra):
    near_came = over_core(near_send)
    vec_came = over_core(vec_rows)
    low, high, message = cross_merge(flags, cross, cross_came)
    near_came, message, low, high = tie(near_came, message, low, high)
    came = over_x(message)
    near, near_came = blocks_of(near), blocks_of(near_came)
    near_send = add(picked(near, 1 - at.y, at.x), picked(near_came, 1 - at.y, at.x))
    near = add(picked(near, at.y, at.x), picked(near_came, at.y, at.x))
    vec_rows = vec_rows + vec_came
    near_send, near, dk, dv, w, far_last = tie(near_send, near, *extra, far_last)
    far_out, far = far_merge(flags, *far, far_last)
    near_came, far_came, vec_came = over_y(near_send), over_z(far_out, SWAP_ONE), over_y(vec_rows)
    gm = memory_grads(dk, dv, w)
    gm, came = tie(gm, came)
    send, cross = cross_second(at, (low, high), came)
    send, near_came, vec_came, cross = tie(send, near_came, vec_came, cross)

    near = add(near, near_came)
    vec_rows = vec_rows + vec_came
    near, vec_rows, send = tie(near, vec_rows, send)
    cross_came, near_came, vec_came = over_y(send), over_z(near, [(3, 2), (1, 0)]), over_z(vec_rows, SWAP_ONE)
    cross = add(cross, cross_came)
    near = add(near, near_came)
    far = add(far, far_came)
    vec_rows = vec_rows + vec_came
    near, cross, vec_rows, far = tie(near, cross, vec_rows, far)

    cut = block // 16 * 8
    cross_came, near_came = over_z(cross, [(3, 2), (0, 1)]), over_z(near, [(2, 0)])
    far_top = over_z(far[:cut], [(0, 2), (1, 3)])
    cross = add(cross, cross_came)
    near_came, cross, far, vec_rows, far_top = tie(near_came, cross, far, vec_rows, far_top)

    cross_came, far_low = over_z(cross, [(2, 1)]), over_z(with_rows(far[cut:], vec_rows), [(0, 2), (1, 3)])
    far_came = jnp.concatenate([far_top, far_low[: block - cut]])
    vec_rows = vec_rows + far_low[block - cut :].astype(F32)
    kept = jnp.where(at.z >= 2, far, jnp.where(at.z == 0, near, cross))
    came = jnp.where(at.z >= 2, far_came, jnp.where(at.z == 0, near_came, cross_came))
    grad_rows = kept.astype(F32) + came.astype(F32)
    start = VEC_ROW - 31 * block
    last = jnp.concatenate([grad_rows[:start], vec_rows, jnp.zeros((block - start - VECS, D), F32)])
    is_last = (lax.axis_index("dp") == 15) & (at.x == 1)
    return jnp.where(is_last, last, grad_rows), gm


def shards(custom, inputs, memory, lengths, matched, cotangent, weights):
    axes = ("dp", "seq")
    share = 1.0 / lax.axis_size("seq")
    images, queries, _ = inputs.shape
    tokens = memory.shape[1]
    block = weights.shape[1]
    at = Place()
    left = lengths - at.x * tokens
    flags = jnp.stack([at.c if custom else 0, at.x, at.y, at.z]).astype(jnp.int32)

    def parts_of(value):
        if custom:
            return [value, over_x(value)]
        gathered = lax.all_gather(value, "seq")
        return [gathered[n] for n in range(gathered.shape[0])]

    if custom:
        bufs = gather(at, weights[0])
    else:
        bufs = [lax.all_gather(weights[0], axes, axis=0, tiled=True)]
    xb = jnp.pad(inputs, ((0, 0), (0, QP - queries), (0, 0))).reshape(images * QP, D)
    qs, ks, vs, os, y1, qc, key, value, mixed, stat, *w = forward(left, flags, xb, memory, bufs, queries)
    w = w[0] if custom else bufs[0]
    vec = w[VEC_ROW : VEC_ROW + VECS].astype(F32)
    near_rows = 4 * D + QUERY_HEAD
    far_rows = 2 * FF - HEAD_ROWS + TAIL
    cross_rows = 4 * D - QUERY_HEAD + HEAD_ROWS
    far_shape = (2, 2, 2 * block, D) if custom else (far_rows, D)
    near_shape = (2, 2 * block, D) if custom else (near_rows, D)
    cross_shape = (2, 2 * block, D) if custom else (cross_rows, D)
    out, *grads, db, doc, tot, dvec_mid = middle(
        flags, y1, parts_of(mixed), parts_of(stat), w, vec, cotangent, matched, far_shape, cross_shape, custom
    )
    far, cross = grads[: 1 + custom], grads[1 + custom :]
    if custom:
        far_came = over_core(far[1])
    dq, dk, dv = cross_backward(left, qc, key, value, doc, tot)
    dq_parts = parts_of(dq)
    if custom:
        far = [far[0], far_came]
        dk, message = tie(dk, far_send(flags, *far))
        far_last = over_y(message)
    dcv_row, *cross = memory_weights(flags, cross, memory, dk, dv, custom)
    if custom:
        dcv_row = dcv_row + over_x(dcv_row)
    da, gq_head, dvec_query, *cross = query_backward(flags, cross, y1, db, dq_parts, w, vec, custom)
    if custom:
        cross_came = over_core(cross[1])
    gq_head, dcv_row = tie(gq_head, dcv_row)
    gx, dvec_self, *near = self_backward(
        flags, xb, qs, ks, vs, os, da, gq_head, w, queries, near_shape, custom
    )
    vec_rows = (dvec_mid + dvec_query + dvec_self) * (1.0 if custom else share)
    is_value_bias = jnp.arange(VECS)[:, None] == 4
    vec_rows = jnp.where(is_value_bias, dcv_row[0:1], vec_rows)
    if custom:
        far_last, near_send = tie(far_last, near[1])
        grad_rows, gm = finish(
            at, flags, block, far, far_last, near[0], near_send, cross[0], cross_came, vec_rows, (dk, dv, w)
        )
    else:
        gm = memory_grads(dk, dv, w)
        low_share = jnp.asarray(share, BF16)
        pad = lax.axis_size(axes) * block - VEC_ROW - VECS
        last = 2 * FF - HEAD_ROWS
        memory_rows = slice(D - QUERY_HEAD, 3 * D - QUERY_HEAD)
        grads = jnp.concatenate(
            [near[0] * low_share, cross[0][: memory_rows.start] * low_share, cross[0][memory_rows]]
            + [cross[0][memory_rows.stop :] * low_share, far[0][:last] * low_share]
            + [vec_rows.astype(BF16), jnp.zeros((pad, D), BF16)]
        )
        grad_rows = lax.psum_scatter(grads, axes, scatter_dimension=0, tiled=True).astype(F32)
    return out[:, :queries], gx[:, :queries], gm, grad_rows[None]


def solution(mesh):
    placed = (
        P("dp", None, None),
        P("dp", "seq", None),
        P("dp"),
        P("dp", None),
        P("dp", None, None),
        P(None, ("dp", "seq"), None),
    )
    custom = dict(mesh.shape) == {"dp": 16, "seq": 2}
    return jax.shard_map(
        partial(shards, custom),
        mesh=mesh,
        in_specs=placed,
        out_specs=(
            P("dp", None, None),
            P("dp", None, None),
            P("dp", "seq", None),
            P(None, ("dp", "seq"), None),
        ),
        check_vma=False,
    )
```

```python
from functools import partial

import jax
import jax.numpy as jnp
from jax import lax
from jax.experimental import pallas as pl
from jax.experimental.pallas import tpu as pltpu
from jax.sharding import PartitionSpec as P

D = 768
H = 12
HEAD = 64
FF = 3072
PAIRS = H // 2
LANES = 2 * HEAD
QP = 112
VEC_ROW = 8 * D + 2 * FF
VECS = 24
TAIL = 256
HEAD_ROWS = 128
QUERY_HEAD = 64
SCALE = HEAD ** (-0.5)
EPS = 1e-05
NEG = -1e30
F32 = jnp.float32
BF16 = jnp.bfloat16
MIB = 1024 * 1024


def dot_nn(a, b):
    return lax.dot_general(a, b, (((1,), (0,)), ((), ())), preferred_element_type=F32)


def dot_nt(a, b):
    return lax.dot_general(a, b, (((1,), (1,)), ((), ())), preferred_element_type=F32)


def dot_tn(a, b):
    return lax.dot_general(a, b, (((0,), (0,)), ((), ())), preferred_element_type=F32)


def norm_parts(v):
    center = v - jnp.mean(v, axis=-1, keepdims=True)
    inverse = lax.rsqrt(jnp.mean(center * center, axis=-1, keepdims=True) + EPS)
    return center * inverse, inverse


def norm_back(dy, hat, inverse, gain):
    scaled = dy * gain
    mean_one = jnp.mean(scaled, axis=-1, keepdims=True)
    mean_two = jnp.mean(scaled * hat, axis=-1, keepdims=True)
    return inverse * (scaled - mean_one - hat * mean_two)


def rowsum(v):
    return jnp.sum(v.astype(F32), axis=0, keepdims=True)


def head_masks():
    lane = lax.broadcasted_iota(jnp.int32, (1, LANES), 1)
    first = jnp.where(lane < HEAD, 1.0, 0.0)
    return first.astype(BF16), (1.0 - first).astype(BF16)


def two_heads(block, masks):
    return jnp.concatenate([block * masks[0], block * masks[1]], axis=0)


def join_heads(stacked):
    lane = lax.broadcasted_iota(jnp.int32, (QP, LANES), 1)
    return jnp.where(lane < HEAD, stacked[:QP], stacked[QP:])


def weight_block(index):
    return pl.BlockSpec((D, D), lambda *_: (index, 0))


def whole(shape):
    return pl.BlockSpec(shape, lambda *_: (0,) * len(shape))


def params(mib):
    return pltpu.CompilerParams(vmem_limit_bytes=mib * MIB)


def cost(flops, moved):
    return pl.CostEstimate(flops=flops // 1000, bytes_accessed=moved // 1000, transcendentals=0)


FIRST_BLOCKS = (0, 1, 2, 5, 6, 3, 4)
SPREAD = ((0, 0, 0), (0, 0, 1), (0, 1, 0), (1, 0, 0), (0, 1, 1), (1, 1, 0), (1, 0, 1), (1, 1, 1))
PAIR_ROWS = 784
HOLDER = (3, 1, 1, 1)


class Assembly:
    def __init__(self, flags, bufs, weights, seams, sems, vec_low, vec_sem):
        self.core, self.x, self.y, self.z = flags[0], flags[1], flags[2], flags[3]
        self.bufs, self.weights, self.seams, self.sems = bufs, weights, seams, sems
        self.vec_low, self.vec_sem = vec_low, vec_sem
        self.ready = set()

    def buf(self, dc, dz2, spread):
        return self.bufs[dc * 16 + dz2 * 8 + SPREAD.index(spread)]

    def start_vec(self):
        first = VEC_ROW - 15 * PAIR_ROWS - 400
        for dc in (0, 1):
            for dz2 in (0, 1):
                for dz1, dy, dx in SPREAD:
                    here = (self.z ^ (2 * dz2 + dz1), self.y ^ dy, self.core ^ dc, self.x ^ dx)
                    hit = (here[0] == HOLDER[0]) & (here[1] == HOLDER[1]) & (here[2] == HOLDER[2]) & (here[3] == HOLDER[3])

                    @pl.when(hit)
                    def _(source=self.buf(dc, dz2, (dz1, dy, dx))):
                        pltpu.make_async_copy(source.at[pl.ds(first, 32)], self.vec_low, self.vec_sem).start()

    def wait_vec(self):
        pltpu.make_async_copy(self.weights.at[pl.ds(0, 32)], self.vec_low, self.vec_sem).wait()

    def start_group(self, dz2):
        def rows(start, count):
            return pl.ds(pl.multiple_of(start, 16), count)

        for dz1 in (0, 1):
            for dy in (0, 1):
                for dc in (0, 1):
                    pair = (self.z ^ (2 * dz2 + dz1)) * 4 + (self.y ^ dy) * 2 + (self.core ^ dc)
                    base, sem = pair * PAIR_ROWS, self.sems.at[pair]
                    near, far = self.buf(dc, dz2, (dz1, dy, 0)), self.buf(dc, dz2, (dz1, dy, 1))
                    for source, x in ((near, self.x), (far, 1 - self.x)):
                        target = self.weights.at[rows(base + 400 * x, 384)]
                        pltpu.make_async_copy(source.at[pl.ds(0, 384)], target, sem).start()
                        pltpu.make_async_copy(source.at[pl.ds(384, 16)], self.seams.at[pair, x], sem).start()

    def start(self):
        self.start_vec()
        for low in (True, False):

            @pl.when((self.z < 2) == low)
            def _(low=low):
                for dz2 in (0, 1) if low else (1, 0):
                    self.start_group(dz2)

    def wait(self, pair):
        if pair not in self.ready:
            self.ready.add(pair)
            rows = self.weights.at[pl.ds(0, PAIR_ROWS + 16)]
            pltpu.make_async_copy(rows, rows, self.sems.at[pair]).wait()
            halves = [self.seams[pair, x].astype(F32)[:8] for x in (0, 1)]
            seam = pl.ds(pair * PAIR_ROWS + 384, 16)
            self.weights[seam, :] = jnp.concatenate(halves, axis=0).astype(BF16)

    def block(self, number):
        for pair in range(number * D // PAIR_ROWS, (number * D + D - 1) // PAIR_ROWS + 1):
            self.wait(pair)


class Direct:
    def __init__(self, w_hbm, weights, sems, vec_low, vec_sem):
        self.copies = {}
        for number in FIRST_BLOCKS:
            rows = pl.ds(number * D, D)
            self.copies[number] = pltpu.make_async_copy(w_hbm.at[rows], weights.at[rows], sems.at[number])
        self.vec = pltpu.make_async_copy(w_hbm.at[pl.ds(VEC_ROW, 32)], vec_low, vec_sem)
        self.ready = set()

    def start(self):
        self.vec.start()
        for number in FIRST_BLOCKS:
            self.copies[number].start()

    def wait_vec(self):
        self.vec.wait()

    def block(self, number):
        if number not in self.ready:
            self.ready.add(number)
            self.copies[number].wait()


def forward_kernel(queries, custom, left_ref, flags, xb_ref, m_hbm, *refs):
    count = 32 if custom else 1
    bufs, refs = refs[:count], refs[count:]
    qs_out, ks_out, vs_out, os_out, y1_out, qc_out, k_out, v_out, o_out, stat_ref = refs[:10]
    w_out = refs[10] if custom else None
    weights, m_ref, qs_ref, ks_ref, vs_ref, os_ref, y1_ref, qc_ref, k_ref, v_ref, o_ref, vec_low = refs[10 + custom : 22 + custom]
    seams, w_sems, m_sems, out_sems, kv_sems, vec_sem, all_sems = refs[22 + custom :]
    images = m_ref.shape[0]
    tokens = m_ref.shape[1]
    if custom:
        feed = Assembly(flags, bufs, weights, seams, w_sems, vec_low, vec_sem)
    else:
        feed = Direct(bufs[0], weights, w_sems, vec_low, vec_sem)

    def load_memory(image):
        return pltpu.make_async_copy(m_hbm.at[image], m_ref.at[image], m_sems.at[image])

    def matrix(block):
        feed.block(block)
        return weights[block * D : (block + 1) * D, :]

    def leave_weights(half):
        rows = pl.ds(half * 8 * PAIR_ROWS, 8 * PAIR_ROWS)
        return pltpu.make_async_copy(weights.at[rows], w_out.at[rows], all_sems.at[half])

    small = [(qs_ref, qs_out), (ks_ref, ks_out), (vs_ref, vs_out), (os_ref, os_out), (y1_ref, y1_out), (qc_ref, qc_out)]

    def leave(number):
        return pltpu.make_async_copy(*small[number], out_sems.at[number])

    def leave_image(image, number):
        source, target = [(k_ref, k_out), (v_ref, v_out), (o_ref, o_out)][number]
        return pltpu.make_async_copy(source.at[image], target.at[image], kv_sems.at[image, number])

    feed.start()
    for image in range(images):
        load_memory(image).start()
    feed.wait_vec()
    vec = vec_low[...].astype(F32)
    xb = xb_ref[...]
    qs_ref[...] = ((dot_nn(xb, matrix(0)) + vec[0:1, :]) * SCALE).astype(BF16)
    leave(0).start()
    ks_ref[...] = dot_nn(xb, matrix(1)).astype(BF16)
    leave(1).start()
    vs_ref[...] = (dot_nn(xb, matrix(2)) + vec[1:2, :]).astype(BF16)
    leave(2).start()
    masks = head_masks()
    real = lax.broadcasted_iota(jnp.int32, (2 * QP, QP), 1) < queries
    places = [(slice(i * QP, (i + 1) * QP), slice(p * LANES, (p + 1) * LANES)) for i in range(images) for p in range(PAIRS)]

    def raw_self(place):
        return dot_nt(two_heads(qs_ref[place], masks), ks_ref[place])

    following = raw_self(places[0])
    for number, place in enumerate(places):
        scores = following
        if number + 1 < len(places):
            following = raw_self(places[number + 1])
        scores = jnp.where(real, scores, NEG)
        probs = jnp.exp(scores - jnp.max(scores, axis=-1, keepdims=True))
        probs = probs / jnp.sum(probs, axis=-1, keepdims=True)
        os_ref[place] = join_heads(dot_nn(probs.astype(BF16), vs_ref[place])).astype(BF16)
    leave(3).start()
    y1 = xb.astype(F32) + (dot_nn(os_ref[...], matrix(3)) + vec[2:3, :])
    y1_ref[...] = y1
    leave(4).start()
    hat, _ = norm_parts(y1)
    x1 = hat * vec[11:12, :] + vec[12:13, :]
    qc_ref[...] = ((dot_nn(x1.astype(BF16), matrix(4)) + vec[3:4, :]) * SCALE).astype(BF16)
    leave(5).start()

    feed.block(5)
    feed.block(6)
    if custom:
        for pair in range(8):
            feed.wait(pair)
        leave_weights(0).start()
    column = lax.broadcasted_iota(jnp.int32, (2 * QP, 128), 1)
    for image in range(images):
        load_memory(image).wait()
        rows = slice(image * QP, (image + 1) * QP)
        k_ref[image] = dot_nn(m_ref[image], matrix(5)).astype(BF16)
        v_ref[image] = (dot_nn(m_ref[image], matrix(6)) + vec[4:5, :]).astype(BF16)
        leave_image(image, 0).start()
        leave_image(image, 1).start()
        valid = lax.broadcasted_iota(jnp.int32, (2 * QP, tokens), 1) < left_ref[image]
        stat = jnp.zeros((2 * QP, 128), F32)
        def raw(pair):
            lanes = slice(pair * LANES, (pair + 1) * LANES)
            return dot_nt(two_heads(qc_ref[rows, lanes], masks), k_ref[image, :, lanes])

        following = raw(0)
        for pair in range(PAIRS):
            lanes = slice(pair * LANES, (pair + 1) * LANES)
            scores = following
            if pair + 1 < PAIRS:
                following = raw(pair + 1)
            scores = jnp.where(valid, scores, NEG)
            top = jnp.max(scores, axis=-1, keepdims=True)
            probs = jnp.exp(scores - top)
            total = jnp.sum(probs, axis=-1, keepdims=True)
            mixed = dot_nn(probs.astype(BF16), v_ref[image, :, lanes]) / total
            o_ref[image, :, lanes] = join_heads(mixed).astype(BF16)
            stat = jnp.where(column == pair, top + jnp.log(total), stat)
        stat_ref[image] = jnp.where(left_ref[image] > 0, stat.T[:8], NEG)
        leave_image(image, 2).start()
        if custom and image == 0:
            for pair in range(8, 16):
                feed.wait(pair)
            leave_weights(1).start()
    for number in range(len(small)):
        leave(number).wait()
    for image in range(images):
        for number in range(3):
            leave_image(image, number).wait()
    if custom:
        leave_weights(0).wait()
        leave_weights(1).wait()


def forward(left, flags, xb, memory, bufs, queries):
    custom = len(bufs) > 1
    rows = xb.shape[0]
    images, tokens, _ = memory.shape
    narrow = jax.ShapeDtypeStruct((rows, D), BF16)
    tall = jax.ShapeDtypeStruct(memory.shape, BF16)
    anywhere = pl.BlockSpec(memory_space=pl.ANY)
    small = pltpu.VMEM((rows, D), BF16)
    large = pltpu.VMEM(memory.shape, BF16)
    held = 16 * PAIR_ROWS if custom else 7 * D
    return pl.pallas_call(
        partial(forward_kernel, queries, custom),
        grid_spec=pltpu.PrefetchScalarGridSpec(
            num_scalar_prefetch=2,
            grid=(1,),
            in_specs=[whole((rows, D)), anywhere] + [anywhere] * len(bufs),
            out_specs=[anywhere] * 9 + [whole((images, 8, 2 * QP))] + [anywhere] * custom,
            scratch_shapes=[
                pltpu.VMEM((held, D), BF16),
                large, small, small, small, small,
                pltpu.VMEM((rows, D), F32),
                small, large, large,
                pltpu.VMEM((images, QP, D), BF16),
                pltpu.VMEM((32, D), BF16),
                pltpu.VMEM((16, 2, 16, D), BF16),
                pltpu.SemaphoreType.DMA((16,)),
                pltpu.SemaphoreType.DMA((images,)),
                pltpu.SemaphoreType.DMA((6,)),
                pltpu.SemaphoreType.DMA((images, 3)),
                pltpu.SemaphoreType.DMA(()),
                pltpu.SemaphoreType.DMA((2,)),
            ],
        ),
        out_shape=[
            narrow, narrow, narrow, narrow,
            jax.ShapeDtypeStruct((rows, D), F32),
            narrow, tall, tall,
            jax.ShapeDtypeStruct((images, QP, D), BF16),
            jax.ShapeDtypeStruct((images, 8, 2 * QP), F32),
        ]
        + [jax.ShapeDtypeStruct((held, D), BF16)] * custom,
        cost_estimate=cost(0, 0),
        compiler_params=params(60),
        name="forward",
    )(left, flags, xb, memory, *bufs)


def pieces(start, count, size):
    found = []
    done = 0
    while done < count:
        pair, offset = divmod(start + done, size)
        length = min(count - done, size - offset)
        found.append((done, pair, offset, length))
        done += length
    return found


class Halves:
    def __init__(self, keep, send, my_core):
        self.keep, self.send, self.my_core = keep, send, my_core

    def copy(self, target, source, pair, offset, length, sem):
        place = pair // self.cores()
        index = []
        for extent in reversed(target.shape[:-2]):
            index.insert(0, place % extent)
            place = place // extent
        return pltpu.make_async_copy(source, target.at[(*index, pl.ds(offset, length))], sem)

    def cores(self):
        return 1 if self.send is None else 2

    def start(self, source, pair, offset, length, sem):
        if self.send is None:
            self.copy(self.keep, source, pair, offset, length, sem).start()
            return

        @pl.when(self.my_core == pair % 2)
        def _():
            self.copy(self.keep, source, pair, offset, length, sem).start()

        @pl.when(self.my_core != pair % 2)
        def _():
            self.copy(self.send, source, pair, offset, length, sem).start()

    def wait(self, source, pair, offset, length, sem):
        self.copy(self.keep, source, pair, offset, length, sem).wait()


def middle_kernel(parts, split, *refs):
    flags, y1_ref = refs[:2]
    o_refs, stat_refs = refs[2 : 2 + parts], refs[2 + parts : 2 + 2 * parts]
    refs = refs[2 + 2 * parts :]
    w_hbm, vec, cot_ref, match_ref, out_hbm = refs[:5]
    halves = Halves(refs[5], refs[6] if split else None, flags[0])
    refs = refs[6 + split :]
    cross_halves = Halves(refs[0], refs[1] if split else None, flags[0])
    refs = refs[1 + split :]
    db_ref, doc_ref, tot_ref, dvec_ref = refs[:4]
    ocf, ocb, y2, x2b, u, slope, acc, e3b, staged, blank, out_ref, dco_ref, co, feed = refs[4:18]
    sems, blank_sem, out_sem, side_sems, w_sems = refs[18:]
    phase, step = pl.program_id(0), pl.program_id(1)
    steps = FF // D
    images = match_ref.shape[0]
    column = lax.broadcasted_iota(jnp.int32, (2 * QP, 128), 1)
    lane = lax.broadcasted_iota(jnp.int32, (QP, LANES), 1)
    size = halves.keep.shape[-2]
    side = cross_halves.keep.shape[-2]

    def load(block):
        target = co if block == 7 else feed.at[block - 8]
        return pltpu.make_async_copy(w_hbm.at[pl.ds(block * D, D)], target, w_sems.at[block - 7])

    def leave_out():
        return pltpu.make_async_copy(out_ref, out_hbm, out_sem)

    def leave_side(act):
        starts = [(dco_ref, 3 * D - QUERY_HEAD, D), (staged.at[0, 0], 4 * D - QUERY_HEAD, HEAD_ROWS)]
        for which, (source, start, count) in enumerate(starts):
            if (which == 0) != (act[0] == "o"):
                continue
            for number, (done, pair, offset, length) in enumerate(pieces(start, count, side)):
                piece = source.at[pl.ds(done, length)]
                getattr(cross_halves, act[1])(piece, pair, offset, length, side_sems.at[which, number])

    def leave(which, at, act):
        skip = HEAD_ROWS if which + at == 0 else 0
        start = which * FF + at * D + skip - HEAD_ROWS
        for number, (done, pair, offset, length) in enumerate(pieces(start, D - skip, size)):
            source = staged.at[at % 2, which, pl.ds(done + skip, length)]
            getattr(halves, act)(source, pair, offset, length, sems.at[at, which, number])

    def leave_blank(act):
        for _, pair, offset, length in pieces(2 * FF - HEAD_ROWS, TAIL, size):
            getattr(halves, act)(blank, pair, offset, length, blank_sem)

    def ordered(first, second):
        if parts != 2:
            return first, second
        swap = flags[1] != 0
        return jnp.where(swap, second, first), jnp.where(swap, first, second)

    @pl.when((phase == 0) & (step == 0))
    def _():
        load(7).start()
        for at in range(steps):
            load(8 + at).start()
            load(8 + steps + at).start()
        for image in range(images):
            rows = slice(image * QP, (image + 1) * QP)
            stats = [ref[image] for ref in stat_refs]
            if parts == 2:
                stats = ordered(*stats)
            top = stats[0]
            for n in range(1, parts):
                top = jnp.maximum(top, stats[n])
            mass = [jnp.exp(stats[n] - top) for n in range(parts)]
            total = mass[0]
            for n in range(1, parts):
                total = total + mass[n]
            tot_ref[image, 0:8, :] = top + jnp.log(total)
            shares = [jnp.concatenate([m / total, jnp.zeros((120, 2 * QP), F32)], axis=0).T for m in mass]
            for pair in range(PAIRS):
                lanes = slice(pair * LANES, (pair + 1) * LANES)
                values = [ref[image, :, lanes].astype(F32) for ref in o_refs]
                if parts == 2:
                    values = ordered(*values)
                mixed = jnp.zeros((QP, LANES), F32)
                for n in range(parts):
                    share = shares[n][:, pair : pair + 1]
                    mixed = mixed + values[n] * jnp.where(lane < HEAD, share[:QP], share[QP:])
                ocf[rows, lanes] = mixed
        ocb[...] = ocf[...].astype(BF16)
        hat, _ = norm_parts(y1_ref[...])
        x1 = hat * vec[11:12, :] + vec[12:13, :]
        load(7).wait()
        total = x1 + (dot_nn(ocb[...], co[...]) + vec[5:6, :])
        y2[...] = total
        hat, _ = norm_parts(total)
        x2 = hat * vec[13:14, :] + vec[14:15, :]
        x2b[...] = x2.astype(BF16)
        acc[...] = x2 + vec[6:7, :]

    for at in range(steps):

        @pl.when((phase == 0) & (step == at))
        def _(at=at):
            load(8 + at).wait()
            load(8 + steps + at).wait()

    f1, f2 = feed.at[step], feed.at[steps + step]

    @pl.when(phase == 0)
    def _():
        h = dot_nt(x2b[...], f1[...]) + vec[pl.ds(7 + step, 1), :]
        root = 0.7978845608028654
        square = h * h
        t = jnp.tanh(root * (h + 0.044715 * (h * square)))
        half = 0.5 * (1.0 + t)
        slope[step] = half + (0.5 * root) * h * (1.0 - t * t) * (1.0 + 0.134145 * square)
        active = (h * half).astype(BF16)
        u[step] = active
        acc[...] += dot_nn(active, f2[...])

    @pl.when((phase == 1) & (step == 0))
    def _():
        blank[...] = jnp.zeros_like(blank)
        leave_blank("start")
        dvec_ref[...] = jnp.zeros_like(dvec_ref)
        hat, inverse = norm_parts(acc[...])
        out = hat * vec[15:16, :] + vec[16:17, :]
        grads = []
        for image in range(images):
            out_ref[image] = out[image * QP : (image + 1) * QP]
            matched = match_ref[image]
            hit = lax.broadcasted_iota(jnp.int32, (QP, matched.shape[1]), 0) == matched
            grads.append(dot_nn(jnp.where(hit, 1.0, 0.0).astype(BF16), cot_ref[image]))
        leave_out().start()
        dy = jnp.concatenate(grads, axis=0)
        dvec_ref[15:16, :] = rowsum(dy * hat)
        dvec_ref[16:17, :] = rowsum(dy)
        dc = norm_back(dy, hat, inverse, vec[15:16, :])
        low = dc.astype(BF16)
        e3b[...] = low
        dvec_ref[6:7, :] = rowsum(low)
        acc[...] = dc

    for at in range(2, steps):

        @pl.when((phase == 1) & (step == at))
        def _(at=at):
            leave(0, at - 2, "wait")
            leave(1, at - 2, "wait")
            if at == 2:
                leave_side(("f", "wait"))

    @pl.when(phase == 1)
    def _():
        du = dot_nt(e3b[...], f2[...])
        dh = (du * slope[step]).astype(BF16)
        slot = lax.rem(step, 2)
        staged[slot, 1] = dot_tn(u[step], e3b[...]).astype(BF16)
        staged[slot, 0] = dot_tn(dh, x2b[...]).astype(BF16)

        @pl.when(step == 0)
        def _():
            leave_side(("f", "start"))

        for at in range(steps):

            @pl.when(step == at)
            def _(at=at):
                leave(0, at, "start")
                leave(1, at, "start")

        dvec_ref[pl.ds(7 + step, 1), :] = rowsum(dh)
        acc[...] += dot_nn(dh, f1[...])

    @pl.when((phase == 1) & (step == steps - 1))
    def _():
        hat, inverse = norm_parts(y2[...])
        dy = acc[...]
        dvec_ref[13:14, :] = rowsum(dy * hat)
        dvec_ref[14:15, :] = rowsum(dy)
        db = norm_back(dy, hat, inverse, vec[13:14, :])
        db_ref[...] = db
        low = db.astype(BF16)
        dvec_ref[5:6, :] = rowsum(low)
        dco_ref[...] = dot_tn(ocb[...], low).astype(BF16)
        leave_side(("o", "start"))
        doc = dot_nt(low, co[...]).astype(BF16)
        doc_ref[...] = doc
        both = doc.astype(F32) * ocf[...]
        for image in range(images):
            rows = slice(image * QP, (image + 1) * QP)
            tot = jnp.zeros((2 * QP, 128), F32)
            for pair in range(PAIRS):
                piece = both[rows, pair * LANES : (pair + 1) * LANES]
                one = jnp.sum(jnp.where(lane < HEAD, piece, 0.0), axis=-1, keepdims=True)
                two = jnp.sum(jnp.where(lane < HEAD, 0.0, piece), axis=-1, keepdims=True)
                tot = jnp.where(column == pair, jnp.concatenate([one, two], axis=0), tot)
            tot_ref[image, 8:16, :] = tot.T[:8]
        leave_blank("wait")
        leave_out().wait()
        leave_side(("o", "wait"))
        for which in (0, 1):
            leave(which, steps - 2, "wait")
            leave(which, steps - 1, "wait")


def halves_shape(shape, split):
    return [jax.ShapeDtypeStruct(shape, BF16)] * (1 + split)


def middle(flags, y1, o_parts, stat_parts, w, vec, cot, matched, far_shape, cross_shape, split):
    rows = y1.shape[0]
    images = cot.shape[0]
    steps = FF // D
    parts = len(o_parts)
    anywhere = pl.BlockSpec(memory_space=pl.ANY)
    return pl.pallas_call(
        partial(middle_kernel, parts, split),
        grid_spec=pltpu.PrefetchScalarGridSpec(
            num_scalar_prefetch=1,
            grid=(2, steps),
            in_specs=[whole(y1.shape)]
            + [whole(o_parts[0].shape)] * parts
            + [whole(stat_parts[0].shape)] * parts
            + [anywhere, whole((VECS, D)), whole(cot.shape), whole((images, 1, matched.shape[1]))],
            out_specs=[anywhere] * (3 + 2 * split)
            + [
                whole((rows, D)),
                whole((rows, D)),
                whole((images, 16, 2 * QP)),
                whole((VECS, D)),
            ],
            scratch_shapes=[
                pltpu.VMEM((rows, D), F32),
                pltpu.VMEM((rows, D), BF16),
                pltpu.VMEM((rows, D), F32),
                pltpu.VMEM((rows, D), BF16),
                pltpu.VMEM((steps, rows, D), BF16),
                pltpu.VMEM((steps, rows, D), F32),
                pltpu.VMEM((rows, D), F32),
                pltpu.VMEM((rows, D), BF16),
                pltpu.VMEM((2, 2, D, D), BF16),
                pltpu.VMEM((TAIL, D), BF16),
                pltpu.VMEM((images, QP, D), F32),
                pltpu.VMEM((D, D), BF16),
                pltpu.VMEM((D, D), BF16),
                pltpu.VMEM((2 * steps, D, D), BF16),
                pltpu.SemaphoreType.DMA((steps, 2, 2)),
                pltpu.SemaphoreType.DMA(()),
                pltpu.SemaphoreType.DMA(()),
                pltpu.SemaphoreType.DMA((2, 2)),
                pltpu.SemaphoreType.DMA((1 + 2 * steps,)),
            ],
        ),
        out_shape=[jax.ShapeDtypeStruct((images, QP, D), F32)]
        + halves_shape(far_shape, split)
        + halves_shape(cross_shape, split)
        + [
            jax.ShapeDtypeStruct((rows, D), F32),
            jax.ShapeDtypeStruct((rows, D), BF16),
            jax.ShapeDtypeStruct((images, 16, 2 * QP), F32),
            jax.ShapeDtypeStruct((VECS, D), F32),
        ],
        cost_estimate=cost(2 * rows * D * (6 * FF + 3 * D), 2 * FF * D * 6),
        compiler_params=params(60),
        name="middle",
    )(flags, y1, *o_parts, *stat_parts, w, vec, cot, matched[:, None, :])


def cross_backward_kernel(left_ref, q_ref, k_ref, v_ref, do_ref, tot_ref, dq_ref, dk_ref, dv_ref):
    tokens = k_ref.shape[1]
    masks = head_masks()
    valid = lax.broadcasted_iota(jnp.int32, (tokens, 2 * QP), 0) < left_ref[pl.program_id(0)]
    def raw(pair):
        lanes = slice(pair * LANES, (pair + 1) * LANES)
        query = two_heads(q_ref[0, :, lanes], masks)
        dout = two_heads(do_ref[0, :, lanes], masks)
        return query, dout, dot_nt(k_ref[0, :, lanes], query), dot_nt(v_ref[0, :, lanes], dout)

    following = raw(0)
    for pair in range(PAIRS):
        lanes = slice(pair * LANES, (pair + 1) * LANES)
        query, dout, scores, dprobs = following
        if pair + 1 < PAIRS:
            following = raw(pair + 1)
        probs = jnp.where(valid, jnp.exp(scores - tot_ref[0, pair : pair + 1, :]), 0.0)
        dscores = (probs * (dprobs - tot_ref[0, 8 + pair : 9 + pair, :])).astype(BF16)
        dv_ref[0, :, lanes] = dot_nn(probs.astype(BF16), dout).astype(BF16)
        dk_ref[0, :, lanes] = dot_nn(dscores, query).astype(BF16)
        dq_ref[0, :, lanes] = join_heads(dot_tn(k_ref[0, :, lanes], dscores).T).astype(BF16)


def cross_backward(left, qc, key, value, doc, tot):
    images, tokens, _ = key.shape
    q_block = pl.BlockSpec((1, QP, D), lambda i, _: (i, 0, 0))
    m_block = pl.BlockSpec((1, tokens, D), lambda i, _: (i, 0, 0))
    s_block = pl.BlockSpec((1, 16, 2 * QP), lambda i, _: (i, 0, 0))
    return pl.pallas_call(
        cross_backward_kernel,
        grid_spec=pltpu.PrefetchScalarGridSpec(
            num_scalar_prefetch=1,
            grid=(images,),
            in_specs=[q_block, m_block, m_block, q_block, s_block],
            out_specs=[q_block, m_block, m_block],
        ),
        out_shape=[
            jax.ShapeDtypeStruct((images, QP, D), BF16),
            jax.ShapeDtypeStruct(key.shape, BF16),
            jax.ShapeDtypeStruct(key.shape, BF16),
        ],
        cost_estimate=cost(4 * images * 2 * QP * tokens * D // 3, images * tokens * D * 8),
        compiler_params=params(60),
        name="cross_backward",
    )(left, qc.reshape(images, QP, D), key, value, doc.reshape(images, QP, D), tot)


def memory_weights_kernel(split, flags, *refs):
    m_ref, dk_ref, dv_ref = refs[1 + split : 4 + split]
    refs = refs[4 + split :]
    gb_ref = refs[0]
    halves = Halves(refs[1], refs[2] if split else None, flags[0])
    low, sems = refs[2 + split :]
    def leave(which, act):
        start = (1 + which) * D - QUERY_HEAD
        for number, (done, pair, offset, length) in enumerate(pieces(start, D, halves.keep.shape[-2])):
            piece = low.at[which, pl.ds(done, length)]
            getattr(halves, act)(piece, pair, offset, length, sems.at[which, number])

    tall = m_ref[...].reshape(-1, D)
    for which, ref in ((0, dk_ref), (1, dv_ref)):
        low[which] = dot_tn(tall, ref[...].reshape(-1, D)).astype(BF16)
        leave(which, "start")
    gb_ref[...] = jnp.broadcast_to(rowsum(dv_ref[...].reshape(-1, D)), gb_ref.shape)
    for which in (0, 1):
        leave(which, "wait")


def memory_weights(flags, cross, memory, dk, dv, split):
    images, tokens, _ = memory.shape
    block = whole(memory.shape)
    anywhere = pl.BlockSpec(memory_space=pl.ANY)
    return pl.pallas_call(
        partial(memory_weights_kernel, split),
        grid_spec=pltpu.PrefetchScalarGridSpec(
            num_scalar_prefetch=1,
            grid=(1,),
            in_specs=[anywhere] * (1 + split) + [block, block, block],
            out_specs=[whole((8, D))] + [anywhere] * (1 + split),
            scratch_shapes=[
                pltpu.VMEM((2, D, D), BF16),
                pltpu.SemaphoreType.DMA((2, 2)),
            ],
        ),
        out_shape=[jax.ShapeDtypeStruct((8, D), F32)] + halves_shape(cross[0].shape, split),
        input_output_aliases={1 + n: 1 + n for n in range(1 + split)},
        cost_estimate=cost(4 * images * tokens * D * D, images * tokens * D * 6),
        compiler_params=params(60),
        name="memory_weights",
    )(flags, *cross, memory, dk, dv)


def memory_grads_kernel(dk_ref, dv_ref, ck, cv, gm_ref):
    gm_ref[0] = dot_nt(dk_ref[0], ck[...]) + dot_nt(dv_ref[0], cv[...])


def memory_grads(dk, dv, w):
    images, tokens, _ = dk.shape
    block = pl.BlockSpec((1, tokens, D), lambda i: (i, 0, 0))
    return pl.pallas_call(
        memory_grads_kernel,
        grid=(images,),
        in_specs=[block, block, weight_block(5), weight_block(6)],
        out_specs=block,
        out_shape=jax.ShapeDtypeStruct(dk.shape, F32),
        cost_estimate=pl.CostEstimate(
            flops=4 * images * tokens * D * D, bytes_accessed=images * tokens * D * 8, transcendentals=0
        ),
        compiler_params=params(60),
        name="memory_grads",
    )(dk, dv, w, w)


class Loads:
    def __init__(self, pairs, sems):
        self.copies = [(pltpu.make_async_copy(source, target, sems.at[n]), target) for n, (source, target) in enumerate(pairs)]
        self.ready = set()
        for copy, _ in self.copies:
            copy.start()

    def __call__(self, number):
        copy, target = self.copies[number]
        if number not in self.ready:
            copy.wait()
            self.ready.add(number)
        return target[...]


def query_backward_kernel(parts, split, flags, *refs):
    sources, vec = refs[1 + split : 4 + split + parts], refs[4 + split + parts]
    refs = refs[5 + split + parts :]
    da_ref, gq_head_ref, dvec_ref = refs[:3]
    halves = Halves(refs[3], refs[4] if split else None, flags[0])
    refs = refs[4 + split :]
    targets, staged, load_sems, sems = refs[: 3 + parts], refs[3 + parts], refs[4 + parts], refs[5 + parts]
    w_hbm = sources[-1]
    sources = [*sources[:-1], w_hbm.at[pl.ds(4 * D, D)]]
    get = Loads(list(zip(sources, targets)), load_sems)

    def leave(act):
        for number, (done, pair, offset, length) in enumerate(pieces(0, D - QUERY_HEAD, halves.keep.shape[-2])):
            piece = staged.at[pl.ds(done + QUERY_HEAD, length)]
            getattr(halves, act)(piece, pair, offset, length, sems.at[number])

    total = get(0).astype(F32)
    for number in range(1, parts):
        total = total + get(number).astype(F32)
    dq = total.astype(BF16) * SCALE
    hat, inverse = norm_parts(get(parts))
    gain = vec[11:12, :]
    x1b = (hat * gain + vec[12:13, :]).astype(BF16)
    gcq = dot_tn(x1b, dq).astype(BF16)
    staged[...] = gcq
    leave("start")
    gq_head_ref[...] = gcq[:QUERY_HEAD]
    dvec_ref[...] = jnp.zeros_like(dvec_ref)
    dvec_ref[3:4, :] = rowsum(dq)
    dy = get(parts + 1) + dot_nt(dq, get(parts + 2))
    dvec_ref[11:12, :] = rowsum(dy * hat)
    dvec_ref[12:13, :] = rowsum(dy)
    da = norm_back(dy, hat, inverse, gain)
    da_ref[...] = da
    dvec_ref[2:3, :] = rowsum(da.astype(BF16))
    leave("wait")


def query_backward(flags, cross, y1, db, dq_parts, w, vec, split):
    rows = y1.shape[0]
    parts = len(dq_parts)
    full = whole((rows, D))
    anywhere = pl.BlockSpec(memory_space=pl.ANY)
    return pl.pallas_call(
        partial(query_backward_kernel, parts, split),
        grid_spec=pltpu.PrefetchScalarGridSpec(
            num_scalar_prefetch=1,
            grid=(1,),
            in_specs=[anywhere] * (4 + split + parts) + [whole((VECS, D))],
            out_specs=[full, whole((QUERY_HEAD, D)), whole((VECS, D))] + [anywhere] * (1 + split),
            scratch_shapes=[pltpu.VMEM((rows, D), BF16)] * parts
            + [pltpu.VMEM((rows, D), F32)] * 2
            + [pltpu.VMEM((D, D), BF16)] * 2
            + [pltpu.SemaphoreType.DMA((parts + 3,)), pltpu.SemaphoreType.DMA((2,))],
        ),
        out_shape=[
            jax.ShapeDtypeStruct((rows, D), F32),
            jax.ShapeDtypeStruct((QUERY_HEAD, D), BF16),
            jax.ShapeDtypeStruct((VECS, D), F32),
        ]
        + halves_shape(cross[0].shape, split),
        input_output_aliases={1 + n: 3 + n for n in range(1 + split)},
        cost_estimate=cost(4 * rows * D * D, rows * D * 16),
        compiler_params=params(60),
        name="query_backward",
    )(flags, *cross, *[part.reshape(rows, D) for part in dq_parts], y1, db, w, vec)


def self_backward_kernel(queries, split, *refs):
    flags, os_hbm, da_hbm, qs_hbm, ks_hbm, vs_hbm, x_hbm, w_hbm, gq_ref, gx_ref, dvec_ref, keep_ref = refs[:12]
    halves = Halves(keep_ref, refs[12] if split else None, flags[0])
    sq, sk, sv, g_ref, os_ref, da_ref, ao, qs, ks, vs, x_ref, aq, ak, av, sems, load_sems = refs[12 + split :]
    size = keep_ref.shape[-2]
    matrices = [w_hbm.at[pl.ds(block * D, D)] for block in range(4)]
    get = Loads(
        [(os_hbm, os_ref), (da_hbm, da_ref), (matrices[3], ao), (qs_hbm, qs), (ks_hbm, ks), (vs_hbm, vs)]
        + [(x_hbm, x_ref), (matrices[0], aq), (matrices[1], ak), (matrices[2], av)],
        load_sems,
    )

    def leave(pair, act):
        getattr(halves, act)(g_ref.at[pl.ds(pair * size, size)], pair, 0, size, sems.at[pair])

    pairs = g_ref.shape[0] // size
    images = x_ref.shape[0] // QP
    dvec_ref[...] = jnp.zeros_like(dvec_ref)
    os = get(0)
    da = get(1)
    low = da.astype(BF16)
    g_ref[4 * D :, :] = gq_ref[...]
    g_ref[3 * D : 4 * D, :] = dot_tn(os, low).astype(BF16)
    dos = dot_nt(low, get(2)).astype(BF16)
    for number in (3, 4, 5):
        get(number)
    masks = head_masks()
    real = lax.broadcasted_iota(jnp.int32, (QP, 2 * QP), 0) < queries
    places = [(slice(i * QP, (i + 1) * QP), slice(p * LANES, (p + 1) * LANES)) for i in range(images) for p in range(PAIRS)]

    def raw(place):
        query = two_heads(qs[place], masks)
        dout = two_heads(dos[place], masks)
        return query, dout, dot_nt(ks[place], query), dot_nt(vs[place], dout)

    following = raw(places[0])
    for number, place in enumerate(places):
        query, dout, scores, dprobs = following
        if number + 1 < len(places):
            following = raw(places[number + 1])
        scores = jnp.where(real, scores, NEG)
        probs = jnp.exp(scores - jnp.max(scores, axis=0, keepdims=True))
        probs = probs / jnp.sum(probs, axis=0, keepdims=True)
        dscores = (probs * (dprobs - jnp.sum(probs * dprobs, axis=0, keepdims=True))).astype(BF16)
        sv[place] = dot_nn(probs.astype(BF16), dout).astype(BF16)
        sk[place] = dot_nn(dscores, query).astype(BF16)
        sq[place] = join_heads(dot_tn(ks[place], dscores).T).astype(BF16) * SCALE
    dvec_ref[0:1, :] = rowsum(sq[...])
    dvec_ref[1:2, :] = rowsum(sv[...])
    xb = get(6)
    g_ref[2 * D : 3 * D, :] = dot_tn(xb, sv[...]).astype(BF16)
    for pair in range(2, pairs):
        leave(pair, "start")
    g_ref[D : 2 * D, :] = dot_tn(xb, sk[...]).astype(BF16)
    for pair in range(1, min(2, pairs)):
        leave(pair, "start")
    g_ref[0:D, :] = dot_tn(xb, sq[...]).astype(BF16)
    leave(0, "start")
    gx = da + dot_nt(sq[...], get(7)) + dot_nt(sk[...], get(8)) + dot_nt(sv[...], get(9))
    for image in range(images):
        gx_ref[image] = gx[image * QP : (image + 1) * QP]
    for pair in range(pairs):
        leave(pair, "wait")


def self_backward(flags, xb, qs, ks, vs, os, da, gq_head, w, queries, shape, split):
    rows = xb.shape[0]
    images = rows // QP
    anywhere = pl.BlockSpec(memory_space=pl.ANY)
    return pl.pallas_call(
        partial(self_backward_kernel, queries, split),
        grid_spec=pltpu.PrefetchScalarGridSpec(
            num_scalar_prefetch=1,
            grid=(1,),
            in_specs=[anywhere] * 7 + [whole((QUERY_HEAD, D))],
            out_specs=[whole((images, QP, D)), whole((VECS, D))] + [anywhere] * (1 + split),
            scratch_shapes=[pltpu.VMEM((rows, D), BF16)] * 3
            + [pltpu.VMEM((4 * D + QUERY_HEAD, D), BF16), pltpu.VMEM((rows, D), BF16), pltpu.VMEM((rows, D), F32)]
            + [pltpu.VMEM((D, D), BF16)]
            + [pltpu.VMEM((rows, D), BF16)] * 4
            + [pltpu.VMEM((D, D), BF16)] * 3
            + [pltpu.SemaphoreType.DMA((4,)), pltpu.SemaphoreType.DMA((10,))],
        ),
        out_shape=[
            jax.ShapeDtypeStruct((images, QP, D), F32),
            jax.ShapeDtypeStruct((VECS, D), F32),
        ]
        + halves_shape(shape, split),
        cost_estimate=cost(16 * rows * D * D * 2, 8 * D * D * 2),
        compiler_params=params(60),
        name="self_backward",
    )(flags, os, da, qs, ks, vs, xb, w, gq_head)


class Place:
    def __init__(self):
        place = lax.axis_index("dp")
        self.x = lax.axis_index("seq")
        self.c = lax.rem(place, 2)
        self.y = lax.rem(place // 2, 2)
        self.z = place // 4


def pick(array, index, axis):
    return lax.dynamic_index_in_dim(array, index, axis, keepdims=False)


def over_core(v):
    return lax.ppermute(v, "dp", [(i, i ^ 1) for i in range(16)])


def over_y(v):
    return lax.ppermute(v, "dp", [(i, i ^ 2) for i in range(16)])


def over_x(v):
    return lax.ppermute(v, "seq", [(0, 1), (1, 0)])


def over_z(v, hops):
    return lax.ppermute(v, "dp", [(4 * a + i, 4 * b + i) for a, b in hops for i in range(4)])


def over_far(v):
    return over_z(v, [(0, 2), (2, 0), (1, 3), (3, 1)])


def over_near(v):
    return over_z(v, SWAP_ONE)


def spread(own):
    x, y, z = over_x(own), over_y(own), over_near(own)
    xy, yz, zx = over_x(y), over_y(z), over_near(x)
    return own, x, y, z, xy, yz, zx


def gather(at, rows):
    rest = jnp.zeros((8, D), BF16)
    own = jnp.where(at.x == 0, jnp.concatenate([rows, rest]), jnp.concatenate([rows[8:], rows[:8], rest]))
    other = over_far(own)
    here, there = spread(own), spread(other)
    found = [*here, over_x(here[5]), *there, over_y(there[6])]
    return found + [over_core(part) for part in found]


def tie(*values):
    return lax.optimization_barrier(values)


def add(kept, came):
    return (kept.astype(F32) + came.astype(F32)).astype(BF16)


def own_half(pairs, x):
    half = pairs.shape[-2] // 2
    return pick(pairs.reshape(*pairs.shape[:-2], 2, half, D), x, pairs.ndim - 2)


def blocks_of(pairs):
    return pairs.reshape(*pairs.shape[:-2], 2, pairs.shape[-2] // 2, D)


def picked(pairs, half, x):
    return pick(pick(pairs, half, 0), x, 0)


def merge(body, flags, sources, out_rows, name):
    parts = 2
    specs = []
    for array, where in sources:
        lead = (None,) * (array.ndim - 2)
        shape = (*lead, array.shape[-2], D // parts)
        specs.append(pl.BlockSpec(shape, lambda i, f, where=where: (*where(f), 0, i)))
    return pl.pallas_call(
        body,
        grid_spec=pltpu.PrefetchScalarGridSpec(
            num_scalar_prefetch=1,
            grid=(parts,),
            in_specs=specs,
            out_specs=[
                pl.BlockSpec((*rows, D // parts), lambda i, f, n=len(rows): (*[0] * n, i)) for rows in out_rows
            ],
        ),
        out_shape=[jax.ShapeDtypeStruct((*rows, D), BF16) for rows in out_rows],
        cost_estimate=cost(0, 0),
        compiler_params=params(60),
        name=name,
    )(flags, *[array for array, _ in sources])


def far_send_kernel(flags, a, b, c, d, out):
    out[0] = add(a[...], b[...])
    out[1] = add(c[...], d[...])


def far_send(flags, kept, came):
    kept, came = blocks_of(kept), blocks_of(came)
    sources = []
    for r in (0, 1):
        sources += [(part, lambda f, r=r: (r, 1 - f[2], f[1])) for part in (kept, came)]
    return merge(far_send_kernel, flags, sources, [(2, kept.shape[-2])], "far_send")[0]


def cross_merge_kernel(flags, *refs):
    ins, outs = refs[:8], refs[8:]
    outs[0][...] = add(ins[0][...], ins[1][...])
    outs[1][...] = add(ins[2][...], ins[3][...])
    message = outs[2]
    block = ins[4].shape[0]
    spill = message.shape[0] - (block + 8)
    main = ins[4][...].astype(F32) + ins[5][...].astype(F32)
    total = ins[6][...].astype(F32) + ins[7][...].astype(F32)
    gap = jnp.zeros((8, total.shape[1]), F32)
    message[...] = jnp.concatenate([main, gap, total[block - spill :]], axis=0).astype(BF16)


def cross_merge(flags, cross, cross_came):
    cross, cross_came = blocks_of(cross), blocks_of(cross_came)
    block = cross.shape[-2]
    spill = 2 * block - (D - QUERY_HEAD)
    chosen = [
        lambda f: (0, f[1]),
        lambda f: (1, f[1]),
        lambda f: (1 - f[0], 1 - f[1]),
        lambda f: (0, 1 - f[1]),
    ]
    sources = []
    for where in chosen:
        sources += [(cross, where), (cross_came, where)]
    return merge(cross_merge_kernel, flags, sources, [(block,)] * 2 + [(block + 8 + spill,)], "cross_merge")


def far_merge_kernel(flags, *refs):
    ins, outs = refs[:6], refs[6:]
    for number in range(2):
        first, second, third = ins[3 * number : 3 * number + 3]
        outs[number][...] = (first[...].astype(F32) + second[...].astype(F32) + third[...].astype(F32)).astype(BF16)


def far_merge(flags, far, far_came, far_last):
    far, far_came = blocks_of(far), blocks_of(far_came)
    sources = []
    for r in (lambda f: 1 - f[3] % 2, lambda f: f[3] % 2):
        sources += [(part, lambda f, r=r: (r(f), f[2], f[1])) for part in (far, far_came)]
        sources += [(far_last, lambda f, r=r: (r(f),))]
    return merge(far_merge_kernel, flags, sources, [(far.shape[-2],)] * 2, "far_merge")


def cross_second(at, mine, came):
    start = D - QUERY_HEAD
    block = mine[0].shape[-2]
    spill = 2 * block - start
    main = came[:block].astype(F32)
    tall = jnp.concatenate([jnp.zeros((block - spill, D), F32), came[block + 8 :].astype(F32)])
    ids = (at.c * 2 + at.x) * block + jnp.arange(block)[:, None]

    def half(index, y):
        part = jnp.where((at.c == 0) & (y == 0), tall, main)
        place = ids + y * 4 * block
        shared = (place >= start) & (place < start + 2 * D)
        own = jnp.where(index == 0, mine[0], mine[1]).astype(F32)
        return (own + jnp.where(shared, part, 0.0)).astype(BF16)

    return half(1 - at.y, 1 - at.y), half(at.y, at.y)


SWAP_ONE = [(0, 1), (1, 0), (2, 3), (3, 2)]
SWAP_TWO = [(0, 2), (2, 0), (1, 3), (3, 1)]


def with_rows(message, vec_rows):
    return jnp.concatenate([message, vec_rows.astype(BF16)])


def finish(at, flags, block, far, far_last, near, near_send, cross, cross_came, vec_rows, extra):
    near_came = over_core(near_send)
    vec_came = over_core(vec_rows)
    low, high, message = cross_merge(flags, cross, cross_came)
    near_came, message, low, high = tie(near_came, message, low, high)
    came = over_x(message)
    near, near_came = blocks_of(near), blocks_of(near_came)
    near_send = add(picked(near, 1 - at.y, at.x), picked(near_came, 1 - at.y, at.x))
    near = add(picked(near, at.y, at.x), picked(near_came, at.y, at.x))
    vec_rows = vec_rows + vec_came
    near_send, near, dk, dv, w, far_last = tie(near_send, near, *extra, far_last)
    far_out, far = far_merge(flags, *far, far_last)
    near_came, far_came, vec_came = over_y(near_send), over_z(far_out, SWAP_ONE), over_y(vec_rows)
    gm = memory_grads(dk, dv, w)
    gm, came = tie(gm, came)
    send, cross = cross_second(at, (low, high), came)
    send, near_came, vec_came, cross = tie(send, near_came, vec_came, cross)

    near = add(near, near_came)
    vec_rows = vec_rows + vec_came
    near, vec_rows, send = tie(near, vec_rows, send)
    cross_came, near_came, vec_came = over_y(send), over_z(near, [(3, 2), (1, 0)]), over_z(vec_rows, SWAP_ONE)
    cross = add(cross, cross_came)
    near = add(near, near_came)
    far = add(far, far_came)
    vec_rows = vec_rows + vec_came
    near, cross, vec_rows, far = tie(near, cross, vec_rows, far)

    cut = block // 16 * 8
    cross_came, near_came = over_z(cross, [(3, 2), (0, 1)]), over_z(near, [(2, 0)])
    far_top = over_z(far[:cut], [(0, 2), (1, 3)])
    cross = add(cross, cross_came)
    near_came, cross, far, vec_rows, far_top = tie(near_came, cross, far, vec_rows, far_top)

    cross_came, far_low = over_z(cross, [(2, 1)]), over_z(with_rows(far[cut:], vec_rows), [(0, 2), (1, 3)])
    far_came = jnp.concatenate([far_top, far_low[: block - cut]])
    vec_rows = vec_rows + far_low[block - cut :].astype(F32)
    kept = jnp.where(at.z >= 2, far, jnp.where(at.z == 0, near, cross))
    came = jnp.where(at.z >= 2, far_came, jnp.where(at.z == 0, near_came, cross_came))
    grad_rows = kept.astype(F32) + came.astype(F32)
    start = VEC_ROW - 31 * block
    last = jnp.concatenate([grad_rows[:start], vec_rows, jnp.zeros((block - start - VECS, D), F32)])
    is_last = (lax.axis_index("dp") == 15) & (at.x == 1)
    return jnp.where(is_last, last, grad_rows), gm


def shards(custom, inputs, memory, lengths, matched, cotangent, weights):
    axes = ("dp", "seq")
    share = 1.0 / lax.axis_size("seq")
    images, queries, _ = inputs.shape
    tokens = memory.shape[1]
    block = weights.shape[1]
    at = Place()
    left = lengths - at.x * tokens
    flags = jnp.stack([at.c if custom else 0, at.x, at.y, at.z]).astype(jnp.int32)

    def parts_of(value):
        if custom:
            return [value, over_x(value)]
        gathered = lax.all_gather(value, "seq")
        return [gathered[n] for n in range(gathered.shape[0])]

    if custom:
        bufs = gather(at, weights[0])
    else:
        bufs = [lax.all_gather(weights[0], axes, axis=0, tiled=True)]
    xb = jnp.pad(inputs, ((0, 0), (0, QP - queries), (0, 0))).reshape(images * QP, D)
    qs, ks, vs, os, y1, qc, key, value, mixed, stat, *w = forward(left, flags, xb, memory, bufs, queries)
    w = w[0] if custom else bufs[0]
    vec = w[VEC_ROW : VEC_ROW + VECS].astype(F32)
    near_rows = 4 * D + QUERY_HEAD
    far_rows = 2 * FF - HEAD_ROWS + TAIL
    cross_rows = 4 * D - QUERY_HEAD + HEAD_ROWS
    far_shape = (2, 2, 2 * block, D) if custom else (far_rows, D)
    near_shape = (2, 2 * block, D) if custom else (near_rows, D)
    cross_shape = (2, 2 * block, D) if custom else (cross_rows, D)
    out, *grads, db, doc, tot, dvec_mid = middle(
        flags, y1, parts_of(mixed), parts_of(stat), w, vec, cotangent, matched, far_shape, cross_shape, custom
    )
    far, cross = grads[: 1 + custom], grads[1 + custom :]
    if custom:
        far_came = over_core(far[1])
    dq, dk, dv = cross_backward(left, qc, key, value, doc, tot)
    dq_parts = parts_of(dq)
    if custom:
        far = [far[0], far_came]
        dk, message = tie(dk, far_send(flags, *far))
        far_last = over_y(message)
    dcv_row, *cross = memory_weights(flags, cross, memory, dk, dv, custom)
    if custom:
        dcv_row = dcv_row + over_x(dcv_row)
    da, gq_head, dvec_query, *cross = query_backward(flags, cross, y1, db, dq_parts, w, vec, custom)
    if custom:
        cross_came = over_core(cross[1])
    gq_head, dcv_row = tie(gq_head, dcv_row)
    gx, dvec_self, *near = self_backward(
        flags, xb, qs, ks, vs, os, da, gq_head, w, queries, near_shape, custom
    )
    vec_rows = (dvec_mid + dvec_query + dvec_self) * (1.0 if custom else share)
    is_value_bias = jnp.arange(VECS)[:, None] == 4
    vec_rows = jnp.where(is_value_bias, dcv_row[0:1], vec_rows)
    if custom:
        far_last, near_send = tie(far_last, near[1])
        grad_rows, gm = finish(
            at, flags, block, far, far_last, near[0], near_send, cross[0], cross_came, vec_rows, (dk, dv, w)
        )
    else:
        gm = memory_grads(dk, dv, w)
        low_share = jnp.asarray(share, BF16)
        pad = lax.axis_size(axes) * block - VEC_ROW - VECS
        last = 2 * FF - HEAD_ROWS
        memory_rows = slice(D - QUERY_HEAD, 3 * D - QUERY_HEAD)
        grads = jnp.concatenate(
            [near[0] * low_share, cross[0][: memory_rows.start] * low_share, cross[0][memory_rows]]
            + [cross[0][memory_rows.stop :] * low_share, far[0][:last] * low_share]
            + [vec_rows.astype(BF16), jnp.zeros((pad, D), BF16)]
        )
        grad_rows = lax.psum_scatter(grads, axes, scatter_dimension=0, tiled=True).astype(F32)
    return out[:, :queries], gx[:, :queries], gm, grad_rows[None]


def solution(mesh):
    placed = (
        P("dp", None, None),
        P("dp", "seq", None),
        P("dp"),
        P("dp", None),
        P("dp", None, None),
        P(None, ("dp", "seq"), None),
    )
    custom = dict(mesh.shape) == {"dp": 16, "seq": 2}
    return jax.shard_map(
        partial(shards, custom),
        mesh=mesh,
        in_specs=placed,
        out_specs=(
            P("dp", None, None),
            P("dp", None, None),
            P("dp", "seq", None),
            P(None, ("dp", "seq"), None),
        ),
        check_vma=False,
    )
```

```python
from functools import partial

import jax
import jax.numpy as jnp
from jax import lax
from jax.experimental import pallas as pl
from jax.experimental.pallas import tpu as pltpu
from jax.sharding import PartitionSpec as P

D = 768
H = 12
HEAD = 64
FF = 3072
PAIRS = H // 2
LANES = 2 * HEAD
QP = 112
VEC_ROW = 8 * D + 2 * FF
VECS = 24
TAIL = 256
HEAD_ROWS = 128
QUERY_HEAD = 64
SCALE = HEAD ** (-0.5)
EPS = 1e-05
NEG = -1e30
F32 = jnp.float32
BF16 = jnp.bfloat16
MIB = 1024 * 1024


def dot_nn(a, b):
    return lax.dot_general(a, b, (((1,), (0,)), ((), ())), preferred_element_type=F32)


def dot_nt(a, b):
    return lax.dot_general(a, b, (((1,), (1,)), ((), ())), preferred_element_type=F32)


def dot_tn(a, b):
    return lax.dot_general(a, b, (((0,), (0,)), ((), ())), preferred_element_type=F32)


def norm_parts(v):
    center = v - jnp.mean(v, axis=-1, keepdims=True)
    inverse = lax.rsqrt(jnp.mean(center * center, axis=-1, keepdims=True) + EPS)
    return center * inverse, inverse


def norm_back(dy, hat, inverse, gain):
    scaled = dy * gain
    mean_one = jnp.mean(scaled, axis=-1, keepdims=True)
    mean_two = jnp.mean(scaled * hat, axis=-1, keepdims=True)
    return inverse * (scaled - mean_one - hat * mean_two)


def rowsum(v):
    return jnp.sum(v.astype(F32), axis=0, keepdims=True)


def head_masks():
    lane = lax.broadcasted_iota(jnp.int32, (1, LANES), 1)
    first = jnp.where(lane < HEAD, 1.0, 0.0)
    return first.astype(BF16), (1.0 - first).astype(BF16)


def two_heads(block, masks):
    return jnp.concatenate([block * masks[0], block * masks[1]], axis=0)


def join_heads(stacked):
    lane = lax.broadcasted_iota(jnp.int32, (QP, LANES), 1)
    return jnp.where(lane < HEAD, stacked[:QP], stacked[QP:])


def weight_block(index):
    return pl.BlockSpec((D, D), lambda *_: (index, 0))


def whole(shape):
    return pl.BlockSpec(shape, lambda *_: (0,) * len(shape))


def params(mib):
    return pltpu.CompilerParams(vmem_limit_bytes=mib * MIB)


def cost(flops, moved):
    return pl.CostEstimate(flops=flops // 1000, bytes_accessed=moved // 1000, transcendentals=0)


FIRST_BLOCKS = (0, 1, 2, 5, 6, 3, 4)
SPREAD = ((0, 0, 0), (0, 0, 1), (0, 1, 0), (1, 0, 0), (0, 1, 1), (1, 1, 0), (1, 0, 1), (1, 1, 1))
PAIR_ROWS = 784
HOLDER = (3, 1, 1, 1)


class Assembly:
    def __init__(self, flags, bufs, weights, seams, sems, vec_low, vec_sem):
        self.core, self.x, self.y, self.z = flags[0], flags[1], flags[2], flags[3]
        self.bufs, self.weights, self.seams, self.sems = bufs, weights, seams, sems
        self.vec_low, self.vec_sem = vec_low, vec_sem
        self.ready = set()

    def buf(self, dc, dz2, spread):
        return self.bufs[dc * 16 + dz2 * 8 + SPREAD.index(spread)]

    def start_vec(self):
        first = VEC_ROW - 15 * PAIR_ROWS - 400
        for dc in (0, 1):
            for dz2 in (0, 1):
                for dz1, dy, dx in SPREAD:
                    here = (self.z ^ (2 * dz2 + dz1), self.y ^ dy, self.core ^ dc, self.x ^ dx)
                    hit = (here[0] == HOLDER[0]) & (here[1] == HOLDER[1]) & (here[2] == HOLDER[2]) & (here[3] == HOLDER[3])

                    @pl.when(hit)
                    def _(source=self.buf(dc, dz2, (dz1, dy, dx))):
                        pltpu.make_async_copy(source.at[pl.ds(first, 32)], self.vec_low, self.vec_sem).start()

    def wait_vec(self):
        pltpu.make_async_copy(self.weights.at[pl.ds(0, 32)], self.vec_low, self.vec_sem).wait()

    def start_group(self, dz2):
        def rows(start, count):
            return pl.ds(pl.multiple_of(start, 16), count)

        for dz1 in (0, 1):
            for dy in (0, 1):
                for dc in (0, 1):
                    pair = (self.z ^ (2 * dz2 + dz1)) * 4 + (self.y ^ dy) * 2 + (self.core ^ dc)
                    base, sem = pair * PAIR_ROWS, self.sems.at[pair]
                    near, far = self.buf(dc, dz2, (dz1, dy, 0)), self.buf(dc, dz2, (dz1, dy, 1))
                    for source, x in ((near, self.x), (far, 1 - self.x)):
                        target = self.weights.at[rows(base + 400 * x, 384)]
                        pltpu.make_async_copy(source.at[pl.ds(0, 384)], target, sem).start()
                        pltpu.make_async_copy(source.at[pl.ds(384, 16)], self.seams.at[pair, x], sem).start()

    def start(self):
        self.start_vec()
        for low in (True, False):

            @pl.when((self.z < 2) == low)
            def _(low=low):
                for dz2 in (0, 1) if low else (1, 0):
                    self.start_group(dz2)

    def wait(self, pair):
        if pair not in self.ready:
            self.ready.add(pair)
            rows = self.weights.at[pl.ds(0, PAIR_ROWS + 16)]
            pltpu.make_async_copy(rows, rows, self.sems.at[pair]).wait()
            halves = [self.seams[pair, x].astype(F32)[:8] for x in (0, 1)]
            seam = pl.ds(pair * PAIR_ROWS + 384, 16)
            self.weights[seam, :] = jnp.concatenate(halves, axis=0).astype(BF16)

    def block(self, number):
        for pair in range(number * D // PAIR_ROWS, (number * D + D - 1) // PAIR_ROWS + 1):
            self.wait(pair)


class Direct:
    def __init__(self, w_hbm, weights, sems, vec_low, vec_sem):
        self.copies = {}
        for number in FIRST_BLOCKS:
            rows = pl.ds(number * D, D)
            self.copies[number] = pltpu.make_async_copy(w_hbm.at[rows], weights.at[rows], sems.at[number])
        self.vec = pltpu.make_async_copy(w_hbm.at[pl.ds(VEC_ROW, 32)], vec_low, vec_sem)
        self.ready = set()

    def start(self):
        self.vec.start()
        for number in FIRST_BLOCKS:
            self.copies[number].start()

    def wait_vec(self):
        self.vec.wait()

    def block(self, number):
        if number not in self.ready:
            self.ready.add(number)
            self.copies[number].wait()


def forward_kernel(queries, custom, left_ref, flags, xb_ref, m_hbm, *refs):
    count = 32 if custom else 1
    bufs, refs = refs[:count], refs[count:]
    qs_out, ks_out, vs_out, os_out, y1_out, qc_out, k_out, v_out, o_out, stat_ref = refs[:10]
    w_out = refs[10] if custom else None
    weights, m_ref, qs_ref, ks_ref, vs_ref, os_ref, y1_ref, qc_ref, k_ref, v_ref, o_ref, vec_low = refs[10 + custom : 22 + custom]
    seams, w_sems, m_sems, out_sems, kv_sems, vec_sem, all_sems = refs[22 + custom :]
    images = m_ref.shape[0]
    tokens = m_ref.shape[1]
    if custom:
        feed = Assembly(flags, bufs, weights, seams, w_sems, vec_low, vec_sem)
    else:
        feed = Direct(bufs[0], weights, w_sems, vec_low, vec_sem)

    def load_memory(image):
        return pltpu.make_async_copy(m_hbm.at[image], m_ref.at[image], m_sems.at[image])

    def matrix(block):
        feed.block(block)
        return weights[block * D : (block + 1) * D, :]

    def leave_weights(half):
        rows = pl.ds(half * 8 * PAIR_ROWS, 8 * PAIR_ROWS)
        return pltpu.make_async_copy(weights.at[rows], w_out.at[rows], all_sems.at[half])

    small = [(qs_ref, qs_out), (ks_ref, ks_out), (vs_ref, vs_out), (os_ref, os_out), (y1_ref, y1_out), (qc_ref, qc_out)]

    def leave(number):
        return pltpu.make_async_copy(*small[number], out_sems.at[number])

    def leave_image(image, number):
        source, target = [(k_ref, k_out), (v_ref, v_out), (o_ref, o_out)][number]
        return pltpu.make_async_copy(source.at[image], target.at[image], kv_sems.at[image, number])

    feed.start()
    for image in range(images):
        load_memory(image).start()
    feed.wait_vec()
    vec = vec_low[...].astype(F32)
    xb = xb_ref[...]
    qs_ref[...] = ((dot_nn(xb, matrix(0)) + vec[0:1, :]) * SCALE).astype(BF16)
    leave(0).start()
    ks_ref[...] = dot_nn(xb, matrix(1)).astype(BF16)
    leave(1).start()
    vs_ref[...] = (dot_nn(xb, matrix(2)) + vec[1:2, :]).astype(BF16)
    leave(2).start()
    masks = head_masks()
    real = lax.broadcasted_iota(jnp.int32, (2 * QP, QP), 1) < queries
    places = [(slice(i * QP, (i + 1) * QP), slice(p * LANES, (p + 1) * LANES)) for i in range(images) for p in range(PAIRS)]

    def raw_self(place):
        return dot_nt(two_heads(qs_ref[place], masks), ks_ref[place])

    following = raw_self(places[0])
    for number, place in enumerate(places):
        scores = following
        if number + 1 < len(places):
            following = raw_self(places[number + 1])
        scores = jnp.where(real, scores, NEG)
        probs = jnp.exp(scores - jnp.max(scores, axis=-1, keepdims=True))
        probs = probs / jnp.sum(probs, axis=-1, keepdims=True)
        os_ref[place] = join_heads(dot_nn(probs.astype(BF16), vs_ref[place])).astype(BF16)
    leave(3).start()
    y1 = xb.astype(F32) + (dot_nn(os_ref[...], matrix(3)) + vec[2:3, :])
    y1_ref[...] = y1
    leave(4).start()
    hat, _ = norm_parts(y1)
    x1 = hat * vec[11:12, :] + vec[12:13, :]
    qc_ref[...] = ((dot_nn(x1.astype(BF16), matrix(4)) + vec[3:4, :]) * SCALE).astype(BF16)
    leave(5).start()

    feed.block(5)
    feed.block(6)
    if custom:
        for pair in range(8):
            feed.wait(pair)
        leave_weights(0).start()
    column = lax.broadcasted_iota(jnp.int32, (2 * QP, 128), 1)
    for image in range(images):
        load_memory(image).wait()
        rows = slice(image * QP, (image + 1) * QP)
        k_ref[image] = dot_nn(m_ref[image], matrix(5)).astype(BF16)
        v_ref[image] = (dot_nn(m_ref[image], matrix(6)) + vec[4:5, :]).astype(BF16)
        leave_image(image, 0).start()
        leave_image(image, 1).start()
        valid = lax.broadcasted_iota(jnp.int32, (2 * QP, tokens), 1) < left_ref[image]
        stat = jnp.zeros((2 * QP, 128), F32)
        def raw(pair):
            lanes = slice(pair * LANES, (pair + 1) * LANES)
            return dot_nt(two_heads(qc_ref[rows, lanes], masks), k_ref[image, :, lanes])

        following = raw(0)
        for pair in range(PAIRS):
            lanes = slice(pair * LANES, (pair + 1) * LANES)
            scores = following
            if pair + 1 < PAIRS:
                following = raw(pair + 1)
            scores = jnp.where(valid, scores, NEG)
            top = jnp.max(scores, axis=-1, keepdims=True)
            probs = jnp.exp(scores - top)
            total = jnp.sum(probs, axis=-1, keepdims=True)
            mixed = dot_nn(probs.astype(BF16), v_ref[image, :, lanes]) / total
            o_ref[image, :, lanes] = join_heads(mixed).astype(BF16)
            stat = jnp.where(column == pair, top + jnp.log(total), stat)
        stat_ref[image] = jnp.where(left_ref[image] > 0, stat.T[:8], NEG)
        leave_image(image, 2).start()
        if custom and image == 0:
            for pair in range(8, 16):
                feed.wait(pair)
            leave_weights(1).start()
    for number in range(len(small)):
        leave(number).wait()
    for image in range(images):
        for number in range(3):
            leave_image(image, number).wait()
    if custom:
        leave_weights(0).wait()
        leave_weights(1).wait()


def forward(left, flags, xb, memory, bufs, queries):
    custom = len(bufs) > 1
    rows = xb.shape[0]
    images, tokens, _ = memory.shape
    narrow = jax.ShapeDtypeStruct((rows, D), BF16)
    tall = jax.ShapeDtypeStruct(memory.shape, BF16)
    anywhere = pl.BlockSpec(memory_space=pl.ANY)
    small = pltpu.VMEM((rows, D), BF16)
    large = pltpu.VMEM(memory.shape, BF16)
    held = 16 * PAIR_ROWS if custom else 7 * D
    return pl.pallas_call(
        partial(forward_kernel, queries, custom),
        grid_spec=pltpu.PrefetchScalarGridSpec(
            num_scalar_prefetch=2,
            grid=(1,),
            in_specs=[whole((rows, D)), anywhere] + [anywhere] * len(bufs),
            out_specs=[anywhere] * 9 + [whole((images, 8, 2 * QP))] + [anywhere] * custom,
            scratch_shapes=[
                pltpu.VMEM((held, D), BF16),
                large, small, small, small, small,
                pltpu.VMEM((rows, D), F32),
                small, large, large,
                pltpu.VMEM((images, QP, D), BF16),
                pltpu.VMEM((32, D), BF16),
                pltpu.VMEM((16, 2, 16, D), BF16),
                pltpu.SemaphoreType.DMA((16,)),
                pltpu.SemaphoreType.DMA((images,)),
                pltpu.SemaphoreType.DMA((6,)),
                pltpu.SemaphoreType.DMA((images, 3)),
                pltpu.SemaphoreType.DMA(()),
                pltpu.SemaphoreType.DMA((2,)),
            ],
        ),
        out_shape=[
            narrow, narrow, narrow, narrow,
            jax.ShapeDtypeStruct((rows, D), F32),
            narrow, tall, tall,
            jax.ShapeDtypeStruct((images, QP, D), BF16),
            jax.ShapeDtypeStruct((images, 8, 2 * QP), F32),
        ]
        + [jax.ShapeDtypeStruct((held, D), BF16)] * custom,
        cost_estimate=cost(0, 0),
        compiler_params=params(60),
        name="forward",
    )(left, flags, xb, memory, *bufs)


def pieces(start, count, size):
    found = []
    done = 0
    while done < count:
        pair, offset = divmod(start + done, size)
        length = min(count - done, size - offset)
        found.append((done, pair, offset, length))
        done += length
    return found


class Halves:
    def __init__(self, keep, send, my_core):
        self.keep, self.send, self.my_core = keep, send, my_core

    def copy(self, target, source, pair, offset, length, sem):
        place = pair // self.cores()
        index = []
        for extent in reversed(target.shape[:-2]):
            index.insert(0, place % extent)
            place = place // extent
        return pltpu.make_async_copy(source, target.at[(*index, pl.ds(offset, length))], sem)

    def cores(self):
        return 1 if self.send is None else 2

    def start(self, source, pair, offset, length, sem):
        if self.send is None:
            self.copy(self.keep, source, pair, offset, length, sem).start()
            return

        @pl.when(self.my_core == pair % 2)
        def _():
            self.copy(self.keep, source, pair, offset, length, sem).start()

        @pl.when(self.my_core != pair % 2)
        def _():
            self.copy(self.send, source, pair, offset, length, sem).start()

    def wait(self, source, pair, offset, length, sem):
        self.copy(self.keep, source, pair, offset, length, sem).wait()


def middle_kernel(parts, split, *refs):
    flags, y1_ref = refs[:2]
    o_refs, stat_refs = refs[2 : 2 + parts], refs[2 + parts : 2 + 2 * parts]
    refs = refs[2 + 2 * parts :]
    w_hbm, vec, cot_ref, match_ref, out_hbm = refs[:5]
    halves = Halves(refs[5], refs[6] if split else None, flags[0])
    refs = refs[6 + split :]
    cross_halves = Halves(refs[0], refs[1] if split else None, flags[0])
    refs = refs[1 + split :]
    db_ref, doc_ref, tot_ref, dvec_ref = refs[:4]
    ocf, ocb, y2, x2b, u, slope, acc, e3b, staged, blank, out_ref, dco_ref, co, feed = refs[4:18]
    sems, blank_sem, out_sem, side_sems, w_sems = refs[18:]
    phase, step = pl.program_id(0), pl.program_id(1)
    steps = FF // D
    images = match_ref.shape[0]
    column = lax.broadcasted_iota(jnp.int32, (2 * QP, 128), 1)
    lane = lax.broadcasted_iota(jnp.int32, (QP, LANES), 1)
    size = halves.keep.shape[-2]
    side = cross_halves.keep.shape[-2]

    def load(block):
        target = co if block == 7 else feed.at[block - 8]
        return pltpu.make_async_copy(w_hbm.at[pl.ds(block * D, D)], target, w_sems.at[block - 7])

    def leave_out():
        return pltpu.make_async_copy(out_ref, out_hbm, out_sem)

    def leave_side(act):
        starts = [(dco_ref, 3 * D - QUERY_HEAD, D), (staged.at[0, 0], 4 * D - QUERY_HEAD, HEAD_ROWS)]
        for which, (source, start, count) in enumerate(starts):
            if (which == 0) != (act[0] == "o"):
                continue
            for number, (done, pair, offset, length) in enumerate(pieces(start, count, side)):
                piece = source.at[pl.ds(done, length)]
                getattr(cross_halves, act[1])(piece, pair, offset, length, side_sems.at[which, number])

    def leave(which, at, act):
        skip = HEAD_ROWS if which + at == 0 else 0
        start = which * FF + at * D + skip - HEAD_ROWS
        for number, (done, pair, offset, length) in enumerate(pieces(start, D - skip, size)):
            source = staged.at[at % 2, which, pl.ds(done + skip, length)]
            getattr(halves, act)(source, pair, offset, length, sems.at[at, which, number])

    def leave_blank(act):
        for _, pair, offset, length in pieces(2 * FF - HEAD_ROWS, TAIL, size):
            getattr(halves, act)(blank, pair, offset, length, blank_sem)

    def ordered(first, second):
        if parts != 2:
            return first, second
        swap = flags[1] != 0
        return jnp.where(swap, second, first), jnp.where(swap, first, second)

    @pl.when((phase == 0) & (step == 0))
    def _():
        load(7).start()
        for at in range(steps):
            load(8 + at).start()
            load(8 + steps + at).start()
        for image in range(images):
            rows = slice(image * QP, (image + 1) * QP)
            stats = [ref[image] for ref in stat_refs]
            if parts == 2:
                stats = ordered(*stats)
            top = stats[0]
            for n in range(1, parts):
                top = jnp.maximum(top, stats[n])
            mass = [jnp.exp(stats[n] - top) for n in range(parts)]
            total = mass[0]
            for n in range(1, parts):
                total = total + mass[n]
            tot_ref[image, 0:8, :] = top + jnp.log(total)
            shares = [jnp.concatenate([m / total, jnp.zeros((120, 2 * QP), F32)], axis=0).T for m in mass]
            for pair in range(PAIRS):
                lanes = slice(pair * LANES, (pair + 1) * LANES)
                values = [ref[image, :, lanes].astype(F32) for ref in o_refs]
                if parts == 2:
                    values = ordered(*values)
                mixed = jnp.zeros((QP, LANES), F32)
                for n in range(parts):
                    share = shares[n][:, pair : pair + 1]
                    mixed = mixed + values[n] * jnp.where(lane < HEAD, share[:QP], share[QP:])
                ocf[rows, lanes] = mixed
        ocb[...] = ocf[...].astype(BF16)
        hat, _ = norm_parts(y1_ref[...])
        x1 = hat * vec[11:12, :] + vec[12:13, :]
        load(7).wait()
        total = x1 + (dot_nn(ocb[...], co[...]) + vec[5:6, :])
        y2[...] = total
        hat, _ = norm_parts(total)
        x2 = hat * vec[13:14, :] + vec[14:15, :]
        x2b[...] = x2.astype(BF16)
        acc[...] = x2 + vec[6:7, :]

    for at in range(steps):

        @pl.when((phase == 0) & (step == at))
        def _(at=at):
            load(8 + at).wait()
            load(8 + steps + at).wait()

    f1, f2 = feed.at[step], feed.at[steps + step]

    @pl.when(phase == 0)
    def _():
        h = dot_nt(x2b[...], f1[...]) + vec[pl.ds(7 + step, 1), :]
        root = 0.7978845608028654
        square = h * h
        t = jnp.tanh(root * (h + 0.044715 * (h * square)))
        half = 0.5 * (1.0 + t)
        slope[step] = half + (0.5 * root) * h * (1.0 - t * t) * (1.0 + 0.134145 * square)
        active = (h * half).astype(BF16)
        u[step] = active
        acc[...] += dot_nn(active, f2[...])

    @pl.when((phase == 1) & (step == 0))
    def _():
        blank[...] = jnp.zeros_like(blank)
        leave_blank("start")
        dvec_ref[...] = jnp.zeros_like(dvec_ref)
        hat, inverse = norm_parts(acc[...])
        out = hat * vec[15:16, :] + vec[16:17, :]
        grads = []
        for image in range(images):
            out_ref[image] = out[image * QP : (image + 1) * QP]
            matched = match_ref[image]
            hit = lax.broadcasted_iota(jnp.int32, (QP, matched.shape[1]), 0) == matched
            grads.append(dot_nn(jnp.where(hit, 1.0, 0.0).astype(BF16), cot_ref[image]))
        leave_out().start()
        dy = jnp.concatenate(grads, axis=0)
        dvec_ref[15:16, :] = rowsum(dy * hat)
        dvec_ref[16:17, :] = rowsum(dy)
        dc = norm_back(dy, hat, inverse, vec[15:16, :])
        low = dc.astype(BF16)
        e3b[...] = low
        dvec_ref[6:7, :] = rowsum(low)
        acc[...] = dc

    for at in range(2, steps):

        @pl.when((phase == 1) & (step == at))
        def _(at=at):
            leave(0, at - 2, "wait")
            leave(1, at - 2, "wait")
            if at == 2:
                leave_side(("f", "wait"))

    @pl.when(phase == 1)
    def _():
        du = dot_nt(e3b[...], f2[...])
        dh = (du * slope[step]).astype(BF16)
        slot = lax.rem(step, 2)
        staged[slot, 1] = dot_tn(u[step], e3b[...]).astype(BF16)
        staged[slot, 0] = dot_tn(dh, x2b[...]).astype(BF16)

        @pl.when(step == 0)
        def _():
            leave_side(("f", "start"))

        for at in range(steps):

            @pl.when(step == at)
            def _(at=at):
                leave(0, at, "start")
                leave(1, at, "start")

        dvec_ref[pl.ds(7 + step, 1), :] = rowsum(dh)
        acc[...] += dot_nn(dh, f1[...])

    @pl.when((phase == 1) & (step == steps - 1))
    def _():
        hat, inverse = norm_parts(y2[...])
        dy = acc[...]
        dvec_ref[13:14, :] = rowsum(dy * hat)
        dvec_ref[14:15, :] = rowsum(dy)
        db = norm_back(dy, hat, inverse, vec[13:14, :])
        db_ref[...] = db
        low = db.astype(BF16)
        dvec_ref[5:6, :] = rowsum(low)
        dco_ref[...] = dot_tn(ocb[...], low).astype(BF16)
        leave_side(("o", "start"))
        doc = dot_nt(low, co[...]).astype(BF16)
        doc_ref[...] = doc
        both = doc.astype(F32) * ocf[...]
        for image in range(images):
            rows = slice(image * QP, (image + 1) * QP)
            tot = jnp.zeros((2 * QP, 128), F32)
            for pair in range(PAIRS):
                piece = both[rows, pair * LANES : (pair + 1) * LANES]
                one = jnp.sum(jnp.where(lane < HEAD, piece, 0.0), axis=-1, keepdims=True)
                two = jnp.sum(jnp.where(lane < HEAD, 0.0, piece), axis=-1, keepdims=True)
                tot = jnp.where(column == pair, jnp.concatenate([one, two], axis=0), tot)
            tot_ref[image, 8:16, :] = tot.T[:8]
        leave_blank("wait")
        leave_out().wait()
        leave_side(("o", "wait"))
        for which in (0, 1):
            leave(which, steps - 2, "wait")
            leave(which, steps - 1, "wait")


def halves_shape(shape, split):
    return [jax.ShapeDtypeStruct(shape, BF16)] * (1 + split)


def middle(flags, y1, o_parts, stat_parts, w, vec, cot, matched, far_shape, cross_shape, split):
    rows = y1.shape[0]
    images = cot.shape[0]
    steps = FF // D
    parts = len(o_parts)
    anywhere = pl.BlockSpec(memory_space=pl.ANY)
    return pl.pallas_call(
        partial(middle_kernel, parts, split),
        grid_spec=pltpu.PrefetchScalarGridSpec(
            num_scalar_prefetch=1,
            grid=(2, steps),
            in_specs=[whole(y1.shape)]
            + [whole(o_parts[0].shape)] * parts
            + [whole(stat_parts[0].shape)] * parts
            + [anywhere, whole((VECS, D)), whole(cot.shape), whole((images, 1, matched.shape[1]))],
            out_specs=[anywhere] * (3 + 2 * split)
            + [
                whole((rows, D)),
                whole((rows, D)),
                whole((images, 16, 2 * QP)),
                whole((VECS, D)),
            ],
            scratch_shapes=[
                pltpu.VMEM((rows, D), F32),
                pltpu.VMEM((rows, D), BF16),
                pltpu.VMEM((rows, D), F32),
                pltpu.VMEM((rows, D), BF16),
                pltpu.VMEM((steps, rows, D), BF16),
                pltpu.VMEM((steps, rows, D), F32),
                pltpu.VMEM((rows, D), F32),
                pltpu.VMEM((rows, D), BF16),
                pltpu.VMEM((2, 2, D, D), BF16),
                pltpu.VMEM((TAIL, D), BF16),
                pltpu.VMEM((images, QP, D), F32),
                pltpu.VMEM((D, D), BF16),
                pltpu.VMEM((D, D), BF16),
                pltpu.VMEM((2 * steps, D, D), BF16),
                pltpu.SemaphoreType.DMA((steps, 2, 2)),
                pltpu.SemaphoreType.DMA(()),
                pltpu.SemaphoreType.DMA(()),
                pltpu.SemaphoreType.DMA((2, 2)),
                pltpu.SemaphoreType.DMA((1 + 2 * steps,)),
            ],
        ),
        out_shape=[jax.ShapeDtypeStruct((images, QP, D), F32)]
        + halves_shape(far_shape, split)
        + halves_shape(cross_shape, split)
        + [
            jax.ShapeDtypeStruct((rows, D), F32),
            jax.ShapeDtypeStruct((rows, D), BF16),
            jax.ShapeDtypeStruct((images, 16, 2 * QP), F32),
            jax.ShapeDtypeStruct((VECS, D), F32),
        ],
        cost_estimate=cost(2 * rows * D * (6 * FF + 3 * D), 2 * FF * D * 6),
        compiler_params=params(60),
        name="middle",
    )(flags, y1, *o_parts, *stat_parts, w, vec, cot, matched[:, None, :])


def cross_backward_kernel(left_ref, q_ref, k_ref, v_ref, do_ref, tot_ref, dq_ref, dk_ref, dv_ref):
    tokens = k_ref.shape[1]
    masks = head_masks()
    valid = lax.broadcasted_iota(jnp.int32, (tokens, 2 * QP), 0) < left_ref[pl.program_id(0)]
    def raw(pair):
        lanes = slice(pair * LANES, (pair + 1) * LANES)
        query = two_heads(q_ref[0, :, lanes], masks)
        dout = two_heads(do_ref[0, :, lanes], masks)
        return query, dout, dot_nt(k_ref[0, :, lanes], query), dot_nt(v_ref[0, :, lanes], dout)

    following = raw(0)
    for pair in range(PAIRS):
        lanes = slice(pair * LANES, (pair + 1) * LANES)
        query, dout, scores, dprobs = following
        if pair + 1 < PAIRS:
            following = raw(pair + 1)
        probs = jnp.where(valid, jnp.exp(scores - tot_ref[0, pair : pair + 1, :]), 0.0)
        dscores = (probs * (dprobs - tot_ref[0, 8 + pair : 9 + pair, :])).astype(BF16)
        dv_ref[0, :, lanes] = dot_nn(probs.astype(BF16), dout).astype(BF16)
        dk_ref[0, :, lanes] = dot_nn(dscores, query).astype(BF16)
        dq_ref[0, :, lanes] = join_heads(dot_tn(k_ref[0, :, lanes], dscores).T).astype(BF16)


def cross_backward(left, qc, key, value, doc, tot):
    images, tokens, _ = key.shape
    q_block = pl.BlockSpec((1, QP, D), lambda i, _: (i, 0, 0))
    m_block = pl.BlockSpec((1, tokens, D), lambda i, _: (i, 0, 0))
    s_block = pl.BlockSpec((1, 16, 2 * QP), lambda i, _: (i, 0, 0))
    return pl.pallas_call(
        cross_backward_kernel,
        grid_spec=pltpu.PrefetchScalarGridSpec(
            num_scalar_prefetch=1,
            grid=(images,),
            in_specs=[q_block, m_block, m_block, q_block, s_block],
            out_specs=[q_block, m_block, m_block],
        ),
        out_shape=[
            jax.ShapeDtypeStruct((images, QP, D), BF16),
            jax.ShapeDtypeStruct(key.shape, BF16),
            jax.ShapeDtypeStruct(key.shape, BF16),
        ],
        cost_estimate=cost(4 * images * 2 * QP * tokens * D // 3, images * tokens * D * 8),
        compiler_params=params(60),
        name="cross_backward",
    )(left, qc.reshape(images, QP, D), key, value, doc.reshape(images, QP, D), tot)


def memory_weights_kernel(split, flags, *refs):
    m_ref, dk_ref, dv_ref = refs[1 + split : 4 + split]
    refs = refs[4 + split :]
    gb_ref = refs[0]
    halves = Halves(refs[1], refs[2] if split else None, flags[0])
    low, sems = refs[2 + split :]
    def leave(which, act):
        start = (1 + which) * D - QUERY_HEAD
        for number, (done, pair, offset, length) in enumerate(pieces(start, D, halves.keep.shape[-2])):
            piece = low.at[which, pl.ds(done, length)]
            getattr(halves, act)(piece, pair, offset, length, sems.at[which, number])

    tall = m_ref[...].reshape(-1, D)
    for which, ref in ((0, dk_ref), (1, dv_ref)):
        low[which] = dot_tn(tall, ref[...].reshape(-1, D)).astype(BF16)
        leave(which, "start")
    gb_ref[...] = jnp.broadcast_to(rowsum(dv_ref[...].reshape(-1, D)), gb_ref.shape)
    for which in (0, 1):
        leave(which, "wait")


def memory_weights(flags, cross, memory, dk, dv, split):
    images, tokens, _ = memory.shape
    block = whole(memory.shape)
    anywhere = pl.BlockSpec(memory_space=pl.ANY)
    return pl.pallas_call(
        partial(memory_weights_kernel, split),
        grid_spec=pltpu.PrefetchScalarGridSpec(
            num_scalar_prefetch=1,
            grid=(1,),
            in_specs=[anywhere] * (1 + split) + [block, block, block],
            out_specs=[whole((8, D))] + [anywhere] * (1 + split),
            scratch_shapes=[
                pltpu.VMEM((2, D, D), BF16),
                pltpu.SemaphoreType.DMA((2, 2)),
            ],
        ),
        out_shape=[jax.ShapeDtypeStruct((8, D), F32)] + halves_shape(cross[0].shape, split),
        input_output_aliases={1 + n: 1 + n for n in range(1 + split)},
        cost_estimate=cost(4 * images * tokens * D * D, images * tokens * D * 6),
        compiler_params=params(60),
        name="memory_weights",
    )(flags, *cross, memory, dk, dv)


def memory_grads_kernel(dk_ref, dv_ref, ck, cv, gm_ref):
    gm_ref[0] = dot_nt(dk_ref[0], ck[...]) + dot_nt(dv_ref[0], cv[...])


def memory_grads(dk, dv, w):
    images, tokens, _ = dk.shape
    block = pl.BlockSpec((1, tokens, D), lambda i: (i, 0, 0))
    return pl.pallas_call(
        memory_grads_kernel,
        grid=(images,),
        in_specs=[block, block, weight_block(5), weight_block(6)],
        out_specs=block,
        out_shape=jax.ShapeDtypeStruct(dk.shape, F32),
        cost_estimate=pl.CostEstimate(
            flops=4 * images * tokens * D * D, bytes_accessed=images * tokens * D * 8, transcendentals=0
        ),
        compiler_params=params(60),
        name="memory_grads",
    )(dk, dv, w, w)


class Loads:
    def __init__(self, pairs, sems):
        self.copies = [(pltpu.make_async_copy(source, target, sems.at[n]), target) for n, (source, target) in enumerate(pairs)]
        self.ready = set()
        for copy, _ in self.copies:
            copy.start()

    def __call__(self, number):
        copy, target = self.copies[number]
        if number not in self.ready:
            copy.wait()
            self.ready.add(number)
        return target[...]


def query_backward_kernel(parts, split, flags, *refs):
    sources, vec = refs[1 + split : 4 + split + parts], refs[4 + split + parts]
    refs = refs[5 + split + parts :]
    da_ref, gq_head_ref, dvec_ref = refs[:3]
    halves = Halves(refs[3], refs[4] if split else None, flags[0])
    refs = refs[4 + split :]
    targets, staged, load_sems, sems = refs[: 3 + parts], refs[3 + parts], refs[4 + parts], refs[5 + parts]
    w_hbm = sources[-1]
    sources = [*sources[:-1], w_hbm.at[pl.ds(4 * D, D)]]
    get = Loads(list(zip(sources, targets)), load_sems)

    def leave(act):
        for number, (done, pair, offset, length) in enumerate(pieces(0, D - QUERY_HEAD, halves.keep.shape[-2])):
            piece = staged.at[pl.ds(done + QUERY_HEAD, length)]
            getattr(halves, act)(piece, pair, offset, length, sems.at[number])

    total = get(0).astype(F32)
    for number in range(1, parts):
        total = total + get(number).astype(F32)
    dq = total.astype(BF16) * SCALE
    hat, inverse = norm_parts(get(parts))
    gain = vec[11:12, :]
    x1b = (hat * gain + vec[12:13, :]).astype(BF16)
    gcq = dot_tn(x1b, dq).astype(BF16)
    staged[...] = gcq
    leave("start")
    gq_head_ref[...] = gcq[:QUERY_HEAD]
    dvec_ref[...] = jnp.zeros_like(dvec_ref)
    dvec_ref[3:4, :] = rowsum(dq)
    dy = get(parts + 1) + dot_nt(dq, get(parts + 2))
    dvec_ref[11:12, :] = rowsum(dy * hat)
    dvec_ref[12:13, :] = rowsum(dy)
    da = norm_back(dy, hat, inverse, gain)
    da_ref[...] = da
    dvec_ref[2:3, :] = rowsum(da.astype(BF16))
    leave("wait")


def query_backward(flags, cross, y1, db, dq_parts, w, vec, split):
    rows = y1.shape[0]
    parts = len(dq_parts)
    full = whole((rows, D))
    anywhere = pl.BlockSpec(memory_space=pl.ANY)
    return pl.pallas_call(
        partial(query_backward_kernel, parts, split),
        grid_spec=pltpu.PrefetchScalarGridSpec(
            num_scalar_prefetch=1,
            grid=(1,),
            in_specs=[anywhere] * (4 + split + parts) + [whole((VECS, D))],
            out_specs=[full, whole((QUERY_HEAD, D)), whole((VECS, D))] + [anywhere] * (1 + split),
            scratch_shapes=[pltpu.VMEM((rows, D), BF16)] * parts
            + [pltpu.VMEM((rows, D), F32)] * 2
            + [pltpu.VMEM((D, D), BF16)] * 2
            + [pltpu.SemaphoreType.DMA((parts + 3,)), pltpu.SemaphoreType.DMA((2,))],
        ),
        out_shape=[
            jax.ShapeDtypeStruct((rows, D), F32),
            jax.ShapeDtypeStruct((QUERY_HEAD, D), BF16),
            jax.ShapeDtypeStruct((VECS, D), F32),
        ]
        + halves_shape(cross[0].shape, split),
        input_output_aliases={1 + n: 3 + n for n in range(1 + split)},
        cost_estimate=cost(4 * rows * D * D, rows * D * 16),
        compiler_params=params(60),
        name="query_backward",
    )(flags, *cross, *[part.reshape(rows, D) for part in dq_parts], y1, db, w, vec)


def self_backward_kernel(queries, split, *refs):
    flags, os_hbm, da_hbm, qs_hbm, ks_hbm, vs_hbm, x_hbm, w_hbm, gq_ref, gx_ref, dvec_ref, keep_ref = refs[:12]
    halves = Halves(keep_ref, refs[12] if split else None, flags[0])
    sq, sk, sv, g_ref, os_ref, da_ref, ao, qs, ks, vs, x_ref, aq, ak, av, sems, load_sems = refs[12 + split :]
    size = keep_ref.shape[-2]
    matrices = [w_hbm.at[pl.ds(block * D, D)] for block in range(4)]
    get = Loads(
        [(os_hbm, os_ref), (da_hbm, da_ref), (matrices[3], ao), (qs_hbm, qs), (ks_hbm, ks), (vs_hbm, vs)]
        + [(x_hbm, x_ref), (matrices[0], aq), (matrices[1], ak), (matrices[2], av)],
        load_sems,
    )

    def leave(pair, act):
        getattr(halves, act)(g_ref.at[pl.ds(pair * size, size)], pair, 0, size, sems.at[pair])

    pairs = g_ref.shape[0] // size
    images = x_ref.shape[0] // QP
    dvec_ref[...] = jnp.zeros_like(dvec_ref)
    os = get(0)
    da = get(1)
    low = da.astype(BF16)
    g_ref[4 * D :, :] = gq_ref[...]
    g_ref[3 * D : 4 * D, :] = dot_tn(os, low).astype(BF16)
    dos = dot_nt(low, get(2)).astype(BF16)
    for number in (3, 4, 5):
        get(number)
    masks = head_masks()
    real = lax.broadcasted_iota(jnp.int32, (QP, 2 * QP), 0) < queries
    places = [(slice(i * QP, (i + 1) * QP), slice(p * LANES, (p + 1) * LANES)) for i in range(images) for p in range(PAIRS)]

    def raw(place):
        query = two_heads(qs[place], masks)
        dout = two_heads(dos[place], masks)
        return query, dout, dot_nt(ks[place], query), dot_nt(vs[place], dout)

    following = raw(places[0])
    for number, place in enumerate(places):
        query, dout, scores, dprobs = following
        if number + 1 < len(places):
            following = raw(places[number + 1])
        scores = jnp.where(real, scores, NEG)
        probs = jnp.exp(scores - jnp.max(scores, axis=0, keepdims=True))
        probs = probs / jnp.sum(probs, axis=0, keepdims=True)
        dscores = (probs * (dprobs - jnp.sum(probs * dprobs, axis=0, keepdims=True))).astype(BF16)
        sv[place] = dot_nn(probs.astype(BF16), dout).astype(BF16)
        sk[place] = dot_nn(dscores, query).astype(BF16)
        sq[place] = join_heads(dot_tn(ks[place], dscores).T).astype(BF16) * SCALE
    dvec_ref[0:1, :] = rowsum(sq[...])
    dvec_ref[1:2, :] = rowsum(sv[...])
    xb = get(6)
    g_ref[2 * D : 3 * D, :] = dot_tn(xb, sv[...]).astype(BF16)
    for pair in range(2, pairs):
        leave(pair, "start")
    g_ref[D : 2 * D, :] = dot_tn(xb, sk[...]).astype(BF16)
    for pair in range(1, min(2, pairs)):
        leave(pair, "start")
    g_ref[0:D, :] = dot_tn(xb, sq[...]).astype(BF16)
    leave(0, "start")
    gx = da + dot_nt(sq[...], get(7)) + dot_nt(sk[...], get(8)) + dot_nt(sv[...], get(9))
    for image in range(images):
        gx_ref[image] = gx[image * QP : (image + 1) * QP]
    for pair in range(pairs):
        leave(pair, "wait")


def self_backward(flags, xb, qs, ks, vs, os, da, gq_head, w, queries, shape, split):
    rows = xb.shape[0]
    images = rows // QP
    anywhere = pl.BlockSpec(memory_space=pl.ANY)
    return pl.pallas_call(
        partial(self_backward_kernel, queries, split),
        grid_spec=pltpu.PrefetchScalarGridSpec(
            num_scalar_prefetch=1,
            grid=(1,),
            in_specs=[anywhere] * 7 + [whole((QUERY_HEAD, D))],
            out_specs=[whole((images, QP, D)), whole((VECS, D))] + [anywhere] * (1 + split),
            scratch_shapes=[pltpu.VMEM((rows, D), BF16)] * 3
            + [pltpu.VMEM((4 * D + QUERY_HEAD, D), BF16), pltpu.VMEM((rows, D), BF16), pltpu.VMEM((rows, D), F32)]
            + [pltpu.VMEM((D, D), BF16)]
            + [pltpu.VMEM((rows, D), BF16)] * 4
            + [pltpu.VMEM((D, D), BF16)] * 3
            + [pltpu.SemaphoreType.DMA((4,)), pltpu.SemaphoreType.DMA((10,))],
        ),
        out_shape=[
            jax.ShapeDtypeStruct((images, QP, D), F32),
            jax.ShapeDtypeStruct((VECS, D), F32),
        ]
        + halves_shape(shape, split),
        cost_estimate=cost(16 * rows * D * D * 2, 8 * D * D * 2),
        compiler_params=params(60),
        name="self_backward",
    )(flags, os, da, qs, ks, vs, xb, w, gq_head)


class Place:
    def __init__(self):
        place = lax.axis_index("dp")
        self.x = lax.axis_index("seq")
        self.c = lax.rem(place, 2)
        self.y = lax.rem(place // 2, 2)
        self.z = place // 4


def pick(array, index, axis):
    return lax.dynamic_index_in_dim(array, index, axis, keepdims=False)


def over_core(v):
    return lax.ppermute(v, "dp", [(i, i ^ 1) for i in range(16)])


def over_y(v):
    return lax.ppermute(v, "dp", [(i, i ^ 2) for i in range(16)])


def over_x(v):
    return lax.ppermute(v, "seq", [(0, 1), (1, 0)])


def over_z(v, hops):
    return lax.ppermute(v, "dp", [(4 * a + i, 4 * b + i) for a, b in hops for i in range(4)])


def over_far(v):
    return over_z(v, [(0, 2), (2, 0), (1, 3), (3, 1)])


def over_near(v):
    return over_z(v, SWAP_ONE)


def spread(own):
    x, y, z = over_x(own), over_y(own), over_near(own)
    xy, yz, zx = over_x(y), over_y(z), over_near(x)
    return own, x, y, z, xy, yz, zx


def gather(at, rows):
    rest = jnp.zeros((8, D), BF16)
    own = jnp.where(at.x == 0, jnp.concatenate([rows, rest]), jnp.concatenate([rows[8:], rows[:8], rest]))
    other = over_far(own)
    here, there = spread(own), spread(other)
    found = [*here, over_x(here[5]), *there, over_y(there[6])]
    return found + [over_core(part) for part in found]


def tie(*values):
    return lax.optimization_barrier(values)


def add(kept, came):
    return (kept.astype(F32) + came.astype(F32)).astype(BF16)


def own_half(pairs, x):
    half = pairs.shape[-2] // 2
    return pick(pairs.reshape(*pairs.shape[:-2], 2, half, D), x, pairs.ndim - 2)


def blocks_of(pairs):
    return pairs.reshape(*pairs.shape[:-2], 2, pairs.shape[-2] // 2, D)


def picked(pairs, half, x):
    return pick(pick(pairs, half, 0), x, 0)


def merge(body, flags, sources, out_rows, name):
    parts = 2
    specs = []
    for array, where in sources:
        lead = (None,) * (array.ndim - 2)
        shape = (*lead, array.shape[-2], D // parts)
        specs.append(pl.BlockSpec(shape, lambda i, f, where=where: (*where(f), 0, i)))
    return pl.pallas_call(
        body,
        grid_spec=pltpu.PrefetchScalarGridSpec(
            num_scalar_prefetch=1,
            grid=(parts,),
            in_specs=specs,
            out_specs=[
                pl.BlockSpec((*rows, D // parts), lambda i, f, n=len(rows): (*[0] * n, i)) for rows in out_rows
            ],
        ),
        out_shape=[jax.ShapeDtypeStruct((*rows, D), BF16) for rows in out_rows],
        cost_estimate=cost(0, 0),
        compiler_params=params(60),
        name=name,
    )(flags, *[array for array, _ in sources])


def far_send_kernel(flags, a, b, c, d, out):
    out[0] = add(a[...], b[...])
    out[1] = add(c[...], d[...])


def far_send(flags, kept, came):
    kept, came = blocks_of(kept), blocks_of(came)
    sources = []
    for r in (0, 1):
        sources += [(part, lambda f, r=r: (r, 1 - f[2], f[1])) for part in (kept, came)]
    return merge(far_send_kernel, flags, sources, [(2, kept.shape[-2])], "far_send")[0]


def cross_merge_kernel(flags, *refs):
    ins, outs = refs[:8], refs[8:]
    outs[0][...] = add(ins[0][...], ins[1][...])
    outs[1][...] = add(ins[2][...], ins[3][...])
    message = outs[2]
    block = ins[4].shape[0]
    spill = message.shape[0] - (block + 8)
    main = ins[4][...].astype(F32) + ins[5][...].astype(F32)
    total = ins[6][...].astype(F32) + ins[7][...].astype(F32)
    gap = jnp.zeros((8, total.shape[1]), F32)
    message[...] = jnp.concatenate([main, gap, total[block - spill :]], axis=0).astype(BF16)


def cross_merge(flags, cross, cross_came):
    cross, cross_came = blocks_of(cross), blocks_of(cross_came)
    block = cross.shape[-2]
    spill = 2 * block - (D - QUERY_HEAD)
    chosen = [
        lambda f: (0, f[1]),
        lambda f: (1, f[1]),
        lambda f: (1 - f[0], 1 - f[1]),
        lambda f: (0, 1 - f[1]),
    ]
    sources = []
    for where in chosen:
        sources += [(cross, where), (cross_came, where)]
    return merge(cross_merge_kernel, flags, sources, [(block,)] * 2 + [(block + 8 + spill,)], "cross_merge")


def far_merge_kernel(flags, *refs):
    ins, outs = refs[:6], refs[6:]
    for number in range(2):
        first, second, third = ins[3 * number : 3 * number + 3]
        outs[number][...] = (first[...].astype(F32) + second[...].astype(F32) + third[...].astype(F32)).astype(BF16)


def far_merge(flags, far, far_came, far_last):
    far, far_came = blocks_of(far), blocks_of(far_came)
    sources = []
    for r in (lambda f: 1 - f[3] % 2, lambda f: f[3] % 2):
        sources += [(part, lambda f, r=r: (r(f), f[2], f[1])) for part in (far, far_came)]
        sources += [(far_last, lambda f, r=r: (r(f),))]
    return merge(far_merge_kernel, flags, sources, [(far.shape[-2],)] * 2, "far_merge")


def cross_second(at, mine, came):
    start = D - QUERY_HEAD
    block = mine[0].shape[-2]
    spill = 2 * block - start
    main = came[:block].astype(F32)
    tall = jnp.concatenate([jnp.zeros((block - spill, D), F32), came[block + 8 :].astype(F32)])
    ids = (at.c * 2 + at.x) * block + jnp.arange(block)[:, None]

    def half(index, y):
        part = jnp.where((at.c == 0) & (y == 0), tall, main)
        place = ids + y * 4 * block
        shared = (place >= start) & (place < start + 2 * D)
        own = jnp.where(index == 0, mine[0], mine[1]).astype(F32)
        return (own + jnp.where(shared, part, 0.0)).astype(BF16)

    return half(1 - at.y, 1 - at.y), half(at.y, at.y)


SWAP_ONE = [(0, 1), (1, 0), (2, 3), (3, 2)]
SWAP_TWO = [(0, 2), (2, 0), (1, 3), (3, 1)]


def with_rows(message, vec_rows):
    return jnp.concatenate([message, vec_rows.astype(BF16)])


def finish(at, flags, block, far, far_last, near, near_send, cross, cross_came, vec_rows, extra):
    near_came = over_core(near_send)
    vec_came = over_core(vec_rows)
    low, high, message = cross_merge(flags, cross, cross_came)
    near_came, message, low, high = tie(near_came, message, low, high)
    came = over_x(message)
    near, near_came = blocks_of(near), blocks_of(near_came)
    near_send = add(picked(near, 1 - at.y, at.x), picked(near_came, 1 - at.y, at.x))
    vec_rows = vec_rows + vec_came
    near_send, near, near_kept, dk, dv, w, far_last = tie(near_send, near, near_came, *extra, far_last)
    far_out, far = far_merge(flags, *far, far_last)
    near_came, far_came, vec_came = over_y(near_send), over_z(far_out, SWAP_ONE), over_y(vec_rows)
    gm = memory_grads(dk, dv, w)
    gm, came = tie(gm, came)
    send, cross = cross_second(at, (low, high), came)
    send, near_came, vec_came, cross = tie(send, near_came, vec_came, cross)

    near = picked(near, at.y, at.x).astype(F32) + picked(near_kept, at.y, at.x).astype(F32)
    near = (near + near_came.astype(F32)).astype(BF16)
    vec_rows = vec_rows + vec_came
    near, vec_rows, send = tie(near, vec_rows, send)
    cross_came, near_came, vec_came = over_y(send), over_z(near, [(3, 2), (1, 0)]), over_z(vec_rows, SWAP_ONE)
    cross = add(cross, cross_came)
    near = add(near, near_came)
    far = add(far, far_came)
    vec_rows = vec_rows + vec_came
    near, cross, vec_rows, far = tie(near, cross, vec_rows, far)

    cut = block // 16 * 8
    cross_came, near_came = over_z(cross, [(3, 2), (0, 1)]), over_z(near, [(2, 0)])
    far_top = over_z(far[:cut], [(0, 2), (1, 3)])
    cross = add(cross, cross_came)
    near_came, cross, far, vec_rows, far_top = tie(near_came, cross, far, vec_rows, far_top)

    cross_came, far_low = over_z(cross, [(2, 1)]), over_z(with_rows(far[cut:], vec_rows), [(0, 2), (1, 3)])
    far_came = jnp.concatenate([far_top, far_low[: block - cut]])
    vec_rows = vec_rows + far_low[block - cut :].astype(F32)
    kept = jnp.where(at.z >= 2, far, jnp.where(at.z == 0, near, cross))
    came = jnp.where(at.z >= 2, far_came, jnp.where(at.z == 0, near_came, cross_came))
    grad_rows = kept.astype(F32) + came.astype(F32)
    start = VEC_ROW - 31 * block
    last = jnp.concatenate([grad_rows[:start], vec_rows, jnp.zeros((block - start - VECS, D), F32)])
    is_last = (lax.axis_index("dp") == 15) & (at.x == 1)
    return jnp.where(is_last, last, grad_rows), gm


def shards(custom, inputs, memory, lengths, matched, cotangent, weights):
    axes = ("dp", "seq")
    share = 1.0 / lax.axis_size("seq")
    images, queries, _ = inputs.shape
    tokens = memory.shape[1]
    block = weights.shape[1]
    at = Place()
    left = lengths - at.x * tokens
    flags = jnp.stack([at.c if custom else 0, at.x, at.y, at.z]).astype(jnp.int32)

    def parts_of(value):
        if custom:
            return [value, over_x(value)]
        gathered = lax.all_gather(value, "seq")
        return [gathered[n] for n in range(gathered.shape[0])]

    if custom:
        bufs = gather(at, weights[0])
    else:
        bufs = [lax.all_gather(weights[0], axes, axis=0, tiled=True)]
    xb = jnp.pad(inputs, ((0, 0), (0, QP - queries), (0, 0))).reshape(images * QP, D)
    qs, ks, vs, os, y1, qc, key, value, mixed, stat, *w = forward(left, flags, xb, memory, bufs, queries)
    w = w[0] if custom else bufs[0]
    vec = w[VEC_ROW : VEC_ROW + VECS].astype(F32)
    near_rows = 4 * D + QUERY_HEAD
    far_rows = 2 * FF - HEAD_ROWS + TAIL
    cross_rows = 4 * D - QUERY_HEAD + HEAD_ROWS
    far_shape = (2, 2, 2 * block, D) if custom else (far_rows, D)
    near_shape = (2, 2 * block, D) if custom else (near_rows, D)
    cross_shape = (2, 2 * block, D) if custom else (cross_rows, D)
    out, *grads, db, doc, tot, dvec_mid = middle(
        flags, y1, parts_of(mixed), parts_of(stat), w, vec, cotangent, matched, far_shape, cross_shape, custom
    )
    far, cross = grads[: 1 + custom], grads[1 + custom :]
    if custom:
        far_came = over_core(far[1])
    dq, dk, dv = cross_backward(left, qc, key, value, doc, tot)
    dq_parts = parts_of(dq)
    if custom:
        far = [far[0], far_came]
        dk, message = tie(dk, far_send(flags, *far))
        far_last = over_y(message)
    dcv_row, *cross = memory_weights(flags, cross, memory, dk, dv, custom)
    if custom:
        dcv_row = dcv_row + over_x(dcv_row)
    da, gq_head, dvec_query, *cross = query_backward(flags, cross, y1, db, dq_parts, w, vec, custom)
    if custom:
        cross_came = over_core(cross[1])
    gq_head, dcv_row = tie(gq_head, dcv_row)
    gx, dvec_self, *near = self_backward(
        flags, xb, qs, ks, vs, os, da, gq_head, w, queries, near_shape, custom
    )
    vec_rows = (dvec_mid + dvec_query + dvec_self) * (1.0 if custom else share)
    is_value_bias = jnp.arange(VECS)[:, None] == 4
    vec_rows = jnp.where(is_value_bias, dcv_row[0:1], vec_rows)
    if custom:
        far_last, near_send = tie(far_last, near[1])
        grad_rows, gm = finish(
            at, flags, block, far, far_last, near[0], near_send, cross[0], cross_came, vec_rows, (dk, dv, w)
        )
    else:
        gm = memory_grads(dk, dv, w)
        low_share = jnp.asarray(share, BF16)
        pad = lax.axis_size(axes) * block - VEC_ROW - VECS
        last = 2 * FF - HEAD_ROWS
        memory_rows = slice(D - QUERY_HEAD, 3 * D - QUERY_HEAD)
        grads = jnp.concatenate(
            [near[0] * low_share, cross[0][: memory_rows.start] * low_share, cross[0][memory_rows]]
            + [cross[0][memory_rows.stop :] * low_share, far[0][:last] * low_share]
            + [vec_rows.astype(BF16), jnp.zeros((pad, D), BF16)]
        )
        grad_rows = lax.psum_scatter(grads, axes, scatter_dimension=0, tiled=True).astype(F32)
    return out[:, :queries], gx[:, :queries], gm, grad_rows[None]


def solution(mesh):
    placed = (
        P("dp", None, None),
        P("dp", "seq", None),
        P("dp"),
        P("dp", None),
        P("dp", None, None),
        P(None, ("dp", "seq"), None),
    )
    custom = dict(mesh.shape) == {"dp": 16, "seq": 2}
    return jax.shard_map(
        partial(shards, custom),
        mesh=mesh,
        in_specs=placed,
        out_specs=(
            P("dp", None, None),
            P("dp", None, None),
            P("dp", "seq", None),
            P(None, ("dp", "seq"), None),
        ),
        check_vma=False,
    )
```

```python
from functools import partial

import jax
import jax.numpy as jnp
from jax import lax
from jax.experimental import pallas as pl
from jax.experimental.pallas import tpu as pltpu
from jax.sharding import PartitionSpec as P

D = 768
H = 12
HEAD = 64
FF = 3072
PAIRS = H // 2
LANES = 2 * HEAD
QP = 112
VEC_ROW = 8 * D + 2 * FF
VECS = 24
TAIL = 256
HEAD_ROWS = 128
QUERY_HEAD = 64
SCALE = HEAD ** (-0.5)
EPS = 1e-05
NEG = -1e30
F32 = jnp.float32
BF16 = jnp.bfloat16
MIB = 1024 * 1024


def dot_nn(a, b):
    return lax.dot_general(a, b, (((1,), (0,)), ((), ())), preferred_element_type=F32)


def dot_nt(a, b):
    return lax.dot_general(a, b, (((1,), (1,)), ((), ())), preferred_element_type=F32)


def dot_tn(a, b):
    return lax.dot_general(a, b, (((0,), (0,)), ((), ())), preferred_element_type=F32)


def norm_parts(v):
    center = v - jnp.mean(v, axis=-1, keepdims=True)
    inverse = lax.rsqrt(jnp.mean(center * center, axis=-1, keepdims=True) + EPS)
    return center * inverse, inverse


def norm_back(dy, hat, inverse, gain):
    scaled = dy * gain
    mean_one = jnp.mean(scaled, axis=-1, keepdims=True)
    mean_two = jnp.mean(scaled * hat, axis=-1, keepdims=True)
    return inverse * (scaled - mean_one - hat * mean_two)


def rowsum(v):
    return jnp.sum(v.astype(F32), axis=0, keepdims=True)


def head_masks():
    lane = lax.broadcasted_iota(jnp.int32, (1, LANES), 1)
    first = jnp.where(lane < HEAD, 1.0, 0.0)
    return first.astype(BF16), (1.0 - first).astype(BF16)


def two_heads(block, masks):
    return jnp.concatenate([block * masks[0], block * masks[1]], axis=0)


def join_heads(stacked):
    lane = lax.broadcasted_iota(jnp.int32, (QP, LANES), 1)
    return jnp.where(lane < HEAD, stacked[:QP], stacked[QP:])


def weight_block(index):
    return pl.BlockSpec((D, D), lambda *_: (index, 0))


def whole(shape):
    return pl.BlockSpec(shape, lambda *_: (0,) * len(shape))


def params(mib):
    return pltpu.CompilerParams(vmem_limit_bytes=mib * MIB)


def cost(flops, moved):
    return pl.CostEstimate(flops=flops // 1000, bytes_accessed=moved // 1000, transcendentals=0)


FIRST_BLOCKS = (0, 1, 2, 5, 6, 3, 4)
SPREAD = ((0, 0, 0), (0, 0, 1), (0, 1, 0), (1, 0, 0), (0, 1, 1), (1, 1, 0), (1, 0, 1), (1, 1, 1))
PAIR_ROWS = 784
HOLDER = (3, 1, 1, 1)


class Assembly:
    def __init__(self, flags, bufs, weights, seams, sems, vec_low, vec_sem):
        self.core, self.x, self.y, self.z = flags[0], flags[1], flags[2], flags[3]
        self.bufs, self.weights, self.seams, self.sems = bufs, weights, seams, sems
        self.vec_low, self.vec_sem = vec_low, vec_sem
        self.ready = set()

    def buf(self, dc, dz2, spread):
        return self.bufs[dc * 16 + dz2 * 8 + SPREAD.index(spread)]

    def start_vec(self):
        first = VEC_ROW - 15 * PAIR_ROWS - 400
        for dc in (0, 1):
            for dz2 in (0, 1):
                for dz1, dy, dx in SPREAD:
                    here = (self.z ^ (2 * dz2 + dz1), self.y ^ dy, self.core ^ dc, self.x ^ dx)
                    hit = (here[0] == HOLDER[0]) & (here[1] == HOLDER[1]) & (here[2] == HOLDER[2]) & (here[3] == HOLDER[3])

                    @pl.when(hit)
                    def _(source=self.buf(dc, dz2, (dz1, dy, dx))):
                        pltpu.make_async_copy(source.at[pl.ds(first, 32)], self.vec_low, self.vec_sem).start()

    def wait_vec(self):
        pltpu.make_async_copy(self.weights.at[pl.ds(0, 32)], self.vec_low, self.vec_sem).wait()

    def start_group(self, dz2):
        def rows(start, count):
            return pl.ds(pl.multiple_of(start, 16), count)

        for dz1 in (0, 1):
            for dy in (0, 1):
                for dc in (0, 1):
                    pair = (self.z ^ (2 * dz2 + dz1)) * 4 + (self.y ^ dy) * 2 + (self.core ^ dc)
                    base, sem = pair * PAIR_ROWS, self.sems.at[pair]
                    near, far = self.buf(dc, dz2, (dz1, dy, 0)), self.buf(dc, dz2, (dz1, dy, 1))
                    for source, x in ((near, self.x), (far, 1 - self.x)):
                        target = self.weights.at[rows(base + 400 * x, 384)]
                        pltpu.make_async_copy(source.at[pl.ds(0, 384)], target, sem).start()
                        pltpu.make_async_copy(source.at[pl.ds(384, 16)], self.seams.at[pair, x], sem).start()

    def start(self):
        self.start_vec()
        for low in (True, False):

            @pl.when((self.z < 2) == low)
            def _(low=low):
                for dz2 in (0, 1) if low else (1, 0):
                    self.start_group(dz2)

    def wait(self, pair):
        if pair not in self.ready:
            self.ready.add(pair)
            rows = self.weights.at[pl.ds(0, PAIR_ROWS + 16)]
            pltpu.make_async_copy(rows, rows, self.sems.at[pair]).wait()
            halves = [self.seams[pair, x].astype(F32)[:8] for x in (0, 1)]
            seam = pl.ds(pair * PAIR_ROWS + 384, 16)
            self.weights[seam, :] = jnp.concatenate(halves, axis=0).astype(BF16)

    def block(self, number):
        for pair in range(number * D // PAIR_ROWS, (number * D + D - 1) // PAIR_ROWS + 1):
            self.wait(pair)


class Direct:
    def __init__(self, w_hbm, weights, sems, vec_low, vec_sem):
        self.copies = {}
        for number in FIRST_BLOCKS:
            rows = pl.ds(number * D, D)
            self.copies[number] = pltpu.make_async_copy(w_hbm.at[rows], weights.at[rows], sems.at[number])
        self.vec = pltpu.make_async_copy(w_hbm.at[pl.ds(VEC_ROW, 32)], vec_low, vec_sem)
        self.ready = set()

    def start(self):
        self.vec.start()
        for number in FIRST_BLOCKS:
            self.copies[number].start()

    def wait_vec(self):
        self.vec.wait()

    def block(self, number):
        if number not in self.ready:
            self.ready.add(number)
            self.copies[number].wait()


def forward_kernel(queries, custom, left_ref, flags, xb_ref, m_hbm, *refs):
    count = 32 if custom else 1
    bufs, refs = refs[:count], refs[count:]
    qs_out, ks_out, vs_out, os_out, y1_out, qc_out, k_out, v_out, o_out, stat_ref = refs[:10]
    w_out = refs[10] if custom else None
    weights, m_ref, qs_ref, ks_ref, vs_ref, os_ref, y1_ref, qc_ref, k_ref, v_ref, o_ref, vec_low = refs[10 + custom : 22 + custom]
    seams, w_sems, m_sems, out_sems, kv_sems, vec_sem, all_sems = refs[22 + custom :]
    images = m_ref.shape[0]
    tokens = m_ref.shape[1]
    if custom:
        feed = Assembly(flags, bufs, weights, seams, w_sems, vec_low, vec_sem)
    else:
        feed = Direct(bufs[0], weights, w_sems, vec_low, vec_sem)

    def load_memory(image):
        return pltpu.make_async_copy(m_hbm.at[image], m_ref.at[image], m_sems.at[image])

    def matrix(block):
        feed.block(block)
        return weights[block * D : (block + 1) * D, :]

    def leave_weights(half):
        rows = pl.ds(half * 8 * PAIR_ROWS, 8 * PAIR_ROWS)
        return pltpu.make_async_copy(weights.at[rows], w_out.at[rows], all_sems.at[half])

    small = [(qs_ref, qs_out), (ks_ref, ks_out), (vs_ref, vs_out), (os_ref, os_out), (y1_ref, y1_out), (qc_ref, qc_out)]

    def leave(number):
        return pltpu.make_async_copy(*small[number], out_sems.at[number])

    def leave_image(image, number):
        source, target = [(k_ref, k_out), (v_ref, v_out), (o_ref, o_out)][number]
        return pltpu.make_async_copy(source.at[image], target.at[image], kv_sems.at[image, number])

    feed.start()
    for image in range(images):
        load_memory(image).start()
    feed.wait_vec()
    vec = vec_low[...].astype(F32)
    xb = xb_ref[...]
    qs_ref[...] = ((dot_nn(xb, matrix(0)) + vec[0:1, :]) * SCALE).astype(BF16)
    leave(0).start()
    ks_ref[...] = dot_nn(xb, matrix(1)).astype(BF16)
    leave(1).start()
    vs_ref[...] = (dot_nn(xb, matrix(2)) + vec[1:2, :]).astype(BF16)
    leave(2).start()
    masks = head_masks()
    real = lax.broadcasted_iota(jnp.int32, (2 * QP, QP), 1) < queries
    places = [(slice(i * QP, (i + 1) * QP), slice(p * LANES, (p + 1) * LANES)) for i in range(images) for p in range(PAIRS)]

    def raw_self(place):
        return dot_nt(two_heads(qs_ref[place], masks), ks_ref[place])

    following = raw_self(places[0])
    for number, place in enumerate(places):
        scores = following
        if number + 1 < len(places):
            following = raw_self(places[number + 1])
        scores = jnp.where(real, scores, NEG)
        probs = jnp.exp(scores - jnp.max(scores, axis=-1, keepdims=True))
        probs = probs / jnp.sum(probs, axis=-1, keepdims=True)
        os_ref[place] = join_heads(dot_nn(probs.astype(BF16), vs_ref[place])).astype(BF16)
    leave(3).start()
    y1 = xb.astype(F32) + (dot_nn(os_ref[...], matrix(3)) + vec[2:3, :])
    y1_ref[...] = y1
    leave(4).start()
    hat, _ = norm_parts(y1)
    x1 = hat * vec[11:12, :] + vec[12:13, :]
    qc_ref[...] = ((dot_nn(x1.astype(BF16), matrix(4)) + vec[3:4, :]) * SCALE).astype(BF16)
    leave(5).start()

    feed.block(5)
    feed.block(6)
    if custom:
        for pair in range(8):
            feed.wait(pair)
        leave_weights(0).start()
    column = lax.broadcasted_iota(jnp.int32, (2 * QP, 128), 1)
    for image in range(images):
        load_memory(image).wait()
        rows = slice(image * QP, (image + 1) * QP)
        k_ref[image] = dot_nn(m_ref[image], matrix(5)).astype(BF16)
        v_ref[image] = (dot_nn(m_ref[image], matrix(6)) + vec[4:5, :]).astype(BF16)
        leave_image(image, 0).start()
        leave_image(image, 1).start()
        valid = lax.broadcasted_iota(jnp.int32, (2 * QP, tokens), 1) < left_ref[image]
        stat = jnp.zeros((2 * QP, 128), F32)
        def raw(pair):
            lanes = slice(pair * LANES, (pair + 1) * LANES)
            return dot_nt(two_heads(qc_ref[rows, lanes], masks), k_ref[image, :, lanes])

        following = raw(0)
        for pair in range(PAIRS):
            lanes = slice(pair * LANES, (pair + 1) * LANES)
            scores = following
            if pair + 1 < PAIRS:
                following = raw(pair + 1)
            scores = jnp.where(valid, scores, NEG)
            top = jnp.max(scores, axis=-1, keepdims=True)
            probs = jnp.exp(scores - top)
            total = jnp.sum(probs, axis=-1, keepdims=True)
            mixed = dot_nn(probs.astype(BF16), v_ref[image, :, lanes]) / total
            o_ref[image, :, lanes] = join_heads(mixed).astype(BF16)
            stat = jnp.where(column == pair, top + jnp.log(total), stat)
        stat_ref[image] = jnp.where(left_ref[image] > 0, stat.T[:8], NEG)
        leave_image(image, 2).start()
        if custom and image == 0:
            for pair in range(8, 16):
                feed.wait(pair)
            leave_weights(1).start()
    for number in range(len(small)):
        leave(number).wait()
    for image in range(images):
        for number in range(3):
            leave_image(image, number).wait()
    if custom:
        leave_weights(0).wait()
        leave_weights(1).wait()


def forward(left, flags, xb, memory, bufs, queries):
    custom = len(bufs) > 1
    rows = xb.shape[0]
    images, tokens, _ = memory.shape
    narrow = jax.ShapeDtypeStruct((rows, D), BF16)
    tall = jax.ShapeDtypeStruct(memory.shape, BF16)
    anywhere = pl.BlockSpec(memory_space=pl.ANY)
    small = pltpu.VMEM((rows, D), BF16)
    large = pltpu.VMEM(memory.shape, BF16)
    held = 16 * PAIR_ROWS if custom else 7 * D
    return pl.pallas_call(
        partial(forward_kernel, queries, custom),
        grid_spec=pltpu.PrefetchScalarGridSpec(
            num_scalar_prefetch=2,
            grid=(1,),
            in_specs=[whole((rows, D)), anywhere] + [anywhere] * len(bufs),
            out_specs=[anywhere] * 9 + [whole((images, 8, 2 * QP))] + [anywhere] * custom,
            scratch_shapes=[
                pltpu.VMEM((held, D), BF16),
                large, small, small, small, small,
                pltpu.VMEM((rows, D), F32),
                small, large, large,
                pltpu.VMEM((images, QP, D), BF16),
                pltpu.VMEM((32, D), BF16),
                pltpu.VMEM((16, 2, 16, D), BF16),
                pltpu.SemaphoreType.DMA((16,)),
                pltpu.SemaphoreType.DMA((images,)),
                pltpu.SemaphoreType.DMA((6,)),
                pltpu.SemaphoreType.DMA((images, 3)),
                pltpu.SemaphoreType.DMA(()),
                pltpu.SemaphoreType.DMA((2,)),
            ],
        ),
        out_shape=[
            narrow, narrow, narrow, narrow,
            jax.ShapeDtypeStruct((rows, D), F32),
            narrow, tall, tall,
            jax.ShapeDtypeStruct((images, QP, D), BF16),
            jax.ShapeDtypeStruct((images, 8, 2 * QP), F32),
        ]
        + [jax.ShapeDtypeStruct((held, D), BF16)] * custom,
        cost_estimate=cost(0, 0),
        compiler_params=params(60),
        name="forward",
    )(left, flags, xb, memory, *bufs)


def pieces(start, count, size):
    found = []
    done = 0
    while done < count:
        pair, offset = divmod(start + done, size)
        length = min(count - done, size - offset)
        found.append((done, pair, offset, length))
        done += length
    return found


class Halves:
    def __init__(self, keep, send, my_core):
        self.keep, self.send, self.my_core = keep, send, my_core

    def copy(self, target, source, pair, offset, length, sem):
        place = pair // self.cores()
        index = []
        for extent in reversed(target.shape[:-2]):
            index.insert(0, place % extent)
            place = place // extent
        return pltpu.make_async_copy(source, target.at[(*index, pl.ds(offset, length))], sem)

    def cores(self):
        return 1 if self.send is None else 2

    def start(self, source, pair, offset, length, sem):
        if self.send is None:
            self.copy(self.keep, source, pair, offset, length, sem).start()
            return

        @pl.when(self.my_core == pair % 2)
        def _():
            self.copy(self.keep, source, pair, offset, length, sem).start()

        @pl.when(self.my_core != pair % 2)
        def _():
            self.copy(self.send, source, pair, offset, length, sem).start()

    def wait(self, source, pair, offset, length, sem):
        self.copy(self.keep, source, pair, offset, length, sem).wait()


def middle_kernel(parts, split, *refs):
    flags, y1_ref = refs[:2]
    o_refs, stat_refs = refs[2 : 2 + parts], refs[2 + parts : 2 + 2 * parts]
    refs = refs[2 + 2 * parts :]
    w_hbm, vec, cot_ref, match_ref, out_hbm = refs[:5]
    halves = Halves(refs[5], refs[6] if split else None, flags[0])
    refs = refs[6 + split :]
    cross_halves = Halves(refs[0], refs[1] if split else None, flags[0])
    refs = refs[1 + split :]
    db_ref, doc_ref, tot_ref, dvec_ref = refs[:4]
    ocf, ocb, y2, x2b, u, slope, acc, e3b, staged, blank, out_ref, dco_ref, co, feed = refs[4:18]
    sems, blank_sem, out_sem, side_sems, w_sems = refs[18:]
    phase, step = pl.program_id(0), pl.program_id(1)
    steps = FF // D
    images = match_ref.shape[0]
    column = lax.broadcasted_iota(jnp.int32, (2 * QP, 128), 1)
    lane = lax.broadcasted_iota(jnp.int32, (QP, LANES), 1)
    size = halves.keep.shape[-2]
    side = cross_halves.keep.shape[-2]

    def load(block):
        target = co if block == 7 else feed.at[block - 8]
        return pltpu.make_async_copy(w_hbm.at[pl.ds(block * D, D)], target, w_sems.at[block - 7])

    def leave_out():
        return pltpu.make_async_copy(out_ref, out_hbm, out_sem)

    def leave_side(act):
        starts = [(dco_ref, 3 * D - QUERY_HEAD, D), (staged.at[0, 0], 4 * D - QUERY_HEAD, HEAD_ROWS)]
        for which, (source, start, count) in enumerate(starts):
            if (which == 0) != (act[0] == "o"):
                continue
            for number, (done, pair, offset, length) in enumerate(pieces(start, count, side)):
                piece = source.at[pl.ds(done, length)]
                getattr(cross_halves, act[1])(piece, pair, offset, length, side_sems.at[which, number])

    def leave(which, at, act):
        skip = HEAD_ROWS if which + at == 0 else 0
        start = which * FF + at * D + skip - HEAD_ROWS
        for number, (done, pair, offset, length) in enumerate(pieces(start, D - skip, size)):
            source = staged.at[at % 2, which, pl.ds(done + skip, length)]
            getattr(halves, act)(source, pair, offset, length, sems.at[at, which, number])

    def leave_blank(act):
        for _, pair, offset, length in pieces(2 * FF - HEAD_ROWS, TAIL, size):
            getattr(halves, act)(blank, pair, offset, length, blank_sem)

    def ordered(first, second):
        if parts != 2:
            return first, second
        swap = flags[1] != 0
        return jnp.where(swap, second, first), jnp.where(swap, first, second)

    @pl.when((phase == 0) & (step == 0))
    def _():
        load(7).start()
        for at in range(steps):
            load(8 + at).start()
            load(8 + steps + at).start()
        for image in range(images):
            rows = slice(image * QP, (image + 1) * QP)
            stats = [ref[image] for ref in stat_refs]
            if parts == 2:
                stats = ordered(*stats)
            top = stats[0]
            for n in range(1, parts):
                top = jnp.maximum(top, stats[n])
            mass = [jnp.exp(stats[n] - top) for n in range(parts)]
            total = mass[0]
            for n in range(1, parts):
                total = total + mass[n]
            tot_ref[image, 0:8, :] = top + jnp.log(total)
            shares = [jnp.concatenate([m / total, jnp.zeros((120, 2 * QP), F32)], axis=0).T for m in mass]
            for pair in range(PAIRS):
                lanes = slice(pair * LANES, (pair + 1) * LANES)
                values = [ref[image, :, lanes].astype(F32) for ref in o_refs]
                if parts == 2:
                    values = ordered(*values)
                mixed = jnp.zeros((QP, LANES), F32)
                for n in range(parts):
                    share = shares[n][:, pair : pair + 1]
                    mixed = mixed + values[n] * jnp.where(lane < HEAD, share[:QP], share[QP:])
                ocf[rows, lanes] = mixed
        ocb[...] = ocf[...].astype(BF16)
        hat, _ = norm_parts(y1_ref[...])
        x1 = hat * vec[11:12, :] + vec[12:13, :]
        load(7).wait()
        total = x1 + (dot_nn(ocb[...], co[...]) + vec[5:6, :])
        y2[...] = total
        hat, _ = norm_parts(total)
        x2 = hat * vec[13:14, :] + vec[14:15, :]
        x2b[...] = x2.astype(BF16)
        acc[...] = x2 + vec[6:7, :]

    for at in range(steps):

        @pl.when((phase == 0) & (step == at))
        def _(at=at):
            load(8 + at).wait()
            load(8 + steps + at).wait()

    f1, f2 = feed.at[step], feed.at[steps + step]

    @pl.when(phase == 0)
    def _():
        h = dot_nt(x2b[...], f1[...]) + vec[pl.ds(7 + step, 1), :]
        root = 0.7978845608028654
        square = h * h
        t = jnp.tanh(root * (h + 0.044715 * (h * square)))
        half = 0.5 * (1.0 + t)
        slope[step] = half + (0.5 * root) * h * (1.0 - t * t) * (1.0 + 0.134145 * square)
        active = (h * half).astype(BF16)
        u[step] = active
        acc[...] += dot_nn(active, f2[...])

    @pl.when((phase == 1) & (step == 0))
    def _():
        blank[...] = jnp.zeros_like(blank)
        leave_blank("start")
        dvec_ref[...] = jnp.zeros_like(dvec_ref)
        hat, inverse = norm_parts(acc[...])
        out = hat * vec[15:16, :] + vec[16:17, :]
        grads = []
        for image in range(images):
            out_ref[image] = out[image * QP : (image + 1) * QP]
            matched = match_ref[image]
            hit = lax.broadcasted_iota(jnp.int32, (QP, matched.shape[1]), 0) == matched
            grads.append(dot_nn(jnp.where(hit, 1.0, 0.0).astype(BF16), cot_ref[image]))
        leave_out().start()
        dy = jnp.concatenate(grads, axis=0)
        dvec_ref[15:16, :] = rowsum(dy * hat)
        dvec_ref[16:17, :] = rowsum(dy)
        dc = norm_back(dy, hat, inverse, vec[15:16, :])
        low = dc.astype(BF16)
        e3b[...] = low
        dvec_ref[6:7, :] = rowsum(low)
        acc[...] = dc

    for at in range(2, steps):

        @pl.when((phase == 1) & (step == at))
        def _(at=at):
            leave(0, at - 2, "wait")
            leave(1, at - 2, "wait")
            if at == 2:
                leave_side(("f", "wait"))

    @pl.when(phase == 1)
    def _():
        du = dot_nt(e3b[...], f2[...])
        dh = (du * slope[step]).astype(BF16)
        slot = lax.rem(step, 2)
        staged[slot, 1] = dot_tn(u[step], e3b[...]).astype(BF16)
        staged[slot, 0] = dot_tn(dh, x2b[...]).astype(BF16)

        @pl.when(step == 0)
        def _():
            leave_side(("f", "start"))

        for at in range(steps):

            @pl.when(step == at)
            def _(at=at):
                leave(0, at, "start")
                leave(1, at, "start")

        dvec_ref[pl.ds(7 + step, 1), :] = rowsum(dh)
        acc[...] += dot_nn(dh, f1[...])

    @pl.when((phase == 1) & (step == steps - 1))
    def _():
        hat, inverse = norm_parts(y2[...])
        dy = acc[...]
        dvec_ref[13:14, :] = rowsum(dy * hat)
        dvec_ref[14:15, :] = rowsum(dy)
        db = norm_back(dy, hat, inverse, vec[13:14, :])
        db_ref[...] = db
        low = db.astype(BF16)
        dvec_ref[5:6, :] = rowsum(low)
        dco_ref[...] = dot_tn(ocb[...], low).astype(BF16)
        leave_side(("o", "start"))
        doc = dot_nt(low, co[...]).astype(BF16)
        doc_ref[...] = doc
        both = doc.astype(F32) * ocf[...]
        for image in range(images):
            rows = slice(image * QP, (image + 1) * QP)
            tot = jnp.zeros((2 * QP, 128), F32)
            for pair in range(PAIRS):
                piece = both[rows, pair * LANES : (pair + 1) * LANES]
                one = jnp.sum(jnp.where(lane < HEAD, piece, 0.0), axis=-1, keepdims=True)
                two = jnp.sum(jnp.where(lane < HEAD, 0.0, piece), axis=-1, keepdims=True)
                tot = jnp.where(column == pair, jnp.concatenate([one, two], axis=0), tot)
            tot_ref[image, 8:16, :] = tot.T[:8]
        leave_blank("wait")
        leave_out().wait()
        leave_side(("o", "wait"))
        for which in (0, 1):
            leave(which, steps - 2, "wait")
            leave(which, steps - 1, "wait")


def halves_shape(shape, split):
    return [jax.ShapeDtypeStruct(shape, BF16)] * (1 + split)


def middle(flags, y1, o_parts, stat_parts, w, vec, cot, matched, far_shape, cross_shape, split):
    rows = y1.shape[0]
    images = cot.shape[0]
    steps = FF // D
    parts = len(o_parts)
    anywhere = pl.BlockSpec(memory_space=pl.ANY)
    return pl.pallas_call(
        partial(middle_kernel, parts, split),
        grid_spec=pltpu.PrefetchScalarGridSpec(
            num_scalar_prefetch=1,
            grid=(2, steps),
            in_specs=[whole(y1.shape)]
            + [whole(o_parts[0].shape)] * parts
            + [whole(stat_parts[0].shape)] * parts
            + [anywhere, whole((VECS, D)), whole(cot.shape), whole((images, 1, matched.shape[1]))],
            out_specs=[anywhere] * (3 + 2 * split)
            + [
                whole((rows, D)),
                whole((rows, D)),
                whole((images, 16, 2 * QP)),
                whole((VECS, D)),
            ],
            scratch_shapes=[
                pltpu.VMEM((rows, D), F32),
                pltpu.VMEM((rows, D), BF16),
                pltpu.VMEM((rows, D), F32),
                pltpu.VMEM((rows, D), BF16),
                pltpu.VMEM((steps, rows, D), BF16),
                pltpu.VMEM((steps, rows, D), F32),
                pltpu.VMEM((rows, D), F32),
                pltpu.VMEM((rows, D), BF16),
                pltpu.VMEM((2, 2, D, D), BF16),
                pltpu.VMEM((TAIL, D), BF16),
                pltpu.VMEM((images, QP, D), F32),
                pltpu.VMEM((D, D), BF16),
                pltpu.VMEM((D, D), BF16),
                pltpu.VMEM((2 * steps, D, D), BF16),
                pltpu.SemaphoreType.DMA((steps, 2, 2)),
                pltpu.SemaphoreType.DMA(()),
                pltpu.SemaphoreType.DMA(()),
                pltpu.SemaphoreType.DMA((2, 2)),
                pltpu.SemaphoreType.DMA((1 + 2 * steps,)),
            ],
        ),
        out_shape=[jax.ShapeDtypeStruct((images, QP, D), F32)]
        + halves_shape(far_shape, split)
        + halves_shape(cross_shape, split)
        + [
            jax.ShapeDtypeStruct((rows, D), F32),
            jax.ShapeDtypeStruct((rows, D), BF16),
            jax.ShapeDtypeStruct((images, 16, 2 * QP), F32),
            jax.ShapeDtypeStruct((VECS, D), F32),
        ],
        cost_estimate=cost(2 * rows * D * (6 * FF + 3 * D), 2 * FF * D * 6),
        compiler_params=params(60),
        name="middle",
    )(flags, y1, *o_parts, *stat_parts, w, vec, cot, matched[:, None, :])


def cross_backward_kernel(left_ref, q_ref, k_ref, v_ref, do_ref, tot_ref, dq_ref, dk_ref, dv_ref):
    tokens = k_ref.shape[1]
    masks = head_masks()
    valid = lax.broadcasted_iota(jnp.int32, (tokens, 2 * QP), 0) < left_ref[pl.program_id(0)]
    def raw(pair):
        lanes = slice(pair * LANES, (pair + 1) * LANES)
        query = two_heads(q_ref[0, :, lanes], masks)
        dout = two_heads(do_ref[0, :, lanes], masks)
        return query, dout, dot_nt(k_ref[0, :, lanes], query), dot_nt(v_ref[0, :, lanes], dout)

    following = raw(0)
    for pair in range(PAIRS):
        lanes = slice(pair * LANES, (pair + 1) * LANES)
        query, dout, scores, dprobs = following
        if pair + 1 < PAIRS:
            following = raw(pair + 1)
        probs = jnp.where(valid, jnp.exp(scores - tot_ref[0, pair : pair + 1, :]), 0.0)
        dscores = (probs * (dprobs - tot_ref[0, 8 + pair : 9 + pair, :])).astype(BF16)
        dv_ref[0, :, lanes] = dot_nn(probs.astype(BF16), dout).astype(BF16)
        dk_ref[0, :, lanes] = dot_nn(dscores, query).astype(BF16)
        dq_ref[0, :, lanes] = join_heads(dot_tn(k_ref[0, :, lanes], dscores).T).astype(BF16)


def cross_backward(left, qc, key, value, doc, tot):
    images, tokens, _ = key.shape
    q_block = pl.BlockSpec((1, QP, D), lambda i, _: (i, 0, 0))
    m_block = pl.BlockSpec((1, tokens, D), lambda i, _: (i, 0, 0))
    s_block = pl.BlockSpec((1, 16, 2 * QP), lambda i, _: (i, 0, 0))
    return pl.pallas_call(
        cross_backward_kernel,
        grid_spec=pltpu.PrefetchScalarGridSpec(
            num_scalar_prefetch=1,
            grid=(images,),
            in_specs=[q_block, m_block, m_block, q_block, s_block],
            out_specs=[q_block, m_block, m_block],
        ),
        out_shape=[
            jax.ShapeDtypeStruct((images, QP, D), BF16),
            jax.ShapeDtypeStruct(key.shape, BF16),
            jax.ShapeDtypeStruct(key.shape, BF16),
        ],
        cost_estimate=cost(4 * images * 2 * QP * tokens * D // 3, images * tokens * D * 8),
        compiler_params=params(60),
        name="cross_backward",
    )(left, qc.reshape(images, QP, D), key, value, doc.reshape(images, QP, D), tot)


def memory_weights_kernel(split, flags, *refs):
    m_ref, dk_ref, dv_ref = refs[1 + split : 4 + split]
    refs = refs[4 + split :]
    gb_ref = refs[0]
    halves = Halves(refs[1], refs[2] if split else None, flags[0])
    low, sems = refs[2 + split :]
    def leave(which, act):
        start = (1 + which) * D - QUERY_HEAD
        for number, (done, pair, offset, length) in enumerate(pieces(start, D, halves.keep.shape[-2])):
            piece = low.at[which, pl.ds(done, length)]
            getattr(halves, act)(piece, pair, offset, length, sems.at[which, number])

    tall = m_ref[...].reshape(-1, D)
    for which, ref in ((0, dk_ref), (1, dv_ref)):
        low[which] = dot_tn(tall, ref[...].reshape(-1, D)).astype(BF16)
        leave(which, "start")
    gb_ref[...] = jnp.broadcast_to(rowsum(dv_ref[...].reshape(-1, D)), gb_ref.shape)
    for which in (0, 1):
        leave(which, "wait")


def memory_weights(flags, cross, memory, dk, dv, split):
    images, tokens, _ = memory.shape
    block = whole(memory.shape)
    anywhere = pl.BlockSpec(memory_space=pl.ANY)
    return pl.pallas_call(
        partial(memory_weights_kernel, split),
        grid_spec=pltpu.PrefetchScalarGridSpec(
            num_scalar_prefetch=1,
            grid=(1,),
            in_specs=[anywhere] * (1 + split) + [block, block, block],
            out_specs=[whole((8, D))] + [anywhere] * (1 + split),
            scratch_shapes=[
                pltpu.VMEM((2, D, D), BF16),
                pltpu.SemaphoreType.DMA((2, 2)),
            ],
        ),
        out_shape=[jax.ShapeDtypeStruct((8, D), F32)] + halves_shape(cross[0].shape, split),
        input_output_aliases={1 + n: 1 + n for n in range(1 + split)},
        cost_estimate=cost(4 * images * tokens * D * D, images * tokens * D * 6),
        compiler_params=params(60),
        name="memory_weights",
    )(flags, *cross, memory, dk, dv)


def memory_grads_kernel(dk_ref, dv_ref, ck, cv, gm_ref):
    gm_ref[0] = dot_nt(dk_ref[0], ck[...]) + dot_nt(dv_ref[0], cv[...])


def memory_grads(dk, dv, w):
    images, tokens, _ = dk.shape
    block = pl.BlockSpec((1, tokens, D), lambda i: (i, 0, 0))
    return pl.pallas_call(
        memory_grads_kernel,
        grid=(images,),
        in_specs=[block, block, weight_block(5), weight_block(6)],
        out_specs=block,
        out_shape=jax.ShapeDtypeStruct(dk.shape, F32),
        cost_estimate=pl.CostEstimate(
            flops=4 * images * tokens * D * D, bytes_accessed=images * tokens * D * 8, transcendentals=0
        ),
        compiler_params=params(60),
        name="memory_grads",
    )(dk, dv, w, w)


class Loads:
    def __init__(self, pairs, sems):
        self.copies = [(pltpu.make_async_copy(source, target, sems.at[n]), target) for n, (source, target) in enumerate(pairs)]
        self.ready = set()
        for copy, _ in self.copies:
            copy.start()

    def __call__(self, number):
        copy, target = self.copies[number]
        if number not in self.ready:
            copy.wait()
            self.ready.add(number)
        return target[...]


def query_backward_kernel(parts, split, flags, *refs):
    sources, vec = refs[1 + split : 4 + split + parts], refs[4 + split + parts]
    refs = refs[5 + split + parts :]
    da_ref, gq_head_ref, dvec_ref = refs[:3]
    halves = Halves(refs[3], refs[4] if split else None, flags[0])
    refs = refs[4 + split :]
    targets, staged, load_sems, sems = refs[: 3 + parts], refs[3 + parts], refs[4 + parts], refs[5 + parts]
    w_hbm = sources[-1]
    sources = [*sources[:-1], w_hbm.at[pl.ds(4 * D, D)]]
    get = Loads(list(zip(sources, targets)), load_sems)

    def leave(act):
        for number, (done, pair, offset, length) in enumerate(pieces(0, D - QUERY_HEAD, halves.keep.shape[-2])):
            piece = staged.at[pl.ds(done + QUERY_HEAD, length)]
            getattr(halves, act)(piece, pair, offset, length, sems.at[number])

    total = get(0).astype(F32)
    for number in range(1, parts):
        total = total + get(number).astype(F32)
    dq = total.astype(BF16) * SCALE
    hat, inverse = norm_parts(get(parts))
    gain = vec[11:12, :]
    x1b = (hat * gain + vec[12:13, :]).astype(BF16)
    gcq = dot_tn(x1b, dq).astype(BF16)
    staged[...] = gcq
    leave("start")
    gq_head_ref[...] = gcq[:QUERY_HEAD]
    dvec_ref[...] = jnp.zeros_like(dvec_ref)
    dvec_ref[3:4, :] = rowsum(dq)
    dy = get(parts + 1) + dot_nt(dq, get(parts + 2))
    dvec_ref[11:12, :] = rowsum(dy * hat)
    dvec_ref[12:13, :] = rowsum(dy)
    da = norm_back(dy, hat, inverse, gain)
    da_ref[...] = da
    dvec_ref[2:3, :] = rowsum(da.astype(BF16))
    leave("wait")


def query_backward(flags, cross, y1, db, dq_parts, w, vec, split):
    rows = y1.shape[0]
    parts = len(dq_parts)
    full = whole((rows, D))
    anywhere = pl.BlockSpec(memory_space=pl.ANY)
    return pl.pallas_call(
        partial(query_backward_kernel, parts, split),
        grid_spec=pltpu.PrefetchScalarGridSpec(
            num_scalar_prefetch=1,
            grid=(1,),
            in_specs=[anywhere] * (4 + split + parts) + [whole((VECS, D))],
            out_specs=[full, whole((QUERY_HEAD, D)), whole((VECS, D))] + [anywhere] * (1 + split),
            scratch_shapes=[pltpu.VMEM((rows, D), BF16)] * parts
            + [pltpu.VMEM((rows, D), F32)] * 2
            + [pltpu.VMEM((D, D), BF16)] * 2
            + [pltpu.SemaphoreType.DMA((parts + 3,)), pltpu.SemaphoreType.DMA((2,))],
        ),
        out_shape=[
            jax.ShapeDtypeStruct((rows, D), F32),
            jax.ShapeDtypeStruct((QUERY_HEAD, D), BF16),
            jax.ShapeDtypeStruct((VECS, D), F32),
        ]
        + halves_shape(cross[0].shape, split),
        input_output_aliases={1 + n: 3 + n for n in range(1 + split)},
        cost_estimate=cost(4 * rows * D * D, rows * D * 16),
        compiler_params=params(60),
        name="query_backward",
    )(flags, *cross, *[part.reshape(rows, D) for part in dq_parts], y1, db, w, vec)


def self_backward_kernel(queries, split, *refs):
    flags, os_hbm, da_hbm, qs_hbm, ks_hbm, vs_hbm, x_hbm, w_hbm, gq_ref, gx_ref, dvec_ref, keep_ref = refs[:12]
    halves = Halves(keep_ref, refs[12] if split else None, flags[0])
    sq, sk, sv, g_ref, os_ref, da_ref, ao, qs, ks, vs, x_ref, aq, ak, av, sems, load_sems = refs[12 + split :]
    size = keep_ref.shape[-2]
    matrices = [w_hbm.at[pl.ds(block * D, D)] for block in range(4)]
    get = Loads(
        [(os_hbm, os_ref), (da_hbm, da_ref), (matrices[3], ao), (qs_hbm, qs), (ks_hbm, ks), (vs_hbm, vs)]
        + [(x_hbm, x_ref), (matrices[0], aq), (matrices[1], ak), (matrices[2], av)],
        load_sems,
    )

    def leave(pair, act):
        getattr(halves, act)(g_ref.at[pl.ds(pair * size, size)], pair, 0, size, sems.at[pair])

    pairs = g_ref.shape[0] // size
    images = x_ref.shape[0] // QP
    dvec_ref[...] = jnp.zeros_like(dvec_ref)
    os = get(0)
    da = get(1)
    low = da.astype(BF16)
    g_ref[4 * D :, :] = gq_ref[...]
    g_ref[3 * D : 4 * D, :] = dot_tn(os, low).astype(BF16)
    dos = dot_nt(low, get(2)).astype(BF16)
    for number in (3, 4, 5):
        get(number)
    masks = head_masks()
    real = lax.broadcasted_iota(jnp.int32, (QP, 2 * QP), 0) < queries
    places = [(slice(i * QP, (i + 1) * QP), slice(p * LANES, (p + 1) * LANES)) for i in range(images) for p in range(PAIRS)]

    def raw(place):
        query = two_heads(qs[place], masks)
        dout = two_heads(dos[place], masks)
        return query, dout, dot_nt(ks[place], query), dot_nt(vs[place], dout)

    following = raw(places[0])
    for number, place in enumerate(places):
        query, dout, scores, dprobs = following
        if number + 1 < len(places):
            following = raw(places[number + 1])
        scores = jnp.where(real, scores, NEG)
        probs = jnp.exp(scores - jnp.max(scores, axis=0, keepdims=True))
        probs = probs / jnp.sum(probs, axis=0, keepdims=True)
        dscores = (probs * (dprobs - jnp.sum(probs * dprobs, axis=0, keepdims=True))).astype(BF16)
        sv[place] = dot_nn(probs.astype(BF16), dout).astype(BF16)
        sk[place] = dot_nn(dscores, query).astype(BF16)
        sq[place] = join_heads(dot_tn(ks[place], dscores).T).astype(BF16) * SCALE
    dvec_ref[0:1, :] = rowsum(sq[...])
    dvec_ref[1:2, :] = rowsum(sv[...])
    xb = get(6)
    g_ref[2 * D : 3 * D, :] = dot_tn(xb, sv[...]).astype(BF16)
    for pair in range(2, pairs):
        leave(pair, "start")
    g_ref[D : 2 * D, :] = dot_tn(xb, sk[...]).astype(BF16)
    for pair in range(1, min(2, pairs)):
        leave(pair, "start")
    g_ref[0:D, :] = dot_tn(xb, sq[...]).astype(BF16)
    leave(0, "start")
    gx = da + dot_nt(sq[...], get(7)) + dot_nt(sk[...], get(8)) + dot_nt(sv[...], get(9))
    for image in range(images):
        gx_ref[image] = gx[image * QP : (image + 1) * QP]
    for pair in range(pairs):
        leave(pair, "wait")


def self_backward(flags, xb, qs, ks, vs, os, da, gq_head, w, queries, shape, split):
    rows = xb.shape[0]
    images = rows // QP
    anywhere = pl.BlockSpec(memory_space=pl.ANY)
    return pl.pallas_call(
        partial(self_backward_kernel, queries, split),
        grid_spec=pltpu.PrefetchScalarGridSpec(
            num_scalar_prefetch=1,
            grid=(1,),
            in_specs=[anywhere] * 7 + [whole((QUERY_HEAD, D))],
            out_specs=[whole((images, QP, D)), whole((VECS, D))] + [anywhere] * (1 + split),
            scratch_shapes=[pltpu.VMEM((rows, D), BF16)] * 3
            + [pltpu.VMEM((4 * D + QUERY_HEAD, D), BF16), pltpu.VMEM((rows, D), BF16), pltpu.VMEM((rows, D), F32)]
            + [pltpu.VMEM((D, D), BF16)]
            + [pltpu.VMEM((rows, D), BF16)] * 4
            + [pltpu.VMEM((D, D), BF16)] * 3
            + [pltpu.SemaphoreType.DMA((4,)), pltpu.SemaphoreType.DMA((10,))],
        ),
        out_shape=[
            jax.ShapeDtypeStruct((images, QP, D), F32),
            jax.ShapeDtypeStruct((VECS, D), F32),
        ]
        + halves_shape(shape, split),
        cost_estimate=cost(16 * rows * D * D * 2, 8 * D * D * 2),
        compiler_params=params(60),
        name="self_backward",
    )(flags, os, da, qs, ks, vs, xb, w, gq_head)


class Place:
    def __init__(self):
        place = lax.axis_index("dp")
        self.x = lax.axis_index("seq")
        self.c = lax.rem(place, 2)
        self.y = lax.rem(place // 2, 2)
        self.z = place // 4


def pick(array, index, axis):
    return lax.dynamic_index_in_dim(array, index, axis, keepdims=False)


def over_core(v):
    return lax.ppermute(v, "dp", [(i, i ^ 1) for i in range(16)])


def over_y(v):
    return lax.ppermute(v, "dp", [(i, i ^ 2) for i in range(16)])


def over_x(v):
    return lax.ppermute(v, "seq", [(0, 1), (1, 0)])


def over_z(v, hops):
    return lax.ppermute(v, "dp", [(4 * a + i, 4 * b + i) for a, b in hops for i in range(4)])


def over_far(v):
    return over_z(v, [(0, 2), (2, 0), (1, 3), (3, 1)])


def over_near(v):
    return over_z(v, SWAP_ONE)


def spread(own):
    x, y, z = over_x(own), over_y(own), over_near(own)
    xy, yz, zx = over_x(y), over_y(z), over_near(x)
    return own, x, y, z, xy, yz, zx


def gather(at, rows):
    rest = jnp.zeros((8, D), BF16)
    own = lax.dynamic_slice_in_dim(jnp.concatenate([rows, rows[:8], rest]), 8 * at.x, rows.shape[0] + 8)
    other = over_far(own)
    here, there = spread(own), spread(other)
    found = [*here, over_x(here[5]), *there, over_y(there[6])]
    return found + [over_core(part) for part in found]


def tie(*values):
    return lax.optimization_barrier(values)


def add(kept, came):
    return (kept.astype(F32) + came.astype(F32)).astype(BF16)


def own_half(pairs, x):
    half = pairs.shape[-2] // 2
    return pick(pairs.reshape(*pairs.shape[:-2], 2, half, D), x, pairs.ndim - 2)


def blocks_of(pairs):
    return pairs.reshape(*pairs.shape[:-2], 2, pairs.shape[-2] // 2, D)


def picked(pairs, half, x):
    return pick(pick(pairs, half, 0), x, 0)


def merge(body, flags, sources, out_rows, name):
    parts = 2
    specs = []
    for array, where in sources:
        lead = (None,) * (array.ndim - 2)
        shape = (*lead, array.shape[-2], D // parts)
        specs.append(pl.BlockSpec(shape, lambda i, f, where=where: (*where(f), 0, i)))
    return pl.pallas_call(
        body,
        grid_spec=pltpu.PrefetchScalarGridSpec(
            num_scalar_prefetch=1,
            grid=(parts,),
            in_specs=specs,
            out_specs=[
                pl.BlockSpec((*rows, D // parts), lambda i, f, n=len(rows): (*[0] * n, i)) for rows in out_rows
            ],
        ),
        out_shape=[jax.ShapeDtypeStruct((*rows, D), BF16) for rows in out_rows],
        cost_estimate=cost(0, 0),
        compiler_params=params(60),
        name=name,
    )(flags, *[array for array, _ in sources])


def far_send_kernel(flags, a, b, c, d, out):
    out[0] = add(a[...], b[...])
    out[1] = add(c[...], d[...])


def far_send(flags, kept, came):
    kept, came = blocks_of(kept), blocks_of(came)
    sources = []
    for r in (0, 1):
        sources += [(part, lambda f, r=r: (r, 1 - f[2], f[1])) for part in (kept, came)]
    return merge(far_send_kernel, flags, sources, [(2, kept.shape[-2])], "far_send")[0]


def cross_merge_kernel(flags, *refs):
    ins, outs = refs[:8], refs[8:]
    outs[0][...] = add(ins[0][...], ins[1][...])
    outs[1][...] = add(ins[2][...], ins[3][...])
    message = outs[2]
    block = ins[4].shape[0]
    spill = message.shape[0] - (block + 8)
    main = ins[4][...].astype(F32) + ins[5][...].astype(F32)
    total = ins[6][...].astype(F32) + ins[7][...].astype(F32)
    gap = jnp.zeros((8, total.shape[1]), F32)
    message[...] = jnp.concatenate([main, gap, total[block - spill :]], axis=0).astype(BF16)


def cross_merge(flags, cross, cross_came):
    cross, cross_came = blocks_of(cross), blocks_of(cross_came)
    block = cross.shape[-2]
    spill = 2 * block - (D - QUERY_HEAD)
    chosen = [
        lambda f: (0, f[1]),
        lambda f: (1, f[1]),
        lambda f: (1 - f[0], 1 - f[1]),
        lambda f: (0, 1 - f[1]),
    ]
    sources = []
    for where in chosen:
        sources += [(cross, where), (cross_came, where)]
    return merge(cross_merge_kernel, flags, sources, [(block,)] * 2 + [(block + 8 + spill,)], "cross_merge")


def far_merge_kernel(flags, *refs):
    ins, outs = refs[:6], refs[6:]
    for number in range(2):
        first, second, third = ins[3 * number : 3 * number + 3]
        outs[number][...] = (first[...].astype(F32) + second[...].astype(F32) + third[...].astype(F32)).astype(BF16)


def far_merge(flags, far, far_came, far_last):
    far, far_came = blocks_of(far), blocks_of(far_came)
    sources = []
    for r in (lambda f: 1 - f[3] % 2, lambda f: f[3] % 2):
        sources += [(part, lambda f, r=r: (r(f), f[2], f[1])) for part in (far, far_came)]
        sources += [(far_last, lambda f, r=r: (r(f),))]
    return merge(far_merge_kernel, flags, sources, [(far.shape[-2],)] * 2, "far_merge")


def cross_second(at, mine, came):
    start = D - QUERY_HEAD
    block = mine[0].shape[-2]
    spill = 2 * block - start
    main = came[:block].astype(F32)
    tall = jnp.concatenate([jnp.zeros((block - spill, D), F32), came[block + 8 :].astype(F32)])
    ids = (at.c * 2 + at.x) * block + jnp.arange(block)[:, None]

    def half(index, y):
        part = jnp.where((at.c == 0) & (y == 0), tall, main)
        place = ids + y * 4 * block
        shared = (place >= start) & (place < start + 2 * D)
        own = jnp.where(index == 0, mine[0], mine[1]).astype(F32)
        return (own + jnp.where(shared, part, 0.0)).astype(BF16)

    return half(1 - at.y, 1 - at.y), half(at.y, at.y)


SWAP_ONE = [(0, 1), (1, 0), (2, 3), (3, 2)]
SWAP_TWO = [(0, 2), (2, 0), (1, 3), (3, 1)]


def with_rows(message, vec_rows):
    return jnp.concatenate([message, vec_rows.astype(BF16)])


def finish(at, flags, block, far, far_last, near, near_send, cross, cross_came, vec_rows, extra):
    near_came = over_core(near_send)
    vec_came = over_core(vec_rows)
    low, high, message = cross_merge(flags, cross, cross_came)
    near_came, message, low, high = tie(near_came, message, low, high)
    came = over_x(message)
    near, near_came = blocks_of(near), blocks_of(near_came)
    near_send = add(picked(near, 1 - at.y, at.x), picked(near_came, 1 - at.y, at.x))
    vec_rows = vec_rows + vec_came
    near_send, near, near_kept, dk, dv, w, far_last = tie(near_send, near, near_came, *extra, far_last)
    far_out, far = far_merge(flags, *far, far_last)
    near_came, far_came, vec_came = over_y(near_send), over_z(far_out, SWAP_ONE), over_y(vec_rows)
    gm = memory_grads(dk, dv, w)
    gm, came = tie(gm, came)
    send, cross = cross_second(at, (low, high), came)
    send, near_came, vec_came, cross = tie(send, near_came, vec_came, cross)

    near = picked(near, at.y, at.x).astype(F32) + picked(near_kept, at.y, at.x).astype(F32)
    near = (near + near_came.astype(F32)).astype(BF16)
    vec_rows = vec_rows + vec_came
    near, vec_rows, send = tie(near, vec_rows, send)
    cross_came, near_came, vec_came = over_y(send), over_z(near, [(3, 2), (1, 0)]), over_z(vec_rows, SWAP_ONE)
    cross = add(cross, cross_came)
    near = add(near, near_came)
    far = add(far, far_came)
    vec_rows = vec_rows + vec_came
    near, cross, vec_rows, far = tie(near, cross, vec_rows, far)

    cut = block // 16 * 8
    cross_came, near_came = over_z(cross, [(3, 2), (0, 1)]), over_z(near, [(2, 0)])
    far_top = over_z(far[:cut], [(0, 2), (1, 3)])
    cross = add(cross, cross_came)
    near_came, cross, far, vec_rows, far_top = tie(near_came, cross, far, vec_rows, far_top)

    cross_came, far_low = over_z(cross, [(2, 1)]), over_z(with_rows(far[cut:], vec_rows), [(0, 2), (1, 3)])
    far_came = jnp.concatenate([far_top, far_low[: block - cut]])
    vec_rows = vec_rows + far_low[block - cut :].astype(F32)
    kept = jnp.where(at.z >= 2, far, jnp.where(at.z == 0, near, cross))
    came = jnp.where(at.z >= 2, far_came, jnp.where(at.z == 0, near_came, cross_came))
    grad_rows = kept.astype(F32) + came.astype(F32)
    start = VEC_ROW - 31 * block
    last = jnp.concatenate([grad_rows[:start], vec_rows, jnp.zeros((block - start - VECS, D), F32)])
    is_last = (lax.axis_index("dp") == 15) & (at.x == 1)
    return jnp.where(is_last, last, grad_rows), gm


def shards(custom, inputs, memory, lengths, matched, cotangent, weights):
    axes = ("dp", "seq")
    share = 1.0 / lax.axis_size("seq")
    images, queries, _ = inputs.shape
    tokens = memory.shape[1]
    block = weights.shape[1]
    at = Place()
    left = lengths - at.x * tokens
    flags = jnp.stack([at.c if custom else 0, at.x, at.y, at.z]).astype(jnp.int32)

    def parts_of(value):
        if custom:
            return [value, over_x(value)]
        gathered = lax.all_gather(value, "seq")
        return [gathered[n] for n in range(gathered.shape[0])]

    if custom:
        bufs = gather(at, weights[0])
    else:
        bufs = [lax.all_gather(weights[0], axes, axis=0, tiled=True)]
    xb = jnp.pad(inputs, ((0, 0), (0, QP - queries), (0, 0))).reshape(images * QP, D)
    qs, ks, vs, os, y1, qc, key, value, mixed, stat, *w = forward(left, flags, xb, memory, bufs, queries)
    w = w[0] if custom else bufs[0]
    vec = w[VEC_ROW : VEC_ROW + VECS].astype(F32)
    near_rows = 4 * D + QUERY_HEAD
    far_rows = 2 * FF - HEAD_ROWS + TAIL
    cross_rows = 4 * D - QUERY_HEAD + HEAD_ROWS
    far_shape = (2, 2, 2 * block, D) if custom else (far_rows, D)
    near_shape = (2, 2 * block, D) if custom else (near_rows, D)
    cross_shape = (2, 2 * block, D) if custom else (cross_rows, D)
    out, *grads, db, doc, tot, dvec_mid = middle(
        flags, y1, parts_of(mixed), parts_of(stat), w, vec, cotangent, matched, far_shape, cross_shape, custom
    )
    far, cross = grads[: 1 + custom], grads[1 + custom :]
    if custom:
        far_came = over_core(far[1])
    dq, dk, dv = cross_backward(left, qc, key, value, doc, tot)
    dq_parts = parts_of(dq)
    if custom:
        far = [far[0], far_came]
        dk, message = tie(dk, far_send(flags, *far))
        far_last = over_y(message)
    dcv_row, *cross = memory_weights(flags, cross, memory, dk, dv, custom)
    if custom:
        dcv_row = dcv_row + over_x(dcv_row)
    da, gq_head, dvec_query, *cross = query_backward(flags, cross, y1, db, dq_parts, w, vec, custom)
    if custom:
        cross_came = over_core(cross[1])
    gq_head, dcv_row = tie(gq_head, dcv_row)
    gx, dvec_self, *near = self_backward(
        flags, xb, qs, ks, vs, os, da, gq_head, w, queries, near_shape, custom
    )
    vec_rows = (dvec_mid + dvec_query + dvec_self) * (1.0 if custom else share)
    is_value_bias = jnp.arange(VECS)[:, None] == 4
    vec_rows = jnp.where(is_value_bias, dcv_row[0:1], vec_rows)
    if custom:
        far_last, near_send = tie(far_last, near[1])
        grad_rows, gm = finish(
            at, flags, block, far, far_last, near[0], near_send, cross[0], cross_came, vec_rows, (dk, dv, w)
        )
    else:
        gm = memory_grads(dk, dv, w)
        low_share = jnp.asarray(share, BF16)
        pad = lax.axis_size(axes) * block - VEC_ROW - VECS
        last = 2 * FF - HEAD_ROWS
        memory_rows = slice(D - QUERY_HEAD, 3 * D - QUERY_HEAD)
        grads = jnp.concatenate(
            [near[0] * low_share, cross[0][: memory_rows.start] * low_share, cross[0][memory_rows]]
            + [cross[0][memory_rows.stop :] * low_share, far[0][:last] * low_share]
            + [vec_rows.astype(BF16), jnp.zeros((pad, D), BF16)]
        )
        grad_rows = lax.psum_scatter(grads, axes, scatter_dimension=0, tiled=True).astype(F32)
    return out[:, :queries], gx[:, :queries], gm, grad_rows[None]


def solution(mesh):
    placed = (
        P("dp", None, None),
        P("dp", "seq", None),
        P("dp"),
        P("dp", None),
        P("dp", None, None),
        P(None, ("dp", "seq"), None),
    )
    custom = dict(mesh.shape) == {"dp": 16, "seq": 2}
    return jax.shard_map(
        partial(shards, custom),
        mesh=mesh,
        in_specs=placed,
        out_specs=(
            P("dp", None, None),
            P("dp", None, None),
            P("dp", "seq", None),
            P(None, ("dp", "seq"), None),
        ),
        check_vma=False,
    )
```
